256 devices in a mesh: pipe: 16 (over y, x_lo, core), tensor: 8 (over z), dp: 2 (over x_hi).
Axes of the slice: x: 4 (x_hi: 2, x_lo: 2; x = x_hi * 2 + x_lo), y: 4, z: 8, core: 2. Of those that a mesh axis runs over, the one named last changes fastest.
Arguments:
- hidden: bfloat16 [512, 8192], P(('dp', 'pipe', 'tensor')), parts along dimension 0, may hold values from -9 to 9
- lm_weight: bfloat16 [8192, 65536], P(None, ('pipe', 'tensor')), may hold values from -0.150893068 to 0.150893068
- targets: int32 [512], P('dp'), parts along dimension 0, may hold values from 0 to 65535
- loss_grad: float32 [512], P('dp'), parts along dimension 0, may hold values from 8 to 64
Outputs:
- ce_loss: float32 [512], P(('dp', 'pipe', 'tensor')), parts along dimension 0
- z_term: float32 [512], P(('dp', 'pipe', 'tensor')), parts along dimension 0
- hidden_grad: bfloat16 [512, 8192], P(('dp', 'pipe', 'tensor')), parts along dimension 0
The draws below stay inside these ranges and needn't reach their ends.
There are 2 independent parts, one for each index of `dp`. The reference program is written for one: setup_inputs(seed, part) draws one part's arguments, and reference() takes and returns one part's arrays. A program takes and returns all parts, laid end to end along the dimension named above; an argument that names none is the same for every part. Nothing has to cross between parts.
All inputs are finite; a program needn't handle non-finite values.
Results may differ from the reference program's by a relative error of at most 0.0045.
Values may be sent and summed in bfloat16 or wider, within the bound.
No kernel may reach another device: no remote copies, remote signals or barrier semaphores. Data moves between devices by JAX's collectives and lax.ppermute only.
A program may use at most 64 MiB of HBM per device.

```python
import math
import jax
import jax.numpy as jnp
import numpy as np
from jax import lax

D = 8192
TOKENS = 256
VOCAB = 65536


def draw_hidden(key, part):
    key = jax.random.fold_in(key, 11)
    key_scale, key_value = jax.random.split(key, 2)
    scales = jnp.exp(jax.random.uniform(key_scale, (TOKENS, 1), jnp.float32, math.log(0.6), math.log(1.5)))
    values = jnp.clip(jax.random.normal(key_value, (TOKENS, D), jnp.float32), -6.0, 6.0) * scales
    return values.astype(jnp.bfloat16)


def draw_lm_weight(key, part):
    key = jax.random.fold_in(key, 23)
    key_noise = jax.random.fold_in(key, 0)
    spread = 2.0 * D ** (-0.5)
    noise = jnp.clip(jax.random.normal(key_noise, (D, VOCAB), jnp.float32), -6.0, 6.0) * spread
    return noise.astype(jnp.bfloat16)


def set_ends(drawn, key, smallest, high):
    extent = drawn.shape
    spot = [jax.random.randint(jax.random.fold_in(key, axis), (), 0, extent[axis]) for axis in range(len(extent))]
    drawn = drawn.at[tuple(spot)].set(smallest)
    longest = extent.index(max(extent))
    spot[longest] = (spot[longest] + 1) % extent[longest]
    return drawn.at[tuple(spot)].set(high)


def rank_table(number_of, lean):
    weights = [(1 << 20) // math.isqrt(grade ** lean) + 1 for grade in range(1, number_of + 1)]
    scale = 1 + sum(weights) // (1 << 30)
    return np.cumsum(np.array([max(1, weight // scale) for weight in weights]))


def skewed_ids(own_key, dims, number_of, slope):
    listing = rank_table(number_of, slope)
    ticket = jax.random.randint(jax.random.fold_in(own_key, 1), dims, 0, int(listing[number_of - 1]))
    standing = jnp.searchsorted(jnp.asarray(listing, jnp.int32), ticket, side="right")
    return jax.random.permutation(jax.random.fold_in(own_key, 2), number_of)[standing].astype(jnp.int32)


def setup_inputs(seed: int = 0, part: int = 0) -> dict:
    arg_keys = jax.random.split(jax.random.key(seed), 5)
    part_keys = jax.random.split(jax.random.fold_in(arg_keys[4], part), 5)
    hidden = draw_hidden(jax.random.fold_in(jax.random.fold_in(arg_keys[4], part), 71), part)
    lm_weight = draw_lm_weight(jax.random.fold_in(arg_keys[4], 71), part)
    targets = set_ends(skewed_ids(part_keys[2], (TOKENS,), VOCAB, 2), jax.random.fold_in(part_keys[2], 3), 0, VOCAB - 1).astype(jnp.int32)
    loss_grad = jnp.clip(jnp.exp(jax.random.uniform(part_keys[3], (TOKENS,), jnp.float32, math.log(8.0), math.log(64.0))), 8.0, 64.0)
    return {"hidden": hidden, "lm_weight": lm_weight, "targets": targets, "loss_grad": loss_grad}


zloss_coef = 1e-4


def reference(hidden, lm_weight, targets, loss_grad):
    logits = jnp.dot(hidden, lm_weight, preferred_element_type=jnp.float32)
    row_top = jnp.max(logits, axis=1)
    sum_exp = jnp.sum(jnp.exp(logits - row_top[:, None]), axis=1)
    log_total = row_top + jnp.log(sum_exp)
    target_logit = jnp.take_along_axis(logits, targets[:, None].astype(jnp.int32), axis=1)[:, 0]
    ce_loss = log_total - target_logit
    z_term = zloss_coef * log_total * log_total
    columns = jnp.arange(logits.shape[1], dtype=jnp.int32)
    onehot = (columns[None, :] == targets[:, None]).astype(jnp.float32)
    probs = jnp.exp(logits - log_total[:, None])
    factor = 1.0 + 2.0 * zloss_coef * log_total
    logit_grad = (loss_grad[:, None] * (probs * factor[:, None] - onehot)).astype(jnp.bfloat16)
    hidden_grad = lax.dot_general(logit_grad, lm_weight, (((1,), (1,)), ((), ())), preferred_element_type=jnp.float32)
    return ce_loss, z_term, hidden_grad.astype(jnp.bfloat16)
```

```python
import jax
import jax.numpy as jnp
from jax import lax
from jax.sharding import Mesh
from jax.sharding import PartitionSpec as P

zloss_coef = 0.0001
NY, NX, NC, NZ = 4, 2, 2, 8
GROUP = ("y", "x", "c", "z")
OFFSETS = (0, 1, -1, 2)


def index_of(y, x, c, z):
    return (((y % NY) * NX + x % NX) * NC + c % NC) * NZ + z % NZ


def pairs(route):
    every = [(y, x, c, z) for y in range(NY) for x in range(NX) for c in range(NC) for z in range(NZ)]
    return [(index_of(*p), index_of(*route(*p))) for p in every]


def to_x(y, x, c, z):
    return y, x + 1, c, z


def to_c(y, x, c, z):
    return y, x, c + 1, z


def to_z4(y, x, c, z):
    return y, x, c, z + 4


def to_first(step):
    return lambda y, x, c, z: (y, x, c, z + step) if c == 0 else (y + step, x, c, z)


def to_second(step):
    return lambda y, x, c, z: (y + step, x, c, z) if c == 0 else (y, x, c, z + step)


def send(value, route):
    return lax.ppermute(value, GROUP, pairs(route))


def row_numbers(own_rows):
    y, x, c, z = (lax.axis_index(a) for a in GROUP)
    at = jnp.arange(256, dtype=jnp.int32)
    r, xr, z4, q1, q2, cr = at & 1, (at >> 1) & 1, (at >> 2) & 1, (at >> 3) & 3, (at >> 5) & 3, at >> 7
    o1 = jnp.where(q1 == 2, -1, jnp.where(q1 == 3, 2, q1))
    o2 = jnp.where(q2 == 2, -1, jnp.where(q2 == 3, 2, q2))
    core = c ^ cr
    zo = jnp.where(core == 0, o1, o2) + 4 * z4
    yo = jnp.where(core == 0, o2, o1)
    return ((((y + yo) & 3) * 2 + (x ^ xr)) * 2 + core) * 16 + ((z + zo) & 7) * 2 + r


def merge(stats, axis):
    top, total, picked = stats
    highest = jnp.max(top, axis=axis, keepdims=True)
    total = jnp.sum(total * jnp.exp(top - highest), axis=axis)
    return jnp.stack([jnp.squeeze(highest, axis), total, jnp.sum(picked, axis=axis)])


def shards(hidden, lm_weight, targets, loss_grad):
    f32 = jnp.float32
    voc_width = lm_weight.shape[1]
    depth = hidden.shape[1]
    position = lax.axis_index(GROUP)

    rows = row_numbers(hidden.shape[0])
    place = rows[:, None] == jnp.arange(256, dtype=jnp.int32)[None, :]
    own_targets = jnp.sum(jnp.where(place, targets[None, :], 0), axis=1)
    own_grad = jnp.sum(jnp.where(place, loss_grad[None, :], 0.0), axis=1)

    block = jnp.concatenate([hidden, send(hidden, to_x)])
    block = jnp.concatenate([block, send(block, to_z4)])
    block = jnp.concatenate([block] + [send(block, to_first(-o)) for o in OFFSETS[1:]])
    block = jnp.concatenate([block] + [send(block, to_second(-o)) for o in OFFSETS[1:]])
    block = jnp.concatenate([block, send(block, to_c)])

    logits = jnp.dot(block, lm_weight, preferred_element_type=f32)
    columns = jnp.arange(voc_width, dtype=jnp.int32) + position * voc_width
    hit = columns[None, :] == own_targets[:, None]
    top = jnp.max(logits, axis=1)
    total = jnp.sum(jnp.exp(logits - top[:, None]), axis=1)
    picked = jnp.sum(jnp.where(hit, logits, 0.0), axis=1)
    local = jnp.stack([top, total, picked])
    stats = jnp.sum(jnp.where(place[None], local[:, :, None], 0.0), axis=1)
    stats = merge(jnp.stack([stats, send(stats, to_c)], axis=1), 0)
    stats = merge(jnp.stack([stats, send(stats, to_x)], axis=1), 0)
    spread = lax.all_to_all(jnp.broadcast_to(stats[None], (32, 3, 256)), ("y", "z"), 0, 0)
    stats = merge(jnp.swapaxes(spread, 0, 1), 0)
    log_can = stats[0] + jnp.log(stats[1])
    both = jnp.stack([log_can, stats[2]])
    both = jnp.sum(jnp.where(place[None], both[:, None, :], 0.0), axis=2)
    log_total, target_logit = both[0], both[1]

    ce_loss = (log_total - target_logit)[:2]
    z_term = (zloss_coef * log_total * log_total)[:2]
    factor = 1.0 + 2.0 * zloss_coef * log_total
    probs = jnp.exp(logits - log_total[:, None])
    grad = (own_grad[:, None] * (probs * factor[:, None] - hit.astype(f32))).astype(jnp.bfloat16)
    part = lax.dot_general(grad, lm_weight, (((1,), (1,)), ((), ())), preferred_element_type=f32)

    part = part.reshape(2, 128, depth)
    part = part[0] + send(part[1].astype(jnp.bfloat16), to_c).astype(f32)
    part = part.reshape(4, 32, depth)
    part = part[0] + sum(
        send(part[k].astype(jnp.bfloat16), to_second(OFFSETS[k])).astype(f32) for k in (1, 2, 3)
    )
    part = part.reshape(4, 8, depth)
    part = part[0] + sum(
        send(part[k].astype(jnp.bfloat16), to_first(OFFSETS[k])).astype(f32) for k in (1, 2, 3)
    )
    part = part.reshape(2, 4, depth)
    part = part[0] + send(part[1], to_z4)
    part = part.reshape(2, 2, depth)
    part = part[0] + send(part[1], to_x)
    return ce_loss, z_term, part.astype(jnp.bfloat16)


def solution(mesh):
    mesh = Mesh(mesh.devices.reshape(NY, NX, NC, NZ, 2), (*GROUP, "dp"))
    own = ("dp", *GROUP)
    in_specs = (P(own, None), P(None, GROUP), P("dp"), P("dp"))
    out_specs = (P(own), P(own), P(own, None))
    return jax.shard_map(shards, mesh=mesh, in_specs=in_specs, out_specs=out_specs, check_vma=False)
```

```python
import functools

import jax
import jax.numpy as jnp
from jax import lax
from jax.experimental import pallas as pl
from jax.experimental.pallas import tpu as pltpu
from jax.sharding import Mesh
from jax.sharding import PartitionSpec as P

zloss_coef = 0.0001
NY, NX, NC, NZ = 4, 2, 2, 8
GROUP = ("y", "x", "c", "z")
OFFSETS = (0, 1, -1, 2)
BF, F32 = jnp.bfloat16, jnp.float32
ROWS, DEPTH, WIDTH = 256, 8192, 512
CHUNK = 1024
VMEM = pl.BlockSpec(memory_space=pltpu.VMEM)
SMEM = pl.BlockSpec(memory_space=pltpu.SMEM)


def index_of(y, x, c, z):
    return (((y % NY) * NX + x % NX) * NC + c % NC) * NZ + z % NZ


def pairs(route):
    every = [(y, x, c, z) for y in range(NY) for x in range(NX) for c in range(NC) for z in range(NZ)]
    return [(index_of(*p), index_of(*route(*p))) for p in every]


def to_x(y, x, c, z):
    return y, x + 1, c, z


def to_c(y, x, c, z):
    return y, x, c + 1, z


def to_z4(y, x, c, z):
    return y, x, c, z + 4


def to_xz4(y, x, c, z):
    return y, x + 1, c, z + 4


def to_first(step):
    return lambda y, x, c, z: (y, x, c, z + step) if c == 0 else (y + step, x, c, z)


def to_second(step):
    return lambda y, x, c, z: (y + step, x, c, z) if c == 0 else (y, x, c, z + step)


def send(value, route):
    return lax.ppermute(value, GROUP, pairs(route))


def row_numbers():
    y, x, c, z = (lax.axis_index(a) for a in GROUP)
    at = jnp.arange(ROWS, dtype=jnp.int32)
    r, xr, z4, q1, q2, cr = at & 1, (at >> 1) & 1, (at >> 2) & 1, (at >> 3) & 3, (at >> 5) & 3, at >> 7
    o1 = jnp.where(q1 == 2, -1, jnp.where(q1 == 3, 2, q1))
    o2 = jnp.where(q2 == 2, -1, jnp.where(q2 == 3, 2, q2))
    core = c ^ cr
    zo = jnp.where(core == 0, o1, o2) + 4 * z4
    yo = jnp.where(core == 0, o2, o1)
    return ((((y + yo) & 3) * 2 + (x ^ xr)) * 2 + core) * 16 + ((z + zo) & 7) * 2 + r


def params(mib=40):
    return pltpu.CompilerParams(vmem_limit_bytes=mib << 20)


def placed(rows_ref):
    return rows_ref[...] == lax.broadcasted_iota(jnp.int32, (ROWS, ROWS), 1)


def logits_kernel(rows_ref, hit_ref, p0, p1, p2, p3, p4, p5, p6, p7, w_ref, logits_ref, stats_ref):
    pieces = (p0, p1, p2, p3, p4, p5, p6, p7)
    acc = jnp.zeros((ROWS, WIDTH), F32)
    for k in range(0, DEPTH, CHUNK):
        left = jnp.concatenate([p[:, k : k + CHUNK] for p in pieces], axis=0)
        acc += jnp.dot(left, w_ref[k : k + CHUNK, :], preferred_element_type=F32)
    logits_ref[...] = acc
    top = jnp.max(acc, axis=1, keepdims=True)
    total = jnp.sum(jnp.exp(acc - top), axis=1, keepdims=True)
    hit = lax.broadcasted_iota(jnp.int32, (ROWS, WIDTH), 1) == hit_ref[...]
    picked = jnp.sum(jnp.where(hit, acc, 0.0), axis=1, keepdims=True)
    place = placed(rows_ref)
    for i, column in enumerate((top, total, picked)):
        stats_ref[i : i + 1, :] = jnp.sum(jnp.where(place, column, 0.0), axis=0, keepdims=True)


def grad_kernel(start, dtype, rows_ref, hit_ref, top_ref, logits_ref, w_ref, soft_ref, target_ref):
    half = ROWS // 2
    place = placed(rows_ref)[start : start + half]
    top = jnp.sum(jnp.where(place, top_ref[...], 0.0), axis=1, keepdims=True)
    hit = lax.broadcasted_iota(jnp.int32, (half, WIDTH), 1) == hit_ref[start : start + half, :]
    soft = jnp.where(hit, 0.0, jnp.exp(logits_ref[start : start + half, :] - top)).astype(BF)
    left = jnp.concatenate([soft, jnp.where(hit, 1.0, 0.0).astype(BF)], axis=0)
    for k in range(0, DEPTH, CHUNK):
        both = lax.dot_general(left, w_ref[k : k + CHUNK, :], (((1,), (1,)), ((), ())), preferred_element_type=F32)
        soft_ref[:, k : k + CHUNK] = both[:half].astype(dtype)
        target_ref[:, k : k + CHUNK] = both[half:].astype(BF)


def combine_kernel(rows_ref, grad_ref, top_ref, stats_ref, soft_own, soft_in, target_own, target_in, o0, o1, o2, o3, log_ref):
    place = placed(rows_ref)[: ROWS // 2]

    def ordered(row):
        return jnp.sum(jnp.where(place, row, 0.0), axis=1, keepdims=True)

    log_total = ordered(stats_ref[0:1, :] + jnp.log(stats_ref[1:2, :]))
    picked = ordered(stats_ref[2:3, :])
    top = ordered(top_ref[...])
    lane = lax.broadcasted_iota(jnp.int32, (8, 128), 1)
    log_ref[...] = jnp.where(lane == 0, log_total[:8], picked[:8])
    factor = 1.0 + 2.0 * zloss_coef * log_total
    grad = grad_ref[: ROWS // 2, :]
    scale = grad * factor * jnp.exp(top - log_total)
    target = (grad * (jnp.exp(picked - log_total) * factor - 1.0)).astype(BF).astype(F32)
    for q, out in enumerate((o0, o1, o2, o3)):
        at = slice(32 * q, 32 * q + 32)
        for k in range(0, DEPTH, CHUNK):
            cut = slice(k, k + CHUNK)
            soft = soft_own[at, cut] + soft_in[at, cut].astype(F32)
            chosen = target_own[at, cut].astype(F32) + target_in[at, cut].astype(F32)
            out[:, cut] = (scale[at] * soft + target[at] * chosen).astype(out.dtype)


def merge(stats, axis):
    top, total, picked = stats
    highest = jnp.max(top, axis=axis, keepdims=True)
    total = jnp.sum(total * jnp.exp(top - highest), axis=axis)
    return jnp.stack([jnp.squeeze(highest, axis), total, jnp.sum(picked, axis=axis)])


def shards(hidden, lm_weight, targets, loss_grad):
    position = lax.axis_index(GROUP)
    half = ROWS // 2

    rows = row_numbers()[:, None]
    place = rows == jnp.arange(ROWS, dtype=jnp.int32)[None, :]
    own_hit = jnp.sum(jnp.where(place, targets[None, :], 0), axis=1, keepdims=True) - position * WIDTH
    own_grad = jnp.sum(jnp.where(place, loss_grad[None, :], 0.0), axis=1, keepdims=True)

    block = jnp.concatenate([hidden] + [send(hidden, to) for to in (to_x, to_z4, to_xz4)])
    block = jnp.concatenate([block] + [send(block, to_first(-o)) for o in OFFSETS[1:]])
    pieces = [block] + [send(block, to_second(-o)) for o in OFFSETS[1:]]
    pieces = pieces + [send(p, to_c) for p in pieces]

    logits, stats = pl.pallas_call(
        logits_kernel,
        out_shape=(jax.ShapeDtypeStruct((ROWS, WIDTH), F32), jax.ShapeDtypeStruct((3, ROWS), F32)),
        in_specs=[VMEM] * 11,
        out_specs=(VMEM, VMEM),
        compiler_params=params(),
        cost_estimate=pl.CostEstimate(flops=2 * ROWS * DEPTH * WIDTH, bytes_accessed=13 << 20, transcendentals=ROWS * WIDTH),
        name="logits",
    )(rows, own_hit, *pieces, lm_weight)
    stats = merge(jnp.stack([stats, send(stats, to_c)], axis=1), 0)
    top = stats[:1]

    def product(start, dtype):
        return pl.pallas_call(
            functools.partial(grad_kernel, start, dtype),
            out_shape=(jax.ShapeDtypeStruct((half, DEPTH), dtype), jax.ShapeDtypeStruct((half, DEPTH), BF)),
            in_specs=[VMEM] * 5,
            out_specs=(VMEM, VMEM),
            compiler_params=params(),
            cost_estimate=pl.CostEstimate(flops=2 * ROWS * DEPTH * WIDTH, bytes_accessed=12 << 20, transcendentals=half * WIDTH),
            name="product",
        )(rows, own_hit, top, logits, lm_weight)

    soft_out, target_out = product(half, BF)
    soft_in, target_in = send(soft_out, to_c), send(target_out, to_c)
    soft_own, target_own = product(0, F32)

    stats = merge(jnp.stack([stats, send(stats, to_x)], axis=1), 0)
    spread = lax.all_to_all(jnp.broadcast_to(stats[None], (32, 3, ROWS)), ("y", "z"), 0, 0)
    stats = merge(jnp.swapaxes(spread, 0, 1), 0)

    *pieces, logs = pl.pallas_call(
        combine_kernel,
        out_shape=[jax.ShapeDtypeStruct((32, DEPTH), F32)]
        + [jax.ShapeDtypeStruct((32, DEPTH), BF)] * 3
        + [jax.ShapeDtypeStruct((8, 128), F32)],
        in_specs=[VMEM] * 8,
        out_specs=[VMEM] * 5,
        compiler_params=params(),
        cost_estimate=pl.CostEstimate(flops=6 * half * DEPTH, bytes_accessed=13 << 20, transcendentals=0),
        name="combine",
    )(rows, own_grad, top, stats, soft_own, soft_in, target_own, target_in)
    log_total, target_logit = logs[:2, 0], logs[:2, 1]
    ce_loss = log_total - target_logit
    z_term = zloss_coef * log_total * log_total

    part = pieces[0] + sum(send(pieces[k], to_second(OFFSETS[k])).astype(F32) for k in (1, 2, 3))
    part = part.reshape(4, 8, DEPTH)
    part = part[0] + sum(send(part[k].astype(BF), to_first(OFFSETS[k])).astype(F32) for k in (1, 2, 3))
    part = [part[0:2]] + [send(part[2 * k : 2 * k + 2], to) for k, to in ((1, to_x), (2, to_z4), (3, to_xz4))]
    part = (part[0] + part[1]) + (part[2] + part[3])
    return ce_loss, z_term, part.astype(BF)


def solution(mesh):
    mesh = Mesh(mesh.devices.reshape(NY, NX, NC, NZ, 2), (*GROUP, "dp"))
    own = ("dp", *GROUP)
    in_specs = (P(own, None), P(None, GROUP), P("dp"), P("dp"))
    out_specs = (P(own), P(own), P(own, None))
    return jax.shard_map(shards, mesh=mesh, in_specs=in_specs, out_specs=out_specs, check_vma=False)
```

```python
import functools

import jax
import jax.numpy as jnp
from jax import lax
from jax.experimental import pallas as pl
from jax.experimental.pallas import tpu as pltpu
from jax.sharding import Mesh
from jax.sharding import PartitionSpec as P

zloss_coef = 0.0001
NY, NX, NC, NZ = 4, 2, 2, 8
GROUP = ("y", "x", "c", "z")
OFFSETS = (0, 1, -1, 2)
BF, F32 = jnp.bfloat16, jnp.float32
ROWS, DEPTH, WIDTH = 256, 8192, 512
CHUNK = 1024
VMEM = pl.BlockSpec(memory_space=pltpu.VMEM)
SMEM = pl.BlockSpec(memory_space=pltpu.SMEM)


def index_of(y, x, c, z):
    return (((y % NY) * NX + x % NX) * NC + c % NC) * NZ + z % NZ


def pairs(route):
    every = [(y, x, c, z) for y in range(NY) for x in range(NX) for c in range(NC) for z in range(NZ)]
    return [(index_of(*p), index_of(*route(*p))) for p in every]


def to_x(y, x, c, z):
    return y, x + 1, c, z


def to_c(y, x, c, z):
    return y, x, c + 1, z


def to_z4(y, x, c, z):
    return y, x, c, z + 4


def to_xc(y, x, c, z):
    return y, x + 1, c + 1, z


def to_xz4(y, x, c, z):
    return y, x + 1, c, z + 4


def to_first(step):
    return lambda y, x, c, z: (y, x, c, z + step) if c == 0 else (y + step, x, c, z)


def to_second(step):
    return lambda y, x, c, z: (y + step, x, c, z) if c == 0 else (y, x, c, z + step)


def send(value, route):
    return lax.ppermute(value, GROUP, pairs(route))


def row_numbers():
    y, x, c, z = (lax.axis_index(a) for a in GROUP)
    at = jnp.arange(ROWS, dtype=jnp.int32)
    r, xr, z4, q1, q2, cr = at & 1, (at >> 1) & 1, (at >> 2) & 1, (at >> 3) & 3, (at >> 5) & 3, at >> 7
    o1 = jnp.where(q1 == 2, -1, jnp.where(q1 == 3, 2, q1))
    o2 = jnp.where(q2 == 2, -1, jnp.where(q2 == 3, 2, q2))
    core = c ^ cr
    zo = jnp.where(core == 0, o1, o2) + 4 * z4
    yo = jnp.where(core == 0, o2, o1)
    return ((((y + yo) & 3) * 2 + (x ^ xr)) * 2 + core) * 16 + ((z + zo) & 7) * 2 + r


def params(mib=8):
    return pltpu.CompilerParams(vmem_limit_bytes=mib << 20)


def placed(rows_ref):
    return rows_ref[...] == lax.broadcasted_iota(jnp.int32, (ROWS, ROWS), 1)


def logits_kernel(rows_ref, hit_ref, p0, p1, p2, p3, p4, p5, p6, p7, w_ref, logits_ref, stats_ref):
    pieces = (p0, p1, p2, p3, p4, p5, p6, p7)
    acc = jnp.zeros((ROWS, WIDTH), F32)
    for k in range(0, DEPTH, CHUNK):
        left = jnp.concatenate([p[:, k : k + CHUNK] for p in pieces], axis=0)
        acc += jnp.dot(left, w_ref[k : k + CHUNK, :], preferred_element_type=F32)
    logits_ref[...] = acc
    top = jnp.max(acc, axis=1, keepdims=True)
    total = jnp.sum(jnp.exp(acc - top), axis=1, keepdims=True)
    hit = lax.broadcasted_iota(jnp.int32, (ROWS, WIDTH), 1) == hit_ref[...]
    picked = jnp.sum(jnp.where(hit, acc, 0.0), axis=1, keepdims=True)
    place = placed(rows_ref)
    for i, column in enumerate((top, total, picked)):
        stats_ref[i : i + 1, :] = jnp.sum(jnp.where(place, column, 0.0), axis=0, keepdims=True)


def product(left, w_ref, out_refs):
    for k in range(0, DEPTH, CHUNK):
        part = lax.dot_general(left, w_ref[k : k + CHUNK, :], (((1,), (1,)), ((), ())), preferred_element_type=F32)
        at = 0
        for out in out_refs:
            out[:, k : k + CHUNK] = part[at : at + out.shape[0]].astype(out.dtype)
            at += out.shape[0]


def target_kernel(hit_ref, w_ref, own_ref, other_ref):
    hit = lax.broadcasted_iota(jnp.int32, (ROWS, WIDTH), 1) == hit_ref[...]
    product(jnp.where(hit, 1.0, 0.0).astype(BF), w_ref, (own_ref, other_ref))


def soft_kernel(start, rows_ref, hit_ref, merged_ref, logits_ref, w_ref, soft_ref):
    half = ROWS // 2
    cut = slice(start, start + half)
    top = jnp.sum(jnp.where(placed(rows_ref)[cut], merged_ref[0, 0:1, :], 0.0), axis=1, keepdims=True)
    hit = lax.broadcasted_iota(jnp.int32, (half, WIDTH), 1) == hit_ref[cut, :]
    product(jnp.where(hit, 0.0, jnp.exp(logits_ref[cut, :] - top)).astype(BF), w_ref, (soft_ref,))


def merge_kernel(own_ref, core_ref, x_ref, both_ref, out_ref):
    refs = (own_ref, core_ref, x_ref, both_ref)
    tops = [r[0:1, :] for r in refs]
    top = jnp.maximum(jnp.maximum(tops[0], tops[1]), jnp.maximum(tops[2], tops[3]))
    total = sum(r[1:2, :] * jnp.exp(t - top) for r, t in zip(refs, tops))
    picked = sum(r[2:3, :] for r in refs)
    merged = jnp.concatenate([top, total, picked], axis=0)
    for i in range(out_ref.shape[0]):
        out_ref[i] = merged


def scales_kernel(rows_ref, grad_ref, merged_ref, spread_ref, out_ref):
    place = placed(rows_ref)[: ROWS // 2]

    def ordered(row):
        return jnp.sum(jnp.where(place, row, 0.0), axis=1, keepdims=True)

    tops = spread_ref[:, 0, :]
    highest = jnp.max(tops, axis=0, keepdims=True)
    total = jnp.sum(spread_ref[:, 1, :] * jnp.exp(tops - highest), axis=0, keepdims=True)
    log_total = ordered(highest + jnp.log(total))
    picked = ordered(jnp.sum(spread_ref[:, 2, :], axis=0, keepdims=True))
    top = ordered(merged_ref[0, 0:1, :])
    factor = 1.0 + 2.0 * zloss_coef * log_total
    grad = grad_ref[: ROWS // 2, :]
    scale = grad * factor * jnp.exp(top - log_total)
    target = (grad * (jnp.exp(picked - log_total) * factor - 1.0)).astype(BF).astype(F32)
    lane = lax.broadcasted_iota(jnp.int32, (ROWS // 2, 128), 1)
    out_ref[...] = jnp.where(lane == 0, scale, jnp.where(lane == 1, target, jnp.where(lane == 2, log_total, picked)))


def combine_kernel(parts, scales_ref, soft_own, soft_in, target_own, target_in, *outs):
    for q, out in zip(parts, outs):
        at = slice(32 * q, 32 * q + 32)
        scale, target = scales_ref[at, 0:1], scales_ref[at, 1:2]
        for k in range(0, DEPTH, CHUNK):
            cut = slice(k, k + CHUNK)
            soft = soft_own[at, cut] + soft_in[at, cut].astype(F32)
            chosen = target_own[at, cut].astype(F32) + target_in[at, cut].astype(F32)
            out[:, cut] = (scale * soft + target * chosen).astype(out.dtype)


def shards(hidden, lm_weight, targets, loss_grad):
    position = lax.axis_index(GROUP)
    half = ROWS // 2

    rows = row_numbers()[:, None]
    place = rows == jnp.arange(ROWS, dtype=jnp.int32)[None, :]
    own_hit = jnp.sum(jnp.where(place, targets[None, :], 0), axis=1, keepdims=True) - position * WIDTH
    own_grad = jnp.sum(jnp.where(place, loss_grad[None, :], 0.0), axis=1, keepdims=True)

    block = jnp.concatenate([hidden] + [send(hidden, to) for to in (to_x, to_z4, to_xz4)])
    block = jnp.concatenate([block] + [send(block, to_first(-o)) for o in OFFSETS[1:]])
    pieces = [block] + [send(block, to_second(-o)) for o in OFFSETS[1:]]
    pieces = pieces + [send(p, to_c) for p in pieces]

    hit, block = lax.optimization_barrier((own_hit, block))
    target_own, target_out = pl.pallas_call(
        target_kernel,
        out_shape=[jax.ShapeDtypeStruct((half, DEPTH), BF)] * 2,
        in_specs=[VMEM] * 2,
        out_specs=[VMEM] * 2,
        compiler_params=params(),
        cost_estimate=pl.CostEstimate(flops=2 * ROWS * DEPTH * WIDTH, bytes_accessed=12 << 20, transcendentals=0),
        name="target",
    )(hit, lm_weight)
    target_in = send(target_out, to_c)
    pieces[0], target_own = lax.optimization_barrier((pieces[0], target_own))

    logits, stats = pl.pallas_call(
        logits_kernel,
        out_shape=(jax.ShapeDtypeStruct((ROWS, WIDTH), F32), jax.ShapeDtypeStruct((3, ROWS), F32)),
        in_specs=[VMEM] * 11,
        out_specs=(VMEM, VMEM),
        compiler_params=params(),
        cost_estimate=pl.CostEstimate(flops=2 * ROWS * DEPTH * WIDTH, bytes_accessed=13 << 20, transcendentals=ROWS * WIDTH),
        name="logits",
    )(rows, own_hit, *pieces, lm_weight)
    stats = [stats] + [send(stats, to) for to in (to_c, to_x, to_xc)]

    merged = pl.pallas_call(
        merge_kernel,
        out_shape=jax.ShapeDtypeStruct((32, 3, ROWS), F32),
        in_specs=[VMEM] * 4,
        out_specs=VMEM,
        compiler_params=params(),
        name="merge",
    )(*stats)

    def soft(start, dtype):
        return pl.pallas_call(
            functools.partial(soft_kernel, start),
            out_shape=jax.ShapeDtypeStruct((half, DEPTH), dtype),
            in_specs=[VMEM] * 5,
            out_specs=VMEM,
            compiler_params=params(),
            cost_estimate=pl.CostEstimate(flops=ROWS * DEPTH * WIDTH, bytes_accessed=10 << 20, transcendentals=half * WIDTH),
            name="soft",
        )(rows, own_hit, merged, logits, lm_weight)

    spread = lax.all_to_all(merged, ("y", "z"), 0, 0)
    soft_in = send(soft(half, BF), to_c)
    soft_own = soft(0, F32)
    scales = pl.pallas_call(
        scales_kernel,
        out_shape=jax.ShapeDtypeStruct((half, 128), F32),
        in_specs=[VMEM] * 4,
        out_specs=VMEM,
        compiler_params=params(),
        name="scales",
    )(rows, own_grad, merged, spread)

    def combine(parts, dtype):
        return pl.pallas_call(
            functools.partial(combine_kernel, parts),
            out_shape=[jax.ShapeDtypeStruct((32, DEPTH), dtype)] * len(parts),
            in_specs=[VMEM] * 5,
            out_specs=[VMEM] * len(parts),
            compiler_params=params(),
            cost_estimate=pl.CostEstimate(flops=6 * 32 * DEPTH, bytes_accessed=2 << 20, transcendentals=0),
            name="combine",
        )(scales, soft_own, soft_in, target_own, target_in)

    pieces = [None, None, None, combine((3,), BF)[0]]
    pieces[1], pieces[2] = combine((1, 2), BF)
    pieces[0] = combine((0,), F32)[0]
    log_total, target_logit = scales[:2, 2], scales[:2, 3]
    ce_loss = log_total - target_logit
    z_term = zloss_coef * log_total * log_total

    part = pieces[0] + sum(send(pieces[k], to_second(OFFSETS[k])).astype(F32) for k in (1, 2, 3))
    part = part.reshape(4, 8, DEPTH)
    part = part[0] + sum(send(part[k].astype(BF), to_first(OFFSETS[k])).astype(F32) for k in (1, 2, 3))
    part = [part[0:2]] + [
        send(part[2 * k : 2 * k + 2].astype(BF), to).astype(F32) for k, to in ((1, to_x), (2, to_z4), (3, to_xz4))
    ]
    part = (part[0] + part[1]) + (part[2] + part[3])
    return ce_loss, z_term, part.astype(BF)


def solution(mesh):
    mesh = Mesh(mesh.devices.reshape(NY, NX, NC, NZ, 2), (*GROUP, "dp"))
    own = ("dp", *GROUP)
    in_specs = (P(own, None), P(None, GROUP), P("dp"), P("dp"))
    out_specs = (P(own), P(own), P(own, None))
    return jax.shard_map(shards, mesh=mesh, in_specs=in_specs, out_specs=out_specs, check_vma=False)
```

```python
import functools

import jax
import jax.numpy as jnp
from jax import lax
from jax.experimental import pallas as pl
from jax.experimental.pallas import tpu as pltpu
from jax.sharding import Mesh
from jax.sharding import PartitionSpec as P

zloss_coef = 0.0001
NY, NX, NC, NZ = 4, 2, 2, 8
GROUP = ("y", "x", "c", "z")
OFFSETS = (0, 1, -1, 2)
BF, F32 = jnp.bfloat16, jnp.float32
ROWS, DEPTH, WIDTH = 256, 8192, 512
CHUNK = 1024
STEPS = DEPTH // CHUNK
VMEM = pl.BlockSpec(memory_space=pltpu.VMEM)
SMEM = pl.BlockSpec(memory_space=pltpu.SMEM)


def index_of(y, x, c, z):
    return (((y % NY) * NX + x % NX) * NC + c % NC) * NZ + z % NZ


def pairs(route):
    every = [(y, x, c, z) for y in range(NY) for x in range(NX) for c in range(NC) for z in range(NZ)]
    return [(index_of(*p), index_of(*route(*p))) for p in every]


def to_x(y, x, c, z):
    return y, x + 1, c, z


def to_c(y, x, c, z):
    return y, x, c + 1, z


def to_z4(y, x, c, z):
    return y, x, c, z + 4


def to_xc(y, x, c, z):
    return y, x + 1, c + 1, z


def to_xz4(y, x, c, z):
    return y, x + 1, c, z + 4


def to_first(step):
    return lambda y, x, c, z: (y, x, c, z + step) if c == 0 else (y + step, x, c, z)


def to_second(step):
    return lambda y, x, c, z: (y + step, x, c, z) if c == 0 else (y, x, c, z + step)


def send(value, route):
    return lax.ppermute(value, GROUP, pairs(route))


def params(mib=24):
    return pltpu.CompilerParams(vmem_limit_bytes=mib << 20)


def placed(at_ref):
    y, x, c, z = (at_ref[i] for i in range(4))
    at = lax.broadcasted_iota(jnp.int32, (ROWS, 1), 0)
    r, xr, z4, q1, q2, cr = at & 1, (at >> 1) & 1, (at >> 2) & 1, (at >> 3) & 3, (at >> 5) & 3, at >> 7
    o1 = jnp.where(q1 == 2, -1, jnp.where(q1 == 3, 2, q1))
    o2 = jnp.where(q2 == 2, -1, jnp.where(q2 == 3, 2, q2))
    core = c ^ cr
    zo = jnp.where(core == 0, o1, o2) + 4 * z4
    yo = jnp.where(core == 0, o2, o1)
    rows = ((((y + yo) & 3) * 2 + (x ^ xr)) * 2 + core) * 16 + ((z + zo) & 7) * 2 + r
    return rows == lax.broadcasted_iota(jnp.int32, (ROWS, ROWS), 1)


def hits(at_ref, targets_ref, place):
    own = jnp.sum(jnp.where(place, targets_ref[...], 0), axis=1, keepdims=True) - at_ref[4]
    return lax.broadcasted_iota(jnp.int32, (ROWS, WIDTH), 1) == own


def logits_kernel(at_ref, targets_ref, p0, p1, p2, p3, p4, p5, p6, p7, w_ref, logits_ref, stats_ref):
    k = pl.program_id(0)
    left = jnp.concatenate([p[...] for p in (p0, p1, p2, p3, p4, p5, p6, p7)], axis=0)
    part = jnp.dot(left, w_ref[...], preferred_element_type=F32)

    @pl.when(k == 0)
    def _():
        logits_ref[...] = part

    @pl.when(k > 0)
    def _():
        logits_ref[...] += part

    @pl.when(k == STEPS - 1)
    def _():
        acc = logits_ref[...]
        top = jnp.max(acc, axis=1, keepdims=True)
        total = jnp.sum(jnp.exp(acc - top), axis=1, keepdims=True)
        place = placed(at_ref)
        picked = jnp.sum(jnp.where(hits(at_ref, targets_ref, place), acc, 0.0), axis=1, keepdims=True)
        for i, column in enumerate((top, total, picked)):
            stats_ref[i : i + 1, :] = jnp.sum(jnp.where(place, column, 0.0), axis=0, keepdims=True)


def times_weights(left, w_ref):
    return lax.dot_general(left, w_ref[...], (((1,), (1,)), ((), ())), preferred_element_type=F32)


def target_kernel(at_ref, targets_ref, w_ref, own_ref, other_ref, left_ref):
    @pl.when(pl.program_id(0) == 0)
    def _():
        left_ref[...] = jnp.where(hits(at_ref, targets_ref, placed(at_ref)), 1.0, 0.0).astype(BF)

    part = times_weights(left_ref[...], w_ref)
    own_ref[...] = part[: ROWS // 2].astype(BF)
    other_ref[...] = part[ROWS // 2 :].astype(BF)


def soft_kernel(start, at_ref, targets_ref, merged_ref, logits_ref, w_ref, soft_ref, left_ref):
    @pl.when(pl.program_id(0) == 0)
    def _():
        cut = slice(start, start + ROWS // 2)
        place = placed(at_ref)
        top = jnp.sum(jnp.where(place[cut], merged_ref[0, 0:1, :], 0.0), axis=1, keepdims=True)
        hit = hits(at_ref, targets_ref, place)[cut]
        left_ref[...] = jnp.where(hit, 0.0, jnp.exp(logits_ref[...] - top)).astype(BF)

    soft_ref[...] = times_weights(left_ref[...], w_ref).astype(soft_ref.dtype)


def merge_kernel(own_ref, core_ref, x_ref, both_ref, out_ref):
    refs = (own_ref, core_ref, x_ref, both_ref)
    tops = [r[0:1, :] for r in refs]
    top = jnp.maximum(jnp.maximum(tops[0], tops[1]), jnp.maximum(tops[2], tops[3]))
    total = sum(r[1:2, :] * jnp.exp(t - top) for r, t in zip(refs, tops))
    picked = sum(r[2:3, :] for r in refs)
    merged = jnp.concatenate([top, total, picked], axis=0)
    for i in range(out_ref.shape[0]):
        out_ref[i] = merged


def scales_kernel(at_ref, grad_ref, merged_ref, spread_ref, out_ref):
    place = placed(at_ref)[: ROWS // 2]

    def ordered(row):
        return jnp.sum(jnp.where(place, row, 0.0), axis=1, keepdims=True)

    tops = spread_ref[:, 0, :]
    highest = jnp.max(tops, axis=0, keepdims=True)
    total = jnp.sum(spread_ref[:, 1, :] * jnp.exp(tops - highest), axis=0, keepdims=True)
    log_total = ordered(highest + jnp.log(total))
    picked = ordered(jnp.sum(spread_ref[:, 2, :], axis=0, keepdims=True))
    top = ordered(merged_ref[0, 0:1, :])
    factor = 1.0 + 2.0 * zloss_coef * log_total
    grad = ordered(grad_ref[...])
    scale = grad * factor * jnp.exp(top - log_total)
    target = (grad * (jnp.exp(picked - log_total) * factor - 1.0)).astype(BF).astype(F32)
    lane = lax.broadcasted_iota(jnp.int32, (ROWS // 2, 128), 1)
    out_ref[...] = jnp.where(lane == 0, scale, jnp.where(lane == 1, target, jnp.where(lane == 2, log_total, picked)))


def combine_kernel(scales_ref, soft_own, soft_in, target_own, target_in, out_ref):
    soft = soft_own[...] + soft_in[...].astype(F32)
    chosen = target_own[...].astype(F32) + target_in[...].astype(F32)
    out_ref[...] = (scales_ref[:, 0:1] * soft + scales_ref[:, 1:2] * chosen).astype(out_ref.dtype)


def shards(hidden, lm_weight, targets, loss_grad):
    half = ROWS // 2
    at = jnp.stack([lax.axis_index(a) for a in GROUP] + [lax.axis_index(GROUP) * WIDTH])
    targets, loss_grad = targets.reshape(1, ROWS), loss_grad.reshape(1, ROWS)
    lm_weight = pltpu.with_memory_space_constraint(lm_weight, pltpu.HBM)
    row = pl.BlockSpec((1, ROWS), lambda k: (0, 0))
    weights = pl.BlockSpec((CHUNK, WIDTH), lambda k: (k, 0))

    block = jnp.concatenate([hidden] + [send(hidden, to) for to in (to_x, to_z4, to_xz4)])
    far, near, back = (send(block, to_first(-o)) for o in (2, 1, -1))
    block = jnp.concatenate([block, near, back, far])
    far, near, back = (send(block, to_second(-o)) for o in (2, 1, -1))

    aim, _ = lax.optimization_barrier((targets, block))
    target_own, target_out = pl.pallas_call(
        target_kernel,
        out_shape=[jax.ShapeDtypeStruct((half, DEPTH), BF)] * 2,
        grid=(STEPS,),
        in_specs=[SMEM, row, weights],
        out_specs=[pl.BlockSpec((half, CHUNK), lambda k: (0, k))] * 2,
        scratch_shapes=[pltpu.VMEM((ROWS, WIDTH), BF)],
        compiler_params=params(),
        cost_estimate=pl.CostEstimate(flops=2 * ROWS * DEPTH * WIDTH, bytes_accessed=12 << 20, transcendentals=0),
        name="target",
    )(at, aim, lm_weight)
    near, target_own, target_out = lax.optimization_barrier((near, target_own, target_out))
    pieces = [block, near, back, far]
    pieces = pieces + [send(p, to_c) for p in pieces]
    target_in = send(target_out, to_c)

    logits, stats = pl.pallas_call(
        logits_kernel,
        out_shape=(jax.ShapeDtypeStruct((ROWS, WIDTH), F32), jax.ShapeDtypeStruct((3, ROWS), F32)),
        grid=(STEPS,),
        in_specs=[SMEM, row] + [pl.BlockSpec((32, CHUNK), lambda k: (0, k))] * 8 + [weights],
        out_specs=(pl.BlockSpec((ROWS, WIDTH), lambda k: (0, 0)), pl.BlockSpec((3, ROWS), lambda k: (0, 0))),
        compiler_params=params(),
        cost_estimate=pl.CostEstimate(flops=2 * ROWS * DEPTH * WIDTH, bytes_accessed=13 << 20, transcendentals=ROWS * WIDTH),
        name="logits",
    )(at, targets, *pieces, lm_weight)
    stats = [stats] + [send(stats, to) for to in (to_c, to_x, to_xc)]
    merged = pl.pallas_call(
        merge_kernel,
        out_shape=jax.ShapeDtypeStruct((32, 3, ROWS), F32),
        in_specs=[VMEM] * 4,
        out_specs=VMEM,
        compiler_params=params(),
        name="merge",
    )(*stats)
    spread = lax.all_to_all(merged, ("y", "z"), 0, 0)

    def soft(start, dtype):
        return pl.pallas_call(
            functools.partial(soft_kernel, start),
            out_shape=jax.ShapeDtypeStruct((half, DEPTH), dtype),
            grid=(STEPS,),
            in_specs=[
                SMEM,
                row,
                pl.BlockSpec((1, 3, ROWS), lambda k: (0, 0, 0)),
                pl.BlockSpec((half, WIDTH), lambda k: (start // half, 0)),
                weights,
            ],
            out_specs=pl.BlockSpec((half, CHUNK), lambda k: (0, k)),
            scratch_shapes=[pltpu.VMEM((half, WIDTH), BF)],
            compiler_params=params(),
            cost_estimate=pl.CostEstimate(flops=1 << 20, bytes_accessed=1 << 16, transcendentals=0),
            name="soft",
        )(at, targets, merged, logits, lm_weight)

    soft_in = send(soft(half, BF), to_c)
    soft_own = soft(0, F32)
    scales = pl.pallas_call(
        scales_kernel,
        out_shape=jax.ShapeDtypeStruct((half, 128), F32),
        in_specs=[SMEM] + [VMEM] * 3,
        out_specs=VMEM,
        compiler_params=params(),
        name="scales",
    )(at, loss_grad, merged, spread)

    def combine(q, dtype):
        piece = pl.BlockSpec((32, 2 * CHUNK), lambda k: (q, k))
        return pl.pallas_call(
            combine_kernel,
            out_shape=jax.ShapeDtypeStruct((32, DEPTH), dtype),
            grid=(STEPS // 2,),
            in_specs=[pl.BlockSpec((32, 128), lambda k: (q, 0))] + [piece] * 4,
            out_specs=pl.BlockSpec((32, 2 * CHUNK), lambda k: (0, k)),
            compiler_params=params(),
            cost_estimate=pl.CostEstimate(flops=6 * 32 * DEPTH, bytes_accessed=3 << 20, transcendentals=0),
            name="combine",
        )(scales, soft_own, soft_in, target_own, target_in)

    arrived = [send(combine(k, BF), to_second(OFFSETS[k])).astype(F32) for k in (3, 1, 2)]
    part = combine(0, F32) + sum(arrived)
    log_total, target_logit = scales[:2, 2], scales[:2, 3]
    ce_loss = log_total - target_logit
    z_term = zloss_coef * log_total * log_total

    part = part.reshape(4, 8, DEPTH)
    part = part[0] + sum(send(part[k].astype(BF), to_first(OFFSETS[k])).astype(F32) for k in (3, 1, 2))
    part = [part[0:2]] + [
        send(part[2 * k : 2 * k + 2].astype(BF), to).astype(F32) for k, to in ((3, to_xz4), (2, to_z4), (1, to_x))
    ]
    part = (part[0] + part[1]) + (part[2] + part[3])
    return ce_loss, z_term, part.astype(BF)


def solution(mesh):
    mesh = Mesh(mesh.devices.reshape(NY, NX, NC, NZ, 2), (*GROUP, "dp"))
    own = ("dp", *GROUP)
    in_specs = (P(own, None), P(None, GROUP), P("dp"), P("dp"))
    out_specs = (P(own), P(own), P(own, None))
    return jax.shard_map(shards, mesh=mesh, in_specs=in_specs, out_specs=out_specs, check_vma=False)
```

```python
import functools

import jax
import jax.numpy as jnp
from jax import lax
from jax.experimental import pallas as pl
from jax.experimental.pallas import tpu as pltpu
from jax.sharding import Mesh
from jax.sharding import PartitionSpec as P

zloss_coef = 0.0001
NY, NX, NC, NZ = 4, 2, 2, 8
GROUP = ("y", "x", "c", "z")
OFFSETS = (0, 1, -1, 2)
BF, F32 = jnp.bfloat16, jnp.float32
ROWS, DEPTH, WIDTH = 256, 8192, 512
CHUNK = 1024
STEPS = DEPTH // CHUNK
VMEM = pl.BlockSpec(memory_space=pltpu.VMEM)
SMEM = pl.BlockSpec(memory_space=pltpu.SMEM)
ANY = pl.BlockSpec(memory_space=pl.ANY)
HBM = pl.BlockSpec(memory_space=pltpu.HBM)


def index_of(y, x, c, z):
    return (((y % NY) * NX + x % NX) * NC + c % NC) * NZ + z % NZ


def pairs(route):
    every = [(y, x, c, z) for y in range(NY) for x in range(NX) for c in range(NC) for z in range(NZ)]
    return [(index_of(*p), index_of(*route(*p))) for p in every]


def to_x(y, x, c, z):
    return y, x + 1, c, z


def to_c(y, x, c, z):
    return y, x, c + 1, z


def to_z4(y, x, c, z):
    return y, x, c, z + 4


def to_xc(y, x, c, z):
    return y, x + 1, c + 1, z


def to_xz4(y, x, c, z):
    return y, x + 1, c, z + 4


def to_first(step):
    return lambda y, x, c, z: (y, x, c, z + step) if c == 0 else (y + step, x, c, z)


def to_second(step):
    return lambda y, x, c, z: (y + step, x, c, z) if c == 0 else (y, x, c, z + step)


def send(value, route):
    return lax.ppermute(value, GROUP, pairs(route))


def params(mib=24):
    return pltpu.CompilerParams(vmem_limit_bytes=mib << 20)


def placed(at_ref):
    y, x, c, z = (at_ref[i] for i in range(4))
    at = lax.broadcasted_iota(jnp.int32, (ROWS, 1), 0)
    r, xr, z4, q1, q2, cr = at & 1, (at >> 1) & 1, (at >> 2) & 1, (at >> 3) & 3, (at >> 5) & 3, at >> 7
    o1 = jnp.where(q1 == 2, -1, jnp.where(q1 == 3, 2, q1))
    o2 = jnp.where(q2 == 2, -1, jnp.where(q2 == 3, 2, q2))
    core = c ^ cr
    zo = jnp.where(core == 0, o1, o2) + 4 * z4
    yo = jnp.where(core == 0, o2, o1)
    rows = ((((y + yo) & 3) * 2 + (x ^ xr)) * 2 + core) * 16 + ((z + zo) & 7) * 2 + r
    return rows == lax.broadcasted_iota(jnp.int32, (ROWS, ROWS), 1)


def hits(at_ref, targets_ref, place):
    own = jnp.sum(jnp.where(place, targets_ref[...], 0), axis=1, keepdims=True) - at_ref[4]
    return lax.broadcasted_iota(jnp.int32, (ROWS, WIDTH), 1) == own


def column_copies(source, target, sems):
    cuts = [pl.ds(k * CHUNK, CHUNK) for k in range(STEPS)]
    return [pltpu.make_async_copy(source.at[:, cut], target.at[:, cut], sems.at[k]) for k, cut in enumerate(cuts)]


def weight_copies(source, target, sems):
    cuts = [pl.ds(k * CHUNK, CHUNK) for k in range(STEPS)]
    copies = [pltpu.make_async_copy(source.at[cut], target.at[cut], sems.at[k]) for k, cut in enumerate(cuts)]
    for copy in copies:
        copy.start()
    return copies


def logits_kernel(at_ref, targets_ref, p0, p1, p2, p3, p4, p5, p6, p7, w_hbm, logits_ref, stats_ref, w_ref, w_sems):
    acc = jnp.zeros((ROWS, WIDTH), F32)
    for k, copy in enumerate(weight_copies(w_hbm, w_ref, w_sems)):
        cut = slice(k * CHUNK, (k + 1) * CHUNK)
        left = jnp.concatenate([p[:, cut] for p in (p0, p1, p2, p3, p4, p5, p6, p7)], axis=0)
        copy.wait()
        acc += jnp.dot(left, w_ref[cut, :], preferred_element_type=F32)
    logits_ref[...] = acc
    top = jnp.max(acc, axis=1, keepdims=True)
    total = jnp.sum(jnp.exp(acc - top), axis=1, keepdims=True)
    place = placed(at_ref)
    picked = jnp.sum(jnp.where(hits(at_ref, targets_ref, place), acc, 0.0), axis=1, keepdims=True)
    for i, column in enumerate((top, total, picked)):
        stats_ref[i : i + 1, :] = jnp.sum(jnp.where(place, column, 0.0), axis=0, keepdims=True)


def products(left, copies, w_ref, pairs):
    for k, copy in enumerate(copies):
        cut = slice(k * CHUNK, (k + 1) * CHUNK)
        copy.wait()
        part = lax.dot_general(left, w_ref[cut, :], (((1,), (1,)), ((), ())), preferred_element_type=F32)
        first = 0
        for buffer, outs in pairs:
            buffer[:, cut] = part[first : first + buffer.shape[0]].astype(buffer.dtype)
            outs[k].start()
            first += buffer.shape[0]
    for _, outs in pairs:
        for copy in outs:
            copy.wait()


def target_kernel(at_ref, targets_ref, w_hbm, own_hbm, other_hbm, w_ref, own_ref, other_ref, w_sems, own_sems, other_sems):
    copies = weight_copies(w_hbm, w_ref, w_sems)
    left = jnp.where(hits(at_ref, targets_ref, placed(at_ref)), 1.0, 0.0).astype(BF)
    own = (own_ref, column_copies(own_ref, own_hbm, own_sems))
    other = (other_ref, column_copies(other_ref, other_hbm, other_sems))
    products(left, copies, w_ref, (own, other))


def soft_kernel(start, at_ref, targets_ref, top_ref, logits_ref, w_hbm, soft_hbm, w_ref, soft_ref, w_sems, soft_sems):
    copies = weight_copies(w_hbm, w_ref, w_sems)
    cut = slice(start, start + ROWS // 2)
    place = placed(at_ref)
    top = jnp.sum(jnp.where(place[cut], top_ref[...], 0.0), axis=1, keepdims=True)
    hit = hits(at_ref, targets_ref, place)[cut]
    left = jnp.where(hit, 0.0, jnp.exp(logits_ref[cut, :] - top)).astype(BF)
    products(left, copies, w_ref, ((soft_ref, column_copies(soft_ref, soft_hbm, soft_sems)),))


def merge_kernel(own_ref, core_ref, x_ref, both_ref, out_ref, top_ref):
    refs = (own_ref, core_ref, x_ref, both_ref)
    tops = [r[0:1, :] for r in refs]
    top = jnp.maximum(jnp.maximum(tops[0], tops[1]), jnp.maximum(tops[2], tops[3]))
    total = sum(r[1:2, :] * jnp.exp(t - top) for r, t in zip(refs, tops))
    picked = sum(r[2:3, :] for r in refs)
    merged = jnp.concatenate([top, total, picked], axis=0)
    for i in range(out_ref.shape[0]):
        out_ref[i] = merged
    top_ref[...] = top


def scales_kernel(at_ref, grad_ref, top_ref, spread_ref, out_ref):
    place = placed(at_ref)[: ROWS // 2]

    def ordered(row):
        return jnp.sum(jnp.where(place, row, 0.0), axis=1, keepdims=True)

    tops = spread_ref[:, 0, :]
    highest = jnp.max(tops, axis=0, keepdims=True)
    total = jnp.sum(spread_ref[:, 1, :] * jnp.exp(tops - highest), axis=0, keepdims=True)
    log_total = ordered(highest + jnp.log(total))
    picked = ordered(jnp.sum(spread_ref[:, 2, :], axis=0, keepdims=True))
    top = ordered(top_ref[...])
    factor = 1.0 + 2.0 * zloss_coef * log_total
    grad = ordered(grad_ref[...])
    scale = grad * factor * jnp.exp(top - log_total)
    target = (grad * (jnp.exp(picked - log_total) * factor - 1.0)).astype(BF).astype(F32)
    lane = lax.broadcasted_iota(jnp.int32, (ROWS // 2, 128), 1)
    out_ref[...] = jnp.where(lane == 0, scale, jnp.where(lane == 1, target, jnp.where(lane == 2, log_total, picked)))


def combine_kernel(parts, scales_ref, soft_own, soft_in, target_own, target_in, *refs):
    outs, (a_ref, b_ref, c_ref, d_ref, sems) = refs[: len(parts)], refs[len(parts) :]
    every = []
    for i, q in enumerate(parts):
        sources = ((soft_own, a_ref), (soft_in, b_ref), (target_own, c_ref), (target_in, d_ref))
        every.append(
            [pltpu.make_async_copy(s.at[pl.ds(32 * q, 32)], t.at[i], sems.at[i, j]) for j, (s, t) in enumerate(sources)]
        )
        for copy in every[-1]:
            copy.start()
    for i, (q, out) in enumerate(zip(parts, outs)):
        for copy in every[i]:
            copy.wait()
        scale, target = scales_ref[32 * q : 32 * q + 32, 0:1], scales_ref[32 * q : 32 * q + 32, 1:2]
        for k in range(0, DEPTH, CHUNK):
            cut = slice(k, k + CHUNK)
            soft = a_ref[i, :, cut] + b_ref[i, :, cut].astype(F32)
            chosen = c_ref[i, :, cut].astype(F32) + d_ref[i, :, cut].astype(F32)
            out[:, cut] = (scale * soft + target * chosen).astype(out.dtype)


def shards(hidden, lm_weight, targets, loss_grad):
    half = ROWS // 2
    at = jnp.stack([lax.axis_index(a) for a in GROUP] + [lax.axis_index(GROUP) * WIDTH])
    targets, loss_grad = targets.reshape(1, ROWS), loss_grad.reshape(1, ROWS)
    lm_weight = pltpu.with_memory_space_constraint(lm_weight, pltpu.HBM)
    weights = [pltpu.VMEM((DEPTH, WIDTH), BF)]
    sems = pltpu.SemaphoreType.DMA((STEPS,))

    block = jnp.concatenate([hidden] + [send(hidden, to) for to in (to_x, to_z4, to_xz4)])
    far, near, back = (send(block, to_first(-o)) for o in (2, 1, -1))
    block = jnp.concatenate([block, near, back, far])
    far, near, back = (send(block, to_second(-o)) for o in (2, 1, -1))

    aim, _ = lax.optimization_barrier((targets, block))
    target_own, target_out = pl.pallas_call(
        target_kernel,
        out_shape=[pltpu.HBM((half, DEPTH), BF)] * 2,
        in_specs=[SMEM, VMEM, ANY],
        out_specs=[HBM] * 2,
        scratch_shapes=weights + [pltpu.VMEM((half, DEPTH), BF)] * 2 + [sems] * 3,
        compiler_params=params(),
        cost_estimate=pl.CostEstimate(flops=2 * ROWS * DEPTH * WIDTH, bytes_accessed=12 << 20, transcendentals=0),
        name="target",
    )(at, aim, lm_weight)
    near, target_own, target_out = lax.optimization_barrier((near, target_own, target_out))
    pieces = [block, near, back, far]
    pieces = pieces + [send(p, to_c) for p in pieces]
    target_in = send(target_out, to_c)

    logits, stats = pl.pallas_call(
        logits_kernel,
        out_shape=(jax.ShapeDtypeStruct((ROWS, WIDTH), F32), jax.ShapeDtypeStruct((3, ROWS), F32)),
        in_specs=[SMEM] + [VMEM] * 9 + [ANY],
        out_specs=(VMEM, VMEM),
        scratch_shapes=weights + [sems],
        compiler_params=params(),
        cost_estimate=pl.CostEstimate(flops=2 * ROWS * DEPTH * WIDTH, bytes_accessed=13 << 20, transcendentals=ROWS * WIDTH),
        name="logits",
    )(at, targets, *pieces, lm_weight)
    stats = [stats] + [send(stats, to) for to in (to_c, to_x, to_xc)]
    merged, top = pl.pallas_call(
        merge_kernel,
        out_shape=(jax.ShapeDtypeStruct((32, 3, ROWS), F32), jax.ShapeDtypeStruct((1, ROWS), F32)),
        in_specs=[VMEM] * 4,
        out_specs=(VMEM, VMEM),
        compiler_params=params(),
        name="merge",
    )(*stats)
    spread = lax.all_to_all(merged, ("y", "z"), 0, 0)

    same_top = send(top, to_c)

    def soft(start, dtype):
        return pl.pallas_call(
            functools.partial(soft_kernel, start),
            out_shape=pltpu.HBM((half, DEPTH), dtype),
            in_specs=[SMEM, VMEM, VMEM, VMEM, ANY],
            out_specs=HBM,
            scratch_shapes=weights + [pltpu.VMEM((half, DEPTH), dtype)] + [sems] * 2,
            compiler_params=params(),
            cost_estimate=pl.CostEstimate(flops=ROWS * DEPTH * WIDTH, bytes_accessed=10 << 20, transcendentals=0),
            name="soft",
        )(at, targets, same_top, logits, lm_weight)

    soft_in = send(soft(half, BF), to_c)
    soft_own = soft(0, F32)
    scales = pl.pallas_call(
        scales_kernel,
        out_shape=jax.ShapeDtypeStruct((half, 128), F32),
        in_specs=[SMEM] + [VMEM] * 3,
        out_specs=VMEM,
        compiler_params=params(),
        name="scales",
    )(at, loss_grad, top, spread)

    def combine(parts, dtype):
        n = len(parts)
        return pl.pallas_call(
            functools.partial(combine_kernel, parts),
            out_shape=[jax.ShapeDtypeStruct((32, DEPTH), dtype)] * n,
            in_specs=[VMEM] + [ANY] * 4,
            out_specs=[VMEM] * n,
            scratch_shapes=[pltpu.VMEM((n, 32, DEPTH), F32)]
            + [pltpu.VMEM((n, 32, DEPTH), BF)] * 3
            + [pltpu.SemaphoreType.DMA((n, 4))],
            compiler_params=params(),
            cost_estimate=pl.CostEstimate(flops=6 * 32 * DEPTH * n, bytes_accessed=n * (3 << 20), transcendentals=0),
            name="combine",
        )(scales, soft_own, soft_in, target_own, target_in)

    far = combine((3,), BF)
    near, back = combine((1, 2), BF)
    arrived = [send(p, to_second(o)).astype(F32) for p, o in ((far[0], 2), (near, 1), (back, -1))]
    part = combine((0,), F32)[0] + sum(arrived)
    log_total, target_logit = scales[:2, 2], scales[:2, 3]
    ce_loss = log_total - target_logit
    z_term = zloss_coef * log_total * log_total

    part = part.reshape(4, 8, DEPTH)
    part = part[0] + sum(send(part[k].astype(BF), to_first(OFFSETS[k])).astype(F32) for k in (3, 1, 2))
    part = [part[0:2]] + [
        send(part[2 * k : 2 * k + 2], to) for k, to in ((3, to_xz4), (2, to_z4), (1, to_x))
    ]
    part = (part[0] + part[1]) + (part[2] + part[3])
    return ce_loss, z_term, part.astype(BF)


def solution(mesh):
    mesh = Mesh(mesh.devices.reshape(NY, NX, NC, NZ, 2), (*GROUP, "dp"))
    own = ("dp", *GROUP)
    in_specs = (P(own, None), P(None, GROUP), P("dp"), P("dp"))
    out_specs = (P(own), P(own), P(own, None))
    return jax.shard_map(shards, mesh=mesh, in_specs=in_specs, out_specs=out_specs, check_vma=False)
```

```python
import functools

import jax
import jax.numpy as jnp
from jax import lax
from jax.experimental import pallas as pl
from jax.experimental.pallas import tpu as pltpu
from jax.sharding import Mesh
from jax.sharding import PartitionSpec as P

zloss_coef = 0.0001
NY, NX, NC, NZ = 4, 2, 2, 8
GROUP = ("y", "x", "c", "z")
OFFSETS = (0, 1, -1, 2)
BF, F32 = jnp.bfloat16, jnp.float32
ROWS, DEPTH, WIDTH = 256, 8192, 512
CHUNK = 1024
STEPS = DEPTH // CHUNK
VMEM = pl.BlockSpec(memory_space=pltpu.VMEM)
SMEM = pl.BlockSpec(memory_space=pltpu.SMEM)
ANY = pl.BlockSpec(memory_space=pl.ANY)
HBM = pl.BlockSpec(memory_space=pltpu.HBM)


def index_of(y, x, c, z):
    return (((y % NY) * NX + x % NX) * NC + c % NC) * NZ + z % NZ


def pairs(route):
    every = [(y, x, c, z) for y in range(NY) for x in range(NX) for c in range(NC) for z in range(NZ)]
    return [(index_of(*p), index_of(*route(*p))) for p in every]


def to_x(y, x, c, z):
    return y, x + 1, c, z


def to_c(y, x, c, z):
    return y, x, c + 1, z


def to_z4(y, x, c, z):
    return y, x, c, z + 4


def to_xc(y, x, c, z):
    return y, x + 1, c + 1, z


def to_xz4(y, x, c, z):
    return y, x + 1, c, z + 4


def to_first(step):
    return lambda y, x, c, z: (y, x, c, z + step) if c == 0 else (y + step, x, c, z)


def to_second(step):
    return lambda y, x, c, z: (y + step, x, c, z) if c == 0 else (y, x, c, z + step)


def send(value, route):
    return lax.ppermute(value, GROUP, pairs(route))


def params(mib=24):
    return pltpu.CompilerParams(vmem_limit_bytes=mib << 20)


def placed(at_ref):
    y, x, c, z = (at_ref[i] for i in range(4))
    at = lax.broadcasted_iota(jnp.int32, (ROWS, 1), 0)
    r, near, q1, q2, cr = at & 1, (at >> 1) & 3, (at >> 3) & 3, (at >> 5) & 3, at >> 7
    xr, z4 = near & 1, near >> 1
    o1 = jnp.where(q1 == 2, -1, jnp.where(q1 == 3, 2, q1))
    o2 = jnp.where(q2 == 2, -1, jnp.where(q2 == 3, 2, q2))
    core = c ^ cr
    zo = jnp.where(core == 0, o1, o2) + 4 * z4
    yo = jnp.where(core == 0, o2, o1)
    rows = ((((y + yo) & 3) * 2 + (x ^ xr)) * 2 + core) * 16 + ((z + zo) & 7) * 2 + r
    return rows == lax.broadcasted_iota(jnp.int32, (ROWS, ROWS), 1)


def hits(at_ref, targets_ref, place):
    own = jnp.sum(jnp.where(place, targets_ref[...], 0), axis=1, keepdims=True) - at_ref[4]
    return lax.broadcasted_iota(jnp.int32, (ROWS, WIDTH), 1) == own


def column_copies(source, target, sems):
    cuts = [pl.ds(k * CHUNK, CHUNK) for k in range(STEPS)]
    return [pltpu.make_async_copy(source.at[:, cut], target.at[:, cut], sems.at[k]) for k, cut in enumerate(cuts)]


def weight_copies(source, target, sems):
    cuts = [pl.ds(k * CHUNK, CHUNK) for k in range(STEPS)]
    copies = [pltpu.make_async_copy(source.at[cut], target.at[cut], sems.at[k]) for k, cut in enumerate(cuts)]
    for copy in copies:
        copy.start()
    return copies


def logits_kernel(at_ref, targets_ref, p0, p1, p2, p3, p4, p5, p6, p7, w_hbm, stats_ref, own_hbm, other_hbm, w_ref, own_ref, other_ref, w_sems, own_sems, other_sems):
    acc = jnp.zeros((ROWS, WIDTH), F32)
    for k, copy in enumerate(weight_copies(w_hbm, w_ref, w_sems)):
        cut = slice(k * CHUNK, (k + 1) * CHUNK)
        left = jnp.concatenate([p[:, cut] for p in (p0, p1, p2, p3, p4, p5, p6, p7)], axis=0)
        copy.wait()
        acc += jnp.dot(left, w_ref[cut, :], preferred_element_type=F32)
    top = jnp.max(acc, axis=1, keepdims=True)
    soft = jnp.exp(acc - top)
    total = jnp.sum(soft, axis=1, keepdims=True)
    place = placed(at_ref)
    hit = hits(at_ref, targets_ref, place)
    picked = jnp.sum(jnp.where(hit, acc, 0.0), axis=1, keepdims=True)
    for i, column in enumerate((top, total, picked)):
        stats_ref[i : i + 1, :] = jnp.sum(jnp.where(place, column, 0.0), axis=0, keepdims=True)
    own = (own_ref, column_copies(own_ref, own_hbm, own_sems))
    other = (other_ref, column_copies(other_ref, other_hbm, other_sems))
    products(jnp.where(hit, 0.0, soft).astype(BF), None, w_ref, (own, other))


def products(left, copies, w_ref, pairs):
    for k in range(STEPS):
        cut = slice(k * CHUNK, (k + 1) * CHUNK)
        if copies is not None:
            copies[k].wait()
        part = lax.dot_general(left, w_ref[cut, :], (((1,), (1,)), ((), ())), preferred_element_type=F32)
        first = 0
        for buffer, outs in pairs:
            buffer[:, cut] = part[first : first + buffer.shape[0]].astype(buffer.dtype)
            outs[k].start()
            first += buffer.shape[0]
    for _, outs in pairs:
        for copy in outs:
            copy.wait()


def target_kernel(at_ref, targets_ref, w_hbm, own_hbm, other_hbm, w_ref, own_ref, other_ref, w_sems, own_sems, other_sems):
    copies = weight_copies(w_hbm, w_ref, w_sems)
    left = jnp.where(hits(at_ref, targets_ref, placed(at_ref)), 1.0, 0.0).astype(BF)
    own = (own_ref, column_copies(own_ref, own_hbm, own_sems))
    other = (other_ref, column_copies(other_ref, other_hbm, other_sems))
    products(left, copies, w_ref, (own, other))


def merge_kernel(own_ref, core_ref, x_ref, both_ref, out_ref):
    refs = (own_ref, core_ref, x_ref, both_ref)
    tops = [r[0:1, :] for r in refs]
    top = jnp.maximum(jnp.maximum(tops[0], tops[1]), jnp.maximum(tops[2], tops[3]))
    total = sum(r[1:2, :] * jnp.exp(t - top) for r, t in zip(refs, tops))
    picked = sum(r[2:3, :] for r in refs)
    merged = jnp.concatenate([top, total, picked], axis=0)
    for i in range(out_ref.shape[0]):
        out_ref[i] = merged


def scales_kernel(at_ref, grad_ref, own_ref, core_ref, spread_ref, out_ref):
    place = placed(at_ref)[: ROWS // 2]

    def ordered(row):
        return jnp.sum(jnp.where(place, row, 0.0), axis=1, keepdims=True)

    tops = spread_ref[:, 0, :]
    highest = jnp.max(tops, axis=0, keepdims=True)
    total = jnp.sum(spread_ref[:, 1, :] * jnp.exp(tops - highest), axis=0, keepdims=True)
    log_total = ordered(highest + jnp.log(total))
    picked = ordered(jnp.sum(spread_ref[:, 2, :], axis=0, keepdims=True))
    factor = 1.0 + 2.0 * zloss_coef * log_total
    grad = ordered(grad_ref[...])
    target = (grad * (jnp.exp(picked - log_total) * factor - 1.0)).astype(BF).astype(F32)
    own, core = (grad * factor * jnp.exp(ordered(ref[0:1, :]) - log_total) for ref in (own_ref, core_ref))
    lane = lax.broadcasted_iota(jnp.int32, (ROWS // 2, 128), 1)
    rest = jnp.where(lane == 2, target, jnp.where(lane == 3, log_total, picked))
    out_ref[...] = jnp.where(lane == 0, own, jnp.where(lane == 1, core, rest))


def combine_kernel(parts, scales_ref, soft_own, soft_in, target_own, target_in, *refs):
    outs, (a_ref, b_ref, c_ref, d_ref, sems) = refs[: len(parts)], refs[len(parts) :]
    every = []
    for i, q in enumerate(parts):
        sources = ((soft_own, a_ref), (soft_in, b_ref), (target_own, c_ref), (target_in, d_ref))
        every.append(
            [pltpu.make_async_copy(s.at[pl.ds(32 * q, 32)], t.at[i], sems.at[i, j]) for j, (s, t) in enumerate(sources)]
        )
        for copy in every[-1]:
            copy.start()
    for i, (q, out) in enumerate(zip(parts, outs)):
        for copy in every[i]:
            copy.wait()
        own, core, target = (scales_ref[32 * q : 32 * q + 32, i : i + 1] for i in range(3))
        for k in range(0, DEPTH, CHUNK):
            cut = slice(k, k + CHUNK)
            soft = own * a_ref[i, :, cut] + core * b_ref[i, :, cut].astype(F32)
            chosen = c_ref[i, :, cut].astype(F32) + d_ref[i, :, cut].astype(F32)
            out[:, cut] = (soft + target * chosen).astype(out.dtype)


def shards(hidden, lm_weight, targets, loss_grad):
    half = ROWS // 2
    at = jnp.stack([lax.axis_index(a) for a in GROUP] + [lax.axis_index(GROUP) * WIDTH])
    targets, loss_grad = targets.reshape(1, ROWS), loss_grad.reshape(1, ROWS)
    lm_weight = pltpu.with_memory_space_constraint(lm_weight, pltpu.HBM)
    weights = [pltpu.VMEM((DEPTH, WIDTH), BF)]
    sems = pltpu.SemaphoreType.DMA((STEPS,))

    block = jnp.concatenate([hidden] + [send(hidden, to) for to in (to_x, to_z4, to_xz4)])
    block = jnp.concatenate([block] + [send(block, to_first(-o)) for o in OFFSETS[1:]])
    near, back, far = (send(block, to_second(-o)) for o in OFFSETS[1:])

    aim, _ = lax.optimization_barrier((targets, block))
    target_own, target_out = pl.pallas_call(
        target_kernel,
        out_shape=[pltpu.HBM((half, DEPTH), BF)] * 2,
        in_specs=[SMEM, VMEM, ANY],
        out_specs=[HBM] * 2,
        scratch_shapes=weights + [pltpu.VMEM((half, DEPTH), BF)] * 2 + [sems] * 3,
        compiler_params=params(),
        cost_estimate=pl.CostEstimate(flops=2 * ROWS * DEPTH * WIDTH, bytes_accessed=12 << 20, transcendentals=0),
        name="target",
    )(at, aim, lm_weight)
    far, target_own, target_out = lax.optimization_barrier((far, target_own, target_out))
    pieces = [block, near, back, far]
    pieces = pieces + [send(p, to_c) for p in pieces]

    stats, soft_own, soft_out = pl.pallas_call(
        logits_kernel,
        out_shape=(jax.ShapeDtypeStruct((3, ROWS), F32), pltpu.HBM((half, DEPTH), F32), pltpu.HBM((half, DEPTH), BF)),
        in_specs=[SMEM] + [VMEM] * 9 + [ANY],
        out_specs=(VMEM, HBM, HBM),
        scratch_shapes=weights + [pltpu.VMEM((half, DEPTH), F32), pltpu.VMEM((half, DEPTH), BF)] + [sems] * 3,
        compiler_params=params(32),
        cost_estimate=pl.CostEstimate(flops=4 * ROWS * DEPTH * WIDTH, bytes_accessed=19 << 20, transcendentals=ROWS * WIDTH),
        name="logits",
    )(at, targets, *pieces, lm_weight)
    stats = [stats] + [send(stats, to) for to in (to_c, to_x, to_xc)]
    merged = pl.pallas_call(
        merge_kernel,
        out_shape=jax.ShapeDtypeStruct((32, 3, ROWS), F32),
        in_specs=[VMEM] * 4,
        out_specs=VMEM,
        compiler_params=params(),
        name="merge",
    )(*stats)
    merged, soft_out, target_out = lax.optimization_barrier((merged, soft_out, target_out))
    soft_in, target_in = send(soft_out, to_c), send(target_out, to_c)
    spread = lax.all_to_all(merged, ("y", "z"), 0, 0)

    scales = pl.pallas_call(
        scales_kernel,
        out_shape=jax.ShapeDtypeStruct((half, 128), F32),
        in_specs=[SMEM] + [VMEM] * 4,
        out_specs=VMEM,
        compiler_params=params(),
        name="scales",
    )(at, loss_grad, stats[0], stats[1], spread)

    soft_own, target_own = (pltpu.with_memory_space_constraint(v, pltpu.HBM) for v in (soft_own, target_own))

    def combine(parts, dtype):
        n = len(parts)
        return pl.pallas_call(
            functools.partial(combine_kernel, parts),
            out_shape=[jax.ShapeDtypeStruct((32, DEPTH), dtype)] * n,
            in_specs=[VMEM] + [ANY] * 4,
            out_specs=[VMEM] * n,
            scratch_shapes=[pltpu.VMEM((n, 32, DEPTH), F32)]
            + [pltpu.VMEM((n, 32, DEPTH), BF)] * 3
            + [pltpu.SemaphoreType.DMA((n, 4))],
            compiler_params=params(),
            cost_estimate=pl.CostEstimate(flops=6 * 32 * DEPTH * n, bytes_accessed=n * (3 << 20), transcendentals=0),
            name="combine",
        )(scales, soft_own, soft_in, target_own, target_in)

    parts = combine((3,), BF) + combine((1, 2), BF)
    arrived = [send(p, to_second(o)).astype(F32) for p, o in zip(parts, (2, 1, -1))]
    part = combine((0,), F32)[0] + sum(arrived)
    log_total, target_logit = scales[:2, 3], scales[:2, 4]
    ce_loss = log_total - target_logit
    z_term = zloss_coef * log_total * log_total

    part = part.reshape(4, 8, DEPTH)
    part = part[0] + sum(send(part[k].astype(BF), to_first(OFFSETS[k])).astype(F32) for k in (3, 1, 2))
    part = [part[0:2]] + [
        send(part[2 * k : 2 * k + 2], to) for k, to in ((1, to_x), (2, to_z4), (3, to_xz4))
    ]
    part = (part[0] + part[1]) + (part[2] + part[3])
    return ce_loss, z_term, part.astype(BF)


def solution(mesh):
    mesh = Mesh(mesh.devices.reshape(NY, NX, NC, NZ, 2), (*GROUP, "dp"))
    own = ("dp", *GROUP)
    in_specs = (P(own, None), P(None, GROUP), P("dp"), P("dp"))
    out_specs = (P(own), P(own), P(own, None))
    return jax.shard_map(shards, mesh=mesh, in_specs=in_specs, out_specs=out_specs, check_vma=False)
```

```python
import functools

import jax
import jax.numpy as jnp
from jax import lax
from jax.experimental import pallas as pl
from jax.experimental.pallas import tpu as pltpu
from jax.sharding import Mesh
from jax.sharding import PartitionSpec as P

zloss_coef = 0.0001
NY, NX, NC, NZ = 4, 2, 2, 8
GROUP = ("y", "x", "c", "z")
OFFSETS = (0, 1, -1, 2)
BF, F32 = jnp.bfloat16, jnp.float32
ROWS, DEPTH, WIDTH = 256, 8192, 512
CHUNK = 1024
STEPS = DEPTH // CHUNK
VMEM = pl.BlockSpec(memory_space=pltpu.VMEM)
SMEM = pl.BlockSpec(memory_space=pltpu.SMEM)
ANY = pl.BlockSpec(memory_space=pl.ANY)
HBM = pl.BlockSpec(memory_space=pltpu.HBM)


def index_of(y, x, c, z):
    return (((y % NY) * NX + x % NX) * NC + c % NC) * NZ + z % NZ


def pairs(route):
    every = [(y, x, c, z) for y in range(NY) for x in range(NX) for c in range(NC) for z in range(NZ)]
    return [(index_of(*p), index_of(*route(*p))) for p in every]


def to_x(y, x, c, z):
    return y, x + 1, c, z


def to_c(y, x, c, z):
    return y, x, c + 1, z


def to_z4(y, x, c, z):
    return y, x, c, z + 4


def to_xc(y, x, c, z):
    return y, x + 1, c + 1, z


def to_xz4(y, x, c, z):
    return y, x + 1, c, z + 4


def to_first(step):
    return lambda y, x, c, z: (y, x, c, z + step) if c == 0 else (y + step, x, c, z)


def to_second(step):
    return lambda y, x, c, z: (y + step, x, c, z) if c == 0 else (y, x, c, z + step)


def send(value, route):
    return lax.ppermute(value, GROUP, pairs(route))


def params(mib=24):
    return pltpu.CompilerParams(vmem_limit_bytes=mib << 20)


def placed(at_ref):
    y, x, c, z = (at_ref[i] for i in range(4))
    at = lax.broadcasted_iota(jnp.int32, (ROWS, 1), 0)
    r, near, q1, q2, cr = at & 1, (at >> 1) & 3, (at >> 3) & 3, (at >> 5) & 3, at >> 7
    xr, z4 = near & 1, near >> 1
    o1 = jnp.where(q1 == 2, -1, jnp.where(q1 == 3, 2, q1))
    o2 = jnp.where(q2 == 2, -1, jnp.where(q2 == 3, 2, q2))
    core = c ^ cr
    zo = jnp.where(core == 0, o1, o2) + 4 * z4
    yo = jnp.where(core == 0, o2, o1)
    rows = ((((y + yo) & 3) * 2 + (x ^ xr)) * 2 + core) * 16 + ((z + zo) & 7) * 2 + r
    return rows == lax.broadcasted_iota(jnp.int32, (ROWS, ROWS), 1)


def hits(at_ref, targets_ref, place):
    own = jnp.sum(jnp.where(place, targets_ref[...], 0), axis=1, keepdims=True) - at_ref[4]
    return lax.broadcasted_iota(jnp.int32, (ROWS, WIDTH), 1) == own


def column_copies(source, target, sems):
    cuts = [pl.ds(k * CHUNK, CHUNK) for k in range(STEPS)]
    return [pltpu.make_async_copy(source.at[:, cut], target.at[:, cut], sems.at[k]) for k, cut in enumerate(cuts)]


def weight_copies(source, target, sems):
    cuts = [pl.ds(k * CHUNK, CHUNK) for k in range(STEPS)]
    copies = [pltpu.make_async_copy(source.at[cut], target.at[cut], sems.at[k]) for k, cut in enumerate(cuts)]
    for copy in copies:
        copy.start()
    return copies


def logits_kernel(at_ref, targets_ref, p0, p1, p2, p3, p4, p5, p6, p7, w_hbm, stats_ref, own_hbm, other_hbm, w_ref, own_ref, other_ref, w_sems, own_sems, other_sems):
    acc = jnp.zeros((ROWS, WIDTH), F32)
    for k, copy in enumerate(weight_copies(w_hbm, w_ref, w_sems)):
        cut = slice(k * CHUNK, (k + 1) * CHUNK)
        left = jnp.concatenate([p[:, cut] for p in (p0, p1, p2, p3, p4, p5, p6, p7)], axis=0)
        copy.wait()
        acc += jnp.dot(left, w_ref[cut, :], preferred_element_type=F32)
    top = jnp.max(acc, axis=1, keepdims=True)
    soft = jnp.exp(acc - top)
    total = jnp.sum(soft, axis=1, keepdims=True)
    place = placed(at_ref)
    hit = hits(at_ref, targets_ref, place)
    picked = jnp.sum(jnp.where(hit, acc, 0.0), axis=1, keepdims=True)
    for i, column in enumerate((top, total, picked)):
        stats_ref[i : i + 1, :] = jnp.sum(jnp.where(place, column, 0.0), axis=0, keepdims=True)
    own = (own_ref, column_copies(own_ref, own_hbm, own_sems))
    other = (other_ref, column_copies(other_ref, other_hbm, other_sems))
    products(jnp.where(hit, 0.0, soft).astype(BF), None, w_ref, (own, other))


def products(left, copies, w_ref, pairs):
    for k in range(STEPS):
        cut = slice(k * CHUNK, (k + 1) * CHUNK)
        if copies is not None:
            copies[k].wait()
        part = lax.dot_general(left, w_ref[cut, :], (((1,), (1,)), ((), ())), preferred_element_type=F32)
        first = 0
        for buffer, outs in pairs:
            buffer[:, cut] = part[first : first + buffer.shape[0]].astype(buffer.dtype)
            outs[k].start()
            first += buffer.shape[0]
    for _, outs in pairs:
        for copy in outs:
            copy.wait()


def target_kernel(at_ref, targets_ref, w_hbm, own_hbm, other_hbm, w_ref, own_ref, other_ref, w_sems, own_sems, other_sems):
    copies = weight_copies(w_hbm, w_ref, w_sems)
    left = jnp.where(hits(at_ref, targets_ref, placed(at_ref)), 1.0, 0.0).astype(BF)
    own = (own_ref, column_copies(own_ref, own_hbm, own_sems))
    other = (other_ref, column_copies(other_ref, other_hbm, other_sems))
    products(left, copies, w_ref, (own, other))


def merge_kernel(own_ref, core_ref, x_ref, both_ref, out_ref):
    refs = (own_ref, core_ref, x_ref, both_ref)
    tops = [r[0:1, :] for r in refs]
    top = jnp.maximum(jnp.maximum(tops[0], tops[1]), jnp.maximum(tops[2], tops[3]))
    total = sum(r[1:2, :] * jnp.exp(t - top) for r, t in zip(refs, tops))
    picked = sum(r[2:3, :] for r in refs)
    merged = jnp.concatenate([top, total, picked], axis=0)
    for i in range(out_ref.shape[0]):
        out_ref[i] = merged


def in_order(place):
    return lambda row: jnp.sum(jnp.where(place, row, 0.0), axis=1, keepdims=True)


def piece_copies(parts, pairs, sems):
    every = []
    for i, q in enumerate(parts):
        copies = [
            pltpu.make_async_copy(source.at[pl.ds(32 * q, 32)], buffer.at[i], sems.at[i, j])
            for j, (source, buffer) in enumerate(pairs)
        ]
        for copy in copies:
            copy.start()
        every.append(copies)
    return every


def target_pair_kernel(own_hbm, in_hbm, o1, o2, o3, a_ref, b_ref, sems):
    every = piece_copies((1, 2, 3), ((own_hbm, a_ref), (in_hbm, b_ref)), sems)
    for i, out in enumerate((o1, o2, o3)):
        for copy in every[i]:
            copy.wait()
        for k in range(0, DEPTH, CHUNK):
            cut = slice(k, k + CHUNK)
            out[:, cut] = (a_ref[i, :, cut].astype(F32) + b_ref[i, :, cut].astype(F32)).astype(BF)


def soft_pair_kernel(parts, at_ref, own_stats, core_stats, merged_ref, own_hbm, in_hbm, *refs):
    outs, (a_ref, b_ref, sems) = refs[: len(parts)], refs[len(parts) :]
    every = piece_copies(parts, ((own_hbm, a_ref), (in_hbm, b_ref)), sems)
    place = placed(at_ref)
    for i, (q, out) in enumerate(zip(parts, outs)):
        ordered = in_order(place[32 * q : 32 * q + 32])
        own, core = (ordered(jnp.exp(r[0:1, :] - merged_ref[0, 0:1, :])) for r in (own_stats, core_stats))
        for copy in every[i]:
            copy.wait()
        for k in range(0, DEPTH, CHUNK):
            cut = slice(k, k + CHUNK)
            out[:, cut] = (own * a_ref[i, :, cut] + core * b_ref[i, :, cut].astype(F32)).astype(BF)


def finish_kernel(at_ref, grad_ref, own_stats, core_stats, spread_ref, *refs):
    own_hbm, in_hbm, target_own, target_in = refs[:4]
    soft_hbm, target_hbm = refs[4:7], refs[7:10]
    out_ref, log_ref, a_ref, b_ref, c_ref, d_ref, soft_ref, target_ref, sems, in_sems = refs[10:]
    first = piece_copies((0,), ((own_hbm, a_ref), (in_hbm, b_ref), (target_own, c_ref), (target_in, d_ref)), sems)[0]
    rest = [pltpu.make_async_copy(h, soft_ref.at[i], in_sems.at[0, i]) for i, h in enumerate(soft_hbm)]
    rest += [pltpu.make_async_copy(h, target_ref.at[i], in_sems.at[1, i]) for i, h in enumerate(target_hbm)]
    for copy in rest:
        copy.start()
    ordered = in_order(placed(at_ref)[:32])
    tops = spread_ref[:, 0, :]
    highest = jnp.max(tops, axis=0, keepdims=True)
    total = jnp.sum(spread_ref[:, 1, :] * jnp.exp(tops - highest), axis=0, keepdims=True)
    log_row = highest + jnp.log(total)
    log_total = ordered(log_row)
    picked = ordered(jnp.sum(spread_ref[:, 2, :], axis=0, keepdims=True))
    log_ref[...] = jnp.where(lax.broadcasted_iota(jnp.int32, (8, 128), 1) == 0, log_total[:8], picked[:8])
    factor = 1.0 + 2.0 * zloss_coef * log_total
    grad = ordered(grad_ref[...])
    target = (grad * (jnp.exp(picked - log_total) * factor - 1.0)).astype(BF).astype(F32)
    y, c, z = at_ref[0], at_ref[2], at_ref[3]

    def scale(top_row):
        return grad * factor * ordered(jnp.exp(top_row - log_row))

    own, core = scale(own_stats[0:1, :]), scale(core_stats[0:1, :])
    others = []
    for o in OFFSETS[1:]:
        sender = jnp.where(c == 0, ((y - o) & 3) * NZ + z, y * NZ + ((z - o) & 7))
        others.append(scale(spread_ref[sender, 0:1, :]))
    for copy in first + rest:
        copy.wait()
    for k in range(0, DEPTH, CHUNK):
        cut = slice(k, k + CHUNK)
        soft = own * a_ref[0, :, cut] + core * b_ref[0, :, cut].astype(F32)
        chosen = c_ref[0, :, cut].astype(F32) + d_ref[0, :, cut].astype(F32)
        for i in range(3):
            soft += others[i] * soft_ref[i, :, cut].astype(F32)
            chosen += target_ref[i, :, cut].astype(F32)
        out_ref[:, cut] = soft + target * chosen


def shards(hidden, lm_weight, targets, loss_grad):
    half = ROWS // 2
    at = jnp.stack([lax.axis_index(a) for a in GROUP] + [lax.axis_index(GROUP) * WIDTH])
    targets, loss_grad = targets.reshape(1, ROWS), loss_grad.reshape(1, ROWS)
    lm_weight = pltpu.with_memory_space_constraint(lm_weight, pltpu.HBM)
    weights = [pltpu.VMEM((DEPTH, WIDTH), BF)]
    sems = pltpu.SemaphoreType.DMA((STEPS,))

    block = jnp.concatenate([hidden, send(hidden, to_x)])
    aim, block = lax.optimization_barrier((targets, block))
    target_own, target_out = pl.pallas_call(
        target_kernel,
        out_shape=[pltpu.HBM((half, DEPTH), BF)] * 2,
        in_specs=[SMEM, VMEM, ANY],
        out_specs=[HBM] * 2,
        scratch_shapes=weights + [pltpu.VMEM((half, DEPTH), BF)] * 2 + [sems] * 3,
        compiler_params=params(),
        cost_estimate=pl.CostEstimate(flops=2 * ROWS * DEPTH * WIDTH, bytes_accessed=12 << 20, transcendentals=0),
        name="target",
    )(at, aim, lm_weight)
    hop, target_out = lax.optimization_barrier((send(block, to_z4), target_out))
    target_in = send(target_out, to_c)
    block = jnp.concatenate([block, hop])
    block = jnp.concatenate([block] + [send(block, to_first(-o)) for o in OFFSETS[1:]])
    near, back, far = (send(block, to_second(-o)) for o in OFFSETS[1:])

    target_own = pltpu.with_memory_space_constraint(target_own, pltpu.HBM)
    target_parts = pl.pallas_call(
        target_pair_kernel,
        out_shape=[jax.ShapeDtypeStruct((32, DEPTH), BF)] * 3,
        in_specs=[ANY] * 2,
        out_specs=[VMEM] * 3,
        scratch_shapes=[pltpu.VMEM((3, 32, DEPTH), BF)] * 2 + [pltpu.SemaphoreType.DMA((3, 2))],
        compiler_params=params(),
        cost_estimate=pl.CostEstimate(flops=3 * 32 * DEPTH, bytes_accessed=5 << 20, transcendentals=0),
        name="target_pair",
    )(target_own, target_in)
    near, back, far, *target_parts = lax.optimization_barrier((near, back, far, *target_parts))
    target_got = [send(p, to_second(o)) for p, o in zip(target_parts, OFFSETS[1:])]
    pieces = [block, near, back, far]
    pieces = pieces + [send(p, to_c) for p in pieces]

    stats, soft_own, soft_out = pl.pallas_call(
        logits_kernel,
        out_shape=(jax.ShapeDtypeStruct((3, ROWS), F32), pltpu.HBM((half, DEPTH), F32), pltpu.HBM((half, DEPTH), BF)),
        in_specs=[SMEM] + [VMEM] * 9 + [ANY],
        out_specs=(VMEM, HBM, HBM),
        scratch_shapes=weights + [pltpu.VMEM((half, DEPTH), F32), pltpu.VMEM((half, DEPTH), BF)] + [sems] * 3,
        compiler_params=params(32),
        cost_estimate=pl.CostEstimate(flops=1 << 20, bytes_accessed=1 << 16, transcendentals=0),
        name="logits",
    )(at, targets, *pieces, lm_weight)
    stats = [stats] + [send(stats, to) for to in (to_c, to_x, to_xc)]
    merged = pl.pallas_call(
        merge_kernel,
        out_shape=jax.ShapeDtypeStruct((32, 3, ROWS), F32),
        in_specs=[VMEM] * 4,
        out_specs=VMEM,
        compiler_params=params(),
        name="merge",
    )(*stats)
    soft_own = pltpu.with_memory_space_constraint(soft_own, pltpu.HBM)

    def soft_pair(parts):
        n = len(parts)
        return pl.pallas_call(
            functools.partial(soft_pair_kernel, parts),
            out_shape=[jax.ShapeDtypeStruct((32, DEPTH), BF)] * n,
            in_specs=[SMEM] + [VMEM] * 3 + [ANY] * 2,
            out_specs=[VMEM] * n,
            scratch_shapes=[pltpu.VMEM((n, 32, DEPTH), F32), pltpu.VMEM((n, 32, DEPTH), BF), pltpu.SemaphoreType.DMA((n, 2))],
            compiler_params=params(),
            cost_estimate=pl.CostEstimate(flops=4 * 32 * DEPTH * n, bytes_accessed=n * (2 << 20), transcendentals=0),
            name="soft_pair",
        )(at, stats[0], stats[1], merged, soft_own, soft_in)

    soft_in = send(soft_out, to_c)
    (far,) = soft_pair((3,))
    near, back = soft_pair((1, 2))
    merged, near, back, far = lax.optimization_barrier((merged, near, back, far))
    soft_got = [send(p, to_second(o)) for p, o in zip((near, back, far), OFFSETS[1:])]
    spread = lax.all_to_all(merged, ("y", "z"), 0, 0)

    piece = pltpu.VMEM((1, 32, DEPTH), BF)
    part, logs = pl.pallas_call(
        finish_kernel,
        out_shape=(jax.ShapeDtypeStruct((32, DEPTH), F32), jax.ShapeDtypeStruct((8, 128), F32)),
        in_specs=[SMEM] + [VMEM] * 4 + [ANY] * 10,
        out_specs=(VMEM, VMEM),
        scratch_shapes=[pltpu.VMEM((1, 32, DEPTH), F32), piece, piece, piece]
        + [pltpu.VMEM((3, 32, DEPTH), BF)] * 2
        + [pltpu.SemaphoreType.DMA((1, 4)), pltpu.SemaphoreType.DMA((2, 3))],
        compiler_params=params(),
        cost_estimate=pl.CostEstimate(flops=16 * 32 * DEPTH, bytes_accessed=7 << 20, transcendentals=0),
        name="finish",
    )(at, loss_grad, stats[0], stats[1], spread, soft_own, soft_in, target_own, target_in, *soft_got, *target_got)
    log_total, target_logit = logs[:2, 0], logs[:2, 1]
    ce_loss = log_total - target_logit
    z_term = zloss_coef * log_total * log_total

    part = part.reshape(4, 8, DEPTH)
    part = part[0] + sum(send(part[k].astype(BF), to_first(OFFSETS[k])).astype(F32) for k in (3, 1, 2))
    part = [part[0:2]] + [
        send(part[2 * k : 2 * k + 2], to) for k, to in ((1, to_x), (2, to_z4), (3, to_xz4))
    ]
    part = (part[0] + part[1]) + (part[2] + part[3])
    return ce_loss, z_term, part.astype(BF)


def solution(mesh):
    mesh = Mesh(mesh.devices.reshape(NY, NX, NC, NZ, 2), (*GROUP, "dp"))
    own = ("dp", *GROUP)
    in_specs = (P(own, None), P(None, GROUP), P("dp"), P("dp"))
    out_specs = (P(own), P(own), P(own, None))
    return jax.shard_map(shards, mesh=mesh, in_specs=in_specs, out_specs=out_specs, check_vma=False)
```

```python
import functools

import jax
import jax.numpy as jnp
from jax import lax
from jax.experimental import pallas as pl
from jax.experimental.pallas import tpu as pltpu
from jax.sharding import Mesh
from jax.sharding import PartitionSpec as P

zloss_coef = 0.0001
NY, NX, NC, NZ = 4, 2, 2, 8
GROUP = ("y", "x", "c", "z")
OFFSETS = (0, 1, -1, 2)
BF, F32 = jnp.bfloat16, jnp.float32
ROWS, DEPTH, WIDTH = 256, 8192, 512
CHUNK = 1024
STEPS = DEPTH // CHUNK
VMEM = pl.BlockSpec(memory_space=pltpu.VMEM)
SMEM = pl.BlockSpec(memory_space=pltpu.SMEM)
ANY = pl.BlockSpec(memory_space=pl.ANY)
HBM = pl.BlockSpec(memory_space=pltpu.HBM)


def index_of(y, x, c, z):
    return (((y % NY) * NX + x % NX) * NC + c % NC) * NZ + z % NZ


def pairs(route):
    every = [(y, x, c, z) for y in range(NY) for x in range(NX) for c in range(NC) for z in range(NZ)]
    return [(index_of(*p), index_of(*route(*p))) for p in every]


def to_x(y, x, c, z):
    return y, x + 1, c, z


def to_c(y, x, c, z):
    return y, x, c + 1, z


def to_z4(y, x, c, z):
    return y, x, c, z + 4


def to_xc(y, x, c, z):
    return y, x + 1, c + 1, z


def to_xz4(y, x, c, z):
    return y, x + 1, c, z + 4


def to_first(step):
    return lambda y, x, c, z: (y, x, c, z + step) if c == 0 else (y + step, x, c, z)


def to_second(step):
    return lambda y, x, c, z: (y + step, x, c, z) if c == 0 else (y, x, c, z + step)


def send(value, route):
    return lax.ppermute(value, GROUP, pairs(route))


def params(mib=24):
    return pltpu.CompilerParams(vmem_limit_bytes=mib << 20)


def placed(at_ref):
    y, x, c, z = (at_ref[i] for i in range(4))
    at = lax.broadcasted_iota(jnp.int32, (ROWS, 1), 0)
    r, near, q1, q2, cr = at & 1, (at >> 1) & 3, (at >> 3) & 3, (at >> 5) & 3, at >> 7
    xr, z4 = near & 1, near >> 1
    o1 = jnp.where(q1 == 2, -1, jnp.where(q1 == 3, 2, q1))
    o2 = jnp.where(q2 == 2, -1, jnp.where(q2 == 3, 2, q2))
    core = c ^ cr
    zo = jnp.where(core == 0, o1, o2) + 4 * z4
    yo = jnp.where(core == 0, o2, o1)
    rows = ((((y + yo) & 3) * 2 + (x ^ xr)) * 2 + core) * 16 + ((z + zo) & 7) * 2 + r
    return rows == lax.broadcasted_iota(jnp.int32, (ROWS, ROWS), 1)


def hits(at_ref, targets_ref, place):
    own = jnp.sum(jnp.where(place, targets_ref[...], 0), axis=1, keepdims=True) - at_ref[4]
    return lax.broadcasted_iota(jnp.int32, (ROWS, WIDTH), 1) == own


def column_copies(source, target, sems):
    cuts = [pl.ds(k * CHUNK, CHUNK) for k in range(STEPS)]
    return [pltpu.make_async_copy(source.at[:, cut], target.at[:, cut], sems.at[k]) for k, cut in enumerate(cuts)]


def weight_copies(source, target, sems):
    cuts = [pl.ds(k * CHUNK, CHUNK) for k in range(STEPS)]
    copies = [pltpu.make_async_copy(source.at[cut], target.at[cut], sems.at[k]) for k, cut in enumerate(cuts)]
    for copy in copies:
        copy.start()
    return copies


def logits_kernel(at_ref, targets_ref, p0, p1, p2, p3, p4, p5, p6, p7, w_ref, stats_ref, own_hbm, other_hbm, own_ref, other_ref, own_sems, other_sems):
    acc = jnp.zeros((ROWS, WIDTH), F32)
    for k in range(STEPS):
        cut = slice(k * CHUNK, (k + 1) * CHUNK)
        left = jnp.concatenate([p[:, cut] for p in (p0, p1, p2, p3, p4, p5, p6, p7)], axis=0)
        acc += jnp.dot(left, w_ref[cut, :], preferred_element_type=F32)
    top = jnp.max(acc, axis=1, keepdims=True)
    soft = jnp.exp(acc - top)
    total = jnp.sum(soft, axis=1, keepdims=True)
    place = placed(at_ref)
    hit = hits(at_ref, targets_ref, place)
    picked = jnp.sum(jnp.where(hit, acc, 0.0), axis=1, keepdims=True)
    for i, column in enumerate((top, total, picked)):
        stats_ref[i : i + 1, :] = jnp.sum(jnp.where(place, column, 0.0), axis=0, keepdims=True)
    own = (own_ref, column_copies(own_ref, own_hbm, own_sems))
    other = (other_ref, column_copies(other_ref, other_hbm, other_sems))
    products(jnp.where(hit, 0.0, soft).astype(BF), None, w_ref, (own, other))


def products(left, copies, w_ref, pairs):
    for k in range(STEPS):
        cut = slice(k * CHUNK, (k + 1) * CHUNK)
        if copies is not None:
            copies[k].wait()
        part = lax.dot_general(left, w_ref[cut, :], (((1,), (1,)), ((), ())), preferred_element_type=F32)
        first = 0
        for buffer, outs in pairs:
            buffer[:, cut] = part[first : first + buffer.shape[0]].astype(buffer.dtype)
            outs[k].start()
            first += buffer.shape[0]
    for _, outs in pairs:
        for copy in outs:
            copy.wait()


def target_kernel(at_ref, targets_ref, w_hbm, own_hbm, other_hbm, w_ref, own_ref, other_ref, w_sems, own_sems, other_sems):
    copies = weight_copies(w_hbm, w_ref, w_sems)
    left = jnp.where(hits(at_ref, targets_ref, placed(at_ref)), 1.0, 0.0).astype(BF)
    own = (own_ref, column_copies(own_ref, own_hbm, own_sems))
    other = (other_ref, column_copies(other_ref, other_hbm, other_sems))
    products(left, copies, w_ref, (own, other))


def merge_kernel(own_ref, core_ref, x_ref, both_ref, out_ref):
    refs = (own_ref, core_ref, x_ref, both_ref)
    tops = [r[0:1, :] for r in refs]
    top = jnp.maximum(jnp.maximum(tops[0], tops[1]), jnp.maximum(tops[2], tops[3]))
    total = sum(r[1:2, :] * jnp.exp(t - top) for r, t in zip(refs, tops))
    picked = sum(r[2:3, :] for r in refs)
    merged = jnp.concatenate([top, total, picked], axis=0)
    for i in range(out_ref.shape[0]):
        out_ref[i] = merged


def row_scales(at_ref, grad_ref, own_ref, core_ref, spread_ref):
    place = placed(at_ref)[: ROWS // 2]

    def ordered(row):
        return jnp.sum(jnp.where(place, row, 0.0), axis=1, keepdims=True)

    tops = spread_ref[:, 0, :]
    highest = jnp.max(tops, axis=0, keepdims=True)
    total = jnp.sum(spread_ref[:, 1, :] * jnp.exp(tops - highest), axis=0, keepdims=True)
    log_total = ordered(highest + jnp.log(total))
    picked = ordered(jnp.sum(spread_ref[:, 2, :], axis=0, keepdims=True))
    factor = 1.0 + 2.0 * zloss_coef * log_total
    grad = ordered(grad_ref[...])
    target = (grad * (jnp.exp(picked - log_total) * factor - 1.0)).astype(BF).astype(F32)
    own, core = (grad * factor * jnp.exp(ordered(ref[0:1, :]) - log_total) for ref in (own_ref, core_ref))
    lane = lax.broadcasted_iota(jnp.int32, (ROWS // 2, 128), 1)
    rest = jnp.where(lane == 2, target, jnp.where(lane == 3, log_total, picked))
    return jnp.where(lane == 0, own, jnp.where(lane == 1, core, rest))


def combine_start(parts, sources, buffers, sems):
    every = []
    for i, q in enumerate(parts):
        copies = [
            pltpu.make_async_copy(s.at[pl.ds(32 * q, 32)], t.at[i], sems.at[i, j])
            for j, (s, t) in enumerate(zip(sources, buffers))
        ]
        for copy in copies:
            copy.start()
        every.append(copies)
    return every


def combine_end(parts, every, scales_ref, buffers, outs):
    a_ref, b_ref, c_ref, d_ref = buffers
    for i, (q, out) in enumerate(zip(parts, outs)):
        for copy in every[i]:
            copy.wait()
        own, core, target = (scales_ref[32 * q : 32 * q + 32, j : j + 1] for j in range(3))
        for k in range(0, DEPTH, CHUNK):
            cut = slice(k, k + CHUNK)
            soft = own * a_ref[i, :, cut] + core * b_ref[i, :, cut].astype(F32)
            chosen = c_ref[i, :, cut].astype(F32) + d_ref[i, :, cut].astype(F32)
            out[:, cut] = (soft + target * chosen).astype(out.dtype)


def first_kernel(parts, at_ref, grad_ref, own_ref, core_ref, spread_ref, *refs):
    sources, scales_ref, outs, buffers, sems = refs[:4], refs[4], refs[5:-5], refs[-5:-1], refs[-1]
    every = combine_start(parts, sources, buffers, sems)
    scales_ref[...] = row_scales(at_ref, grad_ref, own_ref, core_ref, spread_ref)
    combine_end(parts, every, scales_ref, buffers, outs)


def combine_kernel(parts, scales_ref, *refs):
    sources, outs, buffers, sems = refs[:4], refs[4:-5], refs[-5:-1], refs[-1]
    combine_end(parts, combine_start(parts, sources, buffers, sems), scales_ref, buffers, outs)


def shards(hidden, lm_weight, targets, loss_grad):
    half = ROWS // 2
    at = jnp.stack([lax.axis_index(a) for a in GROUP] + [lax.axis_index(GROUP) * WIDTH])
    targets, loss_grad = targets.reshape(1, ROWS), loss_grad.reshape(1, ROWS)
    lm_weight_in, lm_weight = lm_weight, pltpu.with_memory_space_constraint(lm_weight, pltpu.HBM)
    weights = [pltpu.VMEM((DEPTH, WIDTH), BF)]
    sems = pltpu.SemaphoreType.DMA((STEPS,))

    block = jnp.concatenate([hidden, send(hidden, to_x)])
    block = jnp.concatenate([block, send(block, to_z4)])
    block = jnp.concatenate([block] + [send(block, to_first(-o)) for o in OFFSETS[1:]])
    near, back, far = (send(block, to_second(-o)) for o in OFFSETS[1:])

    aim, _ = lax.optimization_barrier((targets, block))
    target_own, target_out = pl.pallas_call(
        target_kernel,
        out_shape=[pltpu.HBM((half, DEPTH), BF)] * 2,
        in_specs=[SMEM, VMEM, ANY],
        out_specs=[HBM] * 2,
        scratch_shapes=weights + [pltpu.VMEM((half, DEPTH), BF)] * 2 + [sems] * 3,
        compiler_params=params(),
        cost_estimate=pl.CostEstimate(flops=2 * ROWS * DEPTH * WIDTH, bytes_accessed=12 << 20, transcendentals=0),
        name="target",
    )(at, aim, lm_weight)
    near, target_out = lax.optimization_barrier((near, target_out))
    pieces = [block, near, back, far]
    pieces = pieces + [send(p, to_c) for p in pieces]

    stats, soft_own, soft_out = pl.pallas_call(
        logits_kernel,
        out_shape=(jax.ShapeDtypeStruct((3, ROWS), F32), pltpu.HBM((half, DEPTH), F32), pltpu.HBM((half, DEPTH), BF)),
        in_specs=[SMEM] + [VMEM] * 10,
        out_specs=(VMEM, HBM, HBM),
        scratch_shapes=[pltpu.VMEM((half, DEPTH), F32), pltpu.VMEM((half, DEPTH), BF)] + [sems] * 2,
        compiler_params=params(16),
        cost_estimate=pl.CostEstimate(flops=4 * ROWS * DEPTH * WIDTH, bytes_accessed=19 << 20, transcendentals=ROWS * WIDTH),
        name="logits",
    )(at, targets, *pieces, pltpu.with_memory_space_constraint(lm_weight_in, pltpu.VMEM))
    stats = [stats] + [send(stats, to) for to in (to_c, to_x, to_xc)]
    merged = pl.pallas_call(
        merge_kernel,
        out_shape=jax.ShapeDtypeStruct((32, 3, ROWS), F32),
        in_specs=[VMEM] * 4,
        out_specs=VMEM,
        compiler_params=params(),
        name="merge",
    )(*stats)
    merged, soft_out, target_out = lax.optimization_barrier((merged, soft_out, target_out))
    soft_in, target_in = send(soft_out, to_c), send(target_out, to_c)
    spread = lax.all_to_all(merged, ("y", "z"), 0, 0)

    soft_own, target_own = (pltpu.with_memory_space_constraint(v, pltpu.HBM) for v in (soft_own, target_own))
    shares = (soft_own, soft_in, target_own, target_in)

    def combine(parts, dtype, kernel=combine_kernel, rows=()):
        n = len(parts)
        first = len(rows) > 1
        scales = [jax.ShapeDtypeStruct((half, 128), F32)] if first else []
        return pl.pallas_call(
            functools.partial(kernel, parts),
            out_shape=scales + [jax.ShapeDtypeStruct((32, DEPTH), dtype)] * n,
            in_specs=([SMEM] if first else []) + [VMEM] * (len(rows) - first) + [ANY] * 4,
            out_specs=[VMEM] * (n + first),
            scratch_shapes=[pltpu.VMEM((n, 32, DEPTH), F32)]
            + [pltpu.VMEM((n, 32, DEPTH), BF)] * 3
            + [pltpu.SemaphoreType.DMA((n, 4))],
            compiler_params=params(),
            cost_estimate=pl.CostEstimate(flops=6 * 32 * DEPTH * n, bytes_accessed=n * (3 << 20), transcendentals=0),
            name="combine",
        )(*rows, *shares)

    scales, far = combine((3,), BF, first_kernel, (at, loss_grad, stats[0], stats[1], spread))
    parts = [far, *combine((1, 2), BF, rows=(scales,))]
    log_total, target_logit = scales[:2, 3], scales[:2, 4]
    ce_loss = log_total - target_logit
    z_term = zloss_coef * log_total * log_total
    arrived = [send(p, to_second(o)).astype(F32) for p, o in zip(parts, (2, 1, -1))]
    part = combine((0,), F32, rows=(scales,))[0] + sum(arrived)
    part = part.reshape(4, 8, DEPTH)
    part = part[0] + sum(send(part[k].astype(BF), to_first(OFFSETS[k])).astype(F32) for k in (3, 1, 2))
    part = [part[0:2], send(part[2:4], to_x)] + [
        send(part[2 * k : 2 * k + 2].astype(BF), to).astype(F32) for k, to in ((2, to_z4), (3, to_xz4))
    ]
    part = (part[0] + part[1]) + (part[2] + part[3])
    return ce_loss, z_term, part.astype(BF)


def solution(mesh):
    mesh = Mesh(mesh.devices.reshape(NY, NX, NC, NZ, 2), (*GROUP, "dp"))
    own = ("dp", *GROUP)
    in_specs = (P(own, None), P(None, GROUP), P("dp"), P("dp"))
    out_specs = (P(own), P(own), P(own, None))
    return jax.shard_map(shards, mesh=mesh, in_specs=in_specs, out_specs=out_specs, check_vma=False)
```

```python
import functools

import jax
import jax.numpy as jnp
from jax import lax
from jax.experimental import pallas as pl
from jax.experimental.pallas import tpu as pltpu
from jax.sharding import Mesh
from jax.sharding import PartitionSpec as P

zloss_coef = 0.0001
NY, NX, NC, NZ = 4, 2, 2, 8
GROUP = ("y", "x", "c", "z")
OFFSETS = (0, 1, -1, 2)
BF, F32 = jnp.bfloat16, jnp.float32
ROWS, DEPTH, WIDTH = 256, 8192, 512
CHUNK = 1024
STEPS = DEPTH // CHUNK
VMEM = pl.BlockSpec(memory_space=pltpu.VMEM)
SMEM = pl.BlockSpec(memory_space=pltpu.SMEM)
ANY = pl.BlockSpec(memory_space=pl.ANY)
HBM = pl.BlockSpec(memory_space=pltpu.HBM)


def index_of(y, x, c, z):
    return (((y % NY) * NX + x % NX) * NC + c % NC) * NZ + z % NZ


def pairs(route):
    every = [(y, x, c, z) for y in range(NY) for x in range(NX) for c in range(NC) for z in range(NZ)]
    return [(index_of(*p), index_of(*route(*p))) for p in every]


def to_x(y, x, c, z):
    return y, x + 1, c, z


def to_c(y, x, c, z):
    return y, x, c + 1, z


def to_z4(y, x, c, z):
    return y, x, c, z + 4


def to_xc(y, x, c, z):
    return y, x + 1, c + 1, z


def to_xz4(y, x, c, z):
    return y, x + 1, c, z + 4


def to_first(step):
    return lambda y, x, c, z: (y, x, c, z + step) if c == 0 else (y + step, x, c, z)


def to_second(step):
    return lambda y, x, c, z: (y + step, x, c, z) if c == 0 else (y, x, c, z + step)


def send(value, route):
    return lax.ppermute(value, GROUP, pairs(route))


def params(mib=24):
    return pltpu.CompilerParams(vmem_limit_bytes=mib << 20)


def placed(at_ref):
    y, x, c, z = (at_ref[i] for i in range(4))
    at = lax.broadcasted_iota(jnp.int32, (ROWS, 1), 0)
    r, near, q1, q2, cr = at & 1, (at >> 1) & 3, (at >> 3) & 3, (at >> 5) & 3, at >> 7
    xr, z4 = near & 1, near >> 1
    o1 = jnp.where(q1 == 2, -1, jnp.where(q1 == 3, 2, q1))
    o2 = jnp.where(q2 == 2, -1, jnp.where(q2 == 3, 2, q2))
    core = c ^ cr
    zo = jnp.where(core == 0, o1, o2) + 4 * z4
    yo = jnp.where(core == 0, o2, o1)
    rows = ((((y + yo) & 3) * 2 + (x ^ xr)) * 2 + core) * 16 + ((z + zo) & 7) * 2 + r
    return rows == lax.broadcasted_iota(jnp.int32, (ROWS, ROWS), 1)


def hits(at_ref, targets_ref, place):
    own = jnp.sum(jnp.where(place, targets_ref[...], 0), axis=1, keepdims=True) - at_ref[4]
    return lax.broadcasted_iota(jnp.int32, (ROWS, WIDTH), 1) == own


def column_copies(source, target, sems):
    cuts = [pl.ds(k * CHUNK, CHUNK) for k in range(STEPS)]
    return [pltpu.make_async_copy(source.at[:, cut], target.at[:, cut], sems.at[k]) for k, cut in enumerate(cuts)]


def weight_copies(source, target, sems):
    cuts = [pl.ds(k * CHUNK, CHUNK) for k in range(STEPS)]
    copies = [pltpu.make_async_copy(source.at[cut], target.at[cut], sems.at[k]) for k, cut in enumerate(cuts)]
    for copy in copies:
        copy.start()
    return copies


def logits_kernel(at_ref, targets_ref, p0, p1, p2, p3, p4, p5, p6, p7, w_ref, stats_ref, own_hbm, other_hbm, own_ref, other_ref, own_sems, other_sems):
    acc = jnp.zeros((ROWS, WIDTH), F32)
    for k in range(STEPS):
        cut = slice(k * CHUNK, (k + 1) * CHUNK)
        left = jnp.concatenate([p[:, cut] for p in (p0, p1, p2, p3, p4, p5, p6, p7)], axis=0)
        acc += jnp.dot(left, w_ref[cut, :], preferred_element_type=F32)
    top = jnp.max(acc, axis=1, keepdims=True)
    soft = jnp.exp(acc - top)
    total = jnp.sum(soft, axis=1, keepdims=True)
    place = placed(at_ref)
    hit = hits(at_ref, targets_ref, place)
    picked = jnp.sum(jnp.where(hit, acc, 0.0), axis=1, keepdims=True)
    for i, column in enumerate((top, total, picked)):
        stats_ref[i : i + 1, :] = jnp.sum(jnp.where(place, column, 0.0), axis=0, keepdims=True)
    own = (own_ref, column_copies(own_ref, own_hbm, own_sems))
    other = (other_ref, column_copies(other_ref, other_hbm, other_sems))
    products(jnp.where(hit, 0.0, soft).astype(BF), None, w_ref, (own, other))


def products(left, copies, w_ref, pairs):
    for k in range(STEPS):
        cut = slice(k * CHUNK, (k + 1) * CHUNK)
        if copies is not None:
            copies[k].wait()
        part = lax.dot_general(left, w_ref[cut, :], (((1,), (1,)), ((), ())), preferred_element_type=F32)
        first = 0
        for buffer, outs in pairs:
            buffer[:, cut] = part[first : first + buffer.shape[0]].astype(buffer.dtype)
            outs[k].start()
            first += buffer.shape[0]
    for _, outs in pairs:
        for copy in outs:
            copy.wait()


def target_kernel(at_ref, targets_ref, w_hbm, own_hbm, other_hbm, w_ref, own_ref, other_ref, w_sems, own_sems, other_sems):
    copies = weight_copies(w_hbm, w_ref, w_sems)
    left = jnp.where(hits(at_ref, targets_ref, placed(at_ref)), 1.0, 0.0).astype(BF)
    own = (own_ref, column_copies(own_ref, own_hbm, own_sems))
    other = (other_ref, column_copies(other_ref, other_hbm, other_sems))
    products(left, copies, w_ref, (own, other))


def merge_kernel(own_ref, core_ref, x_ref, both_ref, out_ref):
    refs = (own_ref, core_ref, x_ref, both_ref)
    tops = [r[0:1, :] for r in refs]
    top = jnp.maximum(jnp.maximum(tops[0], tops[1]), jnp.maximum(tops[2], tops[3]))
    total = sum(r[1:2, :] * jnp.exp(t - top) for r, t in zip(refs, tops))
    picked = sum(r[2:3, :] for r in refs)
    merged = jnp.concatenate([top, total, picked], axis=0)
    for i in range(out_ref.shape[0]):
        out_ref[i] = merged


def row_scales(at_ref, grad_ref, own_ref, core_ref, spread_ref):
    place = placed(at_ref)[: ROWS // 2]

    def ordered(row):
        return jnp.sum(jnp.where(place, row, 0.0), axis=1, keepdims=True)

    tops = spread_ref[:, 0, :]
    highest = jnp.max(tops, axis=0, keepdims=True)
    total = jnp.sum(spread_ref[:, 1, :] * jnp.exp(tops - highest), axis=0, keepdims=True)
    log_total = ordered(highest + jnp.log(total))
    picked = ordered(jnp.sum(spread_ref[:, 2, :], axis=0, keepdims=True))
    factor = 1.0 + 2.0 * zloss_coef * log_total
    grad = ordered(grad_ref[...])
    target = (grad * (jnp.exp(picked - log_total) * factor - 1.0)).astype(BF).astype(F32)
    own, core = (grad * factor * jnp.exp(ordered(ref[0:1, :]) - log_total) for ref in (own_ref, core_ref))
    lane = lax.broadcasted_iota(jnp.int32, (ROWS // 2, 128), 1)
    rest = jnp.where(lane == 2, target, jnp.where(lane == 3, log_total, picked))
    return jnp.where(lane == 0, own, jnp.where(lane == 1, core, rest))


def combine_start(parts, sources, buffers, sems):
    every = []
    for i, q in enumerate(parts):
        copies = [
            pltpu.make_async_copy(s.at[pl.ds(32 * q, 32)], t.at[i], sems.at[i, j])
            for j, (s, t) in enumerate(zip(sources, buffers))
        ]
        for copy in copies:
            copy.start()
        every.append(copies)
    return every


def combine_end(parts, every, scales_ref, buffers, outs):
    a_ref, b_ref, c_ref, d_ref = buffers
    for i, (q, out) in enumerate(zip(parts, outs)):
        for copy in every[i]:
            copy.wait()
        own, core, target = (scales_ref[32 * q : 32 * q + 32, j : j + 1] for j in range(3))
        for k in range(0, DEPTH, CHUNK):
            cut = slice(k, k + CHUNK)
            soft = own * a_ref[i, :, cut] + core * b_ref[i, :, cut].astype(F32)
            chosen = c_ref[i, :, cut].astype(F32) + d_ref[i, :, cut].astype(F32)
            out[:, cut] = (soft + target * chosen).astype(out.dtype)


def first_kernel(parts, at_ref, grad_ref, own_ref, core_ref, spread_ref, *refs):
    sources, scales_ref, outs, buffers, sems = refs[:4], refs[4], refs[5:-5], refs[-5:-1], refs[-1]
    every = combine_start(parts, sources, buffers, sems)
    scales_ref[...] = row_scales(at_ref, grad_ref, own_ref, core_ref, spread_ref)
    combine_end(parts, every, scales_ref, buffers, outs)


def combine_kernel(parts, scales_ref, *refs):
    sources, outs, buffers, sems = refs[:4], refs[4:-5], refs[-5:-1], refs[-1]
    combine_end(parts, combine_start(parts, sources, buffers, sems), scales_ref, buffers, outs)


def shards(hidden, lm_weight, targets, loss_grad):
    half = ROWS // 2
    at = jnp.stack([lax.axis_index(a) for a in GROUP] + [lax.axis_index(GROUP) * WIDTH])
    targets, loss_grad = targets.reshape(1, ROWS), loss_grad.reshape(1, ROWS)
    lm_weight_in, lm_weight = lm_weight, pltpu.with_memory_space_constraint(lm_weight, pltpu.HBM)
    weights = [pltpu.VMEM((DEPTH, WIDTH), BF)]
    sems = pltpu.SemaphoreType.DMA((STEPS,))

    block = jnp.concatenate([hidden] + [send(hidden, to) for to in (to_x, to_z4, to_xz4)])
    block = jnp.concatenate([block] + [send(block, to_first(-o)) for o in OFFSETS[1:]])
    near, back, far = (send(block, to_second(-o)) for o in OFFSETS[1:])

    aim, _ = lax.optimization_barrier((targets, block))
    target_own, target_out = pl.pallas_call(
        target_kernel,
        out_shape=[pltpu.HBM((half, DEPTH), BF)] * 2,
        in_specs=[SMEM, VMEM, ANY],
        out_specs=[HBM] * 2,
        scratch_shapes=weights + [pltpu.VMEM((half, DEPTH), BF)] * 2 + [sems] * 3,
        compiler_params=params(),
        cost_estimate=pl.CostEstimate(flops=2 * ROWS * DEPTH * WIDTH, bytes_accessed=12 << 20, transcendentals=0),
        name="target",
    )(at, aim, lm_weight)
    own, target_out = lax.optimization_barrier((block, target_out))
    pieces = [block, near, back, far] + [send(p, to_c) for p in (own, near, back, far)]

    stats, soft_own, soft_out = pl.pallas_call(
        logits_kernel,
        out_shape=(jax.ShapeDtypeStruct((3, ROWS), F32), pltpu.HBM((half, DEPTH), F32), pltpu.HBM((half, DEPTH), BF)),
        in_specs=[SMEM] + [VMEM] * 10,
        out_specs=(VMEM, HBM, HBM),
        scratch_shapes=[pltpu.VMEM((half, DEPTH), F32), pltpu.VMEM((half, DEPTH), BF)] + [sems] * 2,
        compiler_params=params(16),
        cost_estimate=pl.CostEstimate(flops=4 * ROWS * DEPTH * WIDTH, bytes_accessed=19 << 20, transcendentals=ROWS * WIDTH),
        name="logits",
    )(at, targets, *pieces, pltpu.with_memory_space_constraint(lm_weight_in, pltpu.VMEM))
    stats = [stats] + [send(stats, to) for to in (to_c, to_x, to_xc)]
    merged = pl.pallas_call(
        merge_kernel,
        out_shape=jax.ShapeDtypeStruct((32, 3, ROWS), F32),
        in_specs=[VMEM] * 4,
        out_specs=VMEM,
        compiler_params=params(),
        name="merge",
    )(*stats)
    merged, soft_out, target_out = lax.optimization_barrier((merged, soft_out, target_out))
    soft_in, target_in = send(soft_out, to_c), send(target_out, to_c)
    spread = lax.all_to_all(merged, ("y", "z"), 0, 0)

    soft_own, target_own = (pltpu.with_memory_space_constraint(v, pltpu.HBM) for v in (soft_own, target_own))
    shares = (soft_own, soft_in, target_own, target_in)

    def combine(parts, dtype, kernel=combine_kernel, rows=()):
        n = len(parts)
        first = len(rows) > 1
        scales = [jax.ShapeDtypeStruct((half, 128), F32)] if first else []
        return pl.pallas_call(
            functools.partial(kernel, parts),
            out_shape=scales + [jax.ShapeDtypeStruct((32, DEPTH), dtype)] * n,
            in_specs=([SMEM] if first else []) + [VMEM] * (len(rows) - first) + [ANY] * 4,
            out_specs=[VMEM] * (n + first),
            scratch_shapes=[pltpu.VMEM((n, 32, DEPTH), F32)]
            + [pltpu.VMEM((n, 32, DEPTH), BF)] * 3
            + [pltpu.SemaphoreType.DMA((n, 4))],
            compiler_params=params(),
            cost_estimate=pl.CostEstimate(flops=6 * 32 * DEPTH * n, bytes_accessed=n * (3 << 20), transcendentals=0),
            name="combine",
        )(*rows, *shares)

    scales, far = combine((3,), BF, first_kernel, (at, loss_grad, stats[0], stats[1], spread))
    parts = [far, *combine((1, 2), BF, rows=(scales,))]
    log_total, target_logit = scales[:2, 3], scales[:2, 4]
    ce_loss = log_total - target_logit
    z_term = zloss_coef * log_total * log_total
    arrived = [send(p, to_second(o)).astype(F32) for p, o in zip(parts, (2, 1, -1))]
    part = combine((0,), F32, rows=(scales,))[0] + sum(arrived)
    part = part.reshape(4, 8, DEPTH)
    part = part[0] + sum(send(part[k].astype(BF), to_first(OFFSETS[k])).astype(F32) for k in (3, 1, 2))
    part = [part[0:2], send(part[2:4], to_x)] + [
        send(part[2 * k : 2 * k + 2].astype(BF), to).astype(F32) for k, to in ((2, to_z4), (3, to_xz4))
    ]
    part = (part[0] + part[1]) + (part[2] + part[3])
    return ce_loss, z_term, part.astype(BF)


def solution(mesh):
    mesh = Mesh(mesh.devices.reshape(NY, NX, NC, NZ, 2), (*GROUP, "dp"))
    own = ("dp", *GROUP)
    in_specs = (P(own, None), P(None, GROUP), P("dp"), P("dp"))
    out_specs = (P(own), P(own), P(own, None))
    return jax.shard_map(shards, mesh=mesh, in_specs=in_specs, out_specs=out_specs, check_vma=False)
```

```python
import functools

import jax
import jax.numpy as jnp
from jax import lax
from jax.experimental import pallas as pl
from jax.experimental.pallas import tpu as pltpu
from jax.sharding import Mesh
from jax.sharding import PartitionSpec as P

zloss_coef = 0.0001
NY, NX, NC, NZ = 4, 2, 2, 8
GROUP = ("y", "x", "c", "z")
OFFSETS = (0, 1, -1, 2)
BF, F32 = jnp.bfloat16, jnp.float32
ROWS, DEPTH, WIDTH = 256, 8192, 512
CHUNK = 1024
STEPS = DEPTH // CHUNK
VMEM = pl.BlockSpec(memory_space=pltpu.VMEM)
SMEM = pl.BlockSpec(memory_space=pltpu.SMEM)
ANY = pl.BlockSpec(memory_space=pl.ANY)
HBM = pl.BlockSpec(memory_space=pltpu.HBM)


def index_of(y, x, c, z):
    return (((y % NY) * NX + x % NX) * NC + c % NC) * NZ + z % NZ


def pairs(route):
    every = [(y, x, c, z) for y in range(NY) for x in range(NX) for c in range(NC) for z in range(NZ)]
    return [(index_of(*p), index_of(*route(*p))) for p in every]


def to_x(y, x, c, z):
    return y, x + 1, c, z


def to_c(y, x, c, z):
    return y, x, c + 1, z


def to_z4(y, x, c, z):
    return y, x, c, z + 4


def to_xc(y, x, c, z):
    return y, x + 1, c + 1, z


def to_xz4(y, x, c, z):
    return y, x + 1, c, z + 4


def to_first(step):
    return lambda y, x, c, z: (y, x, c, z + step) if c == 0 else (y + step, x, c, z)


def to_second(step):
    return lambda y, x, c, z: (y + step, x, c, z) if c == 0 else (y, x, c, z + step)


def send(value, route):
    return lax.ppermute(value, GROUP, pairs(route))


def params(mib=24):
    return pltpu.CompilerParams(vmem_limit_bytes=mib << 20)


def row_numbers(at_ref):
    y, x, c, z = (at_ref[i] for i in range(4))
    at = lax.broadcasted_iota(jnp.int32, (ROWS, 1), 0)
    r, near, q1, q2, cr = at & 1, (at >> 1) & 3, (at >> 3) & 3, (at >> 5) & 3, at >> 7
    xr, z4 = near & 1, near >> 1
    o1 = jnp.where(q1 == 2, -1, jnp.where(q1 == 3, 2, q1))
    o2 = jnp.where(q2 == 2, -1, jnp.where(q2 == 3, 2, q2))
    core = c ^ cr
    zo = jnp.where(core == 0, o1, o2) + 4 * z4
    yo = jnp.where(core == 0, o2, o1)
    return ((((y + yo) & 3) * 2 + (x ^ xr)) * 2 + core) * 16 + ((z + zo) & 7) * 2 + r


def placed(rows):
    return rows == lax.broadcasted_iota(jnp.int32, (rows.shape[0], ROWS), 1)


def placed_in_half(rows):
    return (rows >> 5) * 16 + (rows & 15) == lax.broadcasted_iota(jnp.int32, (rows.shape[0], ROWS // 2), 1)


def hits(at_ref, targets_ref, place):
    own = jnp.sum(jnp.where(place, targets_ref[...], 0), axis=1, keepdims=True) - at_ref[4]
    return lax.broadcasted_iota(jnp.int32, (ROWS, WIDTH), 1) == own


def column_copies(source, target, sems):
    cuts = [pl.ds(k * CHUNK, CHUNK) for k in range(STEPS)]
    return [pltpu.make_async_copy(source.at[:, cut], target.at[:, cut], sems.at[k]) for k, cut in enumerate(cuts)]


def weight_copies(source, target, sems):
    cuts = [pl.ds(k * CHUNK, CHUNK) for k in range(STEPS)]
    copies = [pltpu.make_async_copy(source.at[cut], target.at[cut], sems.at[k]) for k, cut in enumerate(cuts)]
    for copy in copies:
        copy.start()
    return copies


def logits_kernel(at_ref, targets_ref, p0, p1, p2, p3, p4, p5, p6, p7, w_ref, stats_ref, other_stats_ref, own_hbm, other_hbm, own_ref, other_ref, own_sems, other_sems):
    acc = jnp.zeros((ROWS, WIDTH), F32)
    for k in range(STEPS):
        cut = slice(k * CHUNK, (k + 1) * CHUNK)
        left = jnp.concatenate([p[:, cut] for p in (p0, p1, p2, p3, p4, p5, p6, p7)], axis=0)
        acc += jnp.dot(left, w_ref[cut, :], preferred_element_type=F32)
    top = jnp.max(acc, axis=1, keepdims=True)
    soft = jnp.exp(acc - top)
    total = jnp.sum(soft, axis=1, keepdims=True)
    rows = row_numbers(at_ref)
    hit = hits(at_ref, targets_ref, placed(rows))
    picked = jnp.sum(jnp.where(hit, acc, 0.0), axis=1, keepdims=True)
    half = ROWS // 2
    place = placed_in_half(rows)
    for i, column in enumerate((top, total, picked)):
        stats_ref[i : i + 1, :] = jnp.sum(jnp.where(place[:half], column[:half], 0.0), axis=0, keepdims=True)
        other_stats_ref[i : i + 1, :] = jnp.sum(jnp.where(place[half:], column[half:], 0.0), axis=0, keepdims=True)
    own = (own_ref, column_copies(own_ref, own_hbm, own_sems))
    other = (other_ref, column_copies(other_ref, other_hbm, other_sems))
    products(jnp.where(hit, 0.0, soft).astype(BF), None, w_ref, (own, other))


def products(left, copies, w_ref, pairs):
    for k in range(STEPS):
        cut = slice(k * CHUNK, (k + 1) * CHUNK)
        if copies is not None:
            copies[k].wait()
        part = lax.dot_general(left, w_ref[cut, :], (((1,), (1,)), ((), ())), preferred_element_type=F32)
        first = 0
        for buffer, outs in pairs:
            buffer[:, cut] = part[first : first + buffer.shape[0]].astype(buffer.dtype)
            outs[k].start()
            first += buffer.shape[0]
    for _, outs in pairs:
        for copy in outs:
            copy.wait()


def target_kernel(at_ref, targets_ref, w_hbm, own_hbm, other_hbm, w_ref, own_ref, other_ref, w_sems, own_sems, other_sems):
    copies = weight_copies(w_hbm, w_ref, w_sems)
    left = jnp.where(hits(at_ref, targets_ref, placed(row_numbers(at_ref))), 1.0, 0.0).astype(BF)
    own = (own_ref, column_copies(own_ref, own_hbm, own_sems))
    other = (other_ref, column_copies(other_ref, other_hbm, other_sems))
    products(left, copies, w_ref, (own, other))


def merge_kernel(own_ref, core_ref, x_ref, both_ref, out_ref):
    refs = (own_ref, core_ref, x_ref, both_ref)
    tops = [r[0:1, :] for r in refs]
    top = jnp.maximum(jnp.maximum(tops[0], tops[1]), jnp.maximum(tops[2], tops[3]))
    total = sum(r[1:2, :] * jnp.exp(t - top) for r, t in zip(refs, tops))
    picked = sum(r[2:3, :] for r in refs)
    merged = jnp.concatenate([top, total, picked], axis=0)
    for i in range(out_ref.shape[0]):
        out_ref[i] = merged


def row_scales(at_ref, grad_ref, own_ref, core_ref, spread_ref):
    rows = row_numbers(at_ref)[: ROWS // 2]
    place = placed_in_half(rows)

    def ordered(row):
        return jnp.sum(jnp.where(place, row, 0.0), axis=1, keepdims=True)

    tops = spread_ref[:, 0, :]
    highest = jnp.max(tops, axis=0, keepdims=True)
    total = jnp.sum(spread_ref[:, 1, :] * jnp.exp(tops - highest), axis=0, keepdims=True)
    log_total = ordered(highest + jnp.log(total))
    picked = ordered(jnp.sum(spread_ref[:, 2, :], axis=0, keepdims=True))
    factor = 1.0 + 2.0 * zloss_coef * log_total
    grad = jnp.sum(jnp.where(placed(rows), grad_ref[...], 0.0), axis=1, keepdims=True)
    target = (grad * (jnp.exp(picked - log_total) * factor - 1.0)).astype(BF).astype(F32)
    own, core = (grad * factor * jnp.exp(ordered(ref[0:1, :]) - log_total) for ref in (own_ref, core_ref))
    lane = lax.broadcasted_iota(jnp.int32, (ROWS // 2, 128), 1)
    rest = jnp.where(lane == 2, target, jnp.where(lane == 3, log_total, picked))
    return jnp.where(lane == 0, own, jnp.where(lane == 1, core, rest))


def combine_start(parts, sources, buffers, sems):
    every = []
    for i, q in enumerate(parts):
        copies = [
            pltpu.make_async_copy(s.at[pl.ds(32 * q, 32)], t.at[i], sems.at[i, j])
            for j, (s, t) in enumerate(zip(sources, buffers))
        ]
        for copy in copies:
            copy.start()
        every.append(copies)
    return every


def combine_end(parts, every, scales_ref, buffers, outs):
    a_ref, b_ref, c_ref, d_ref = buffers
    for i, (q, out) in enumerate(zip(parts, outs)):
        for copy in every[i]:
            copy.wait()
        own, core, target = (scales_ref[32 * q : 32 * q + 32, j : j + 1] for j in range(3))
        for k in range(0, DEPTH, CHUNK):
            cut = slice(k, k + CHUNK)
            soft = own * a_ref[i, :, cut] + core * b_ref[i, :, cut].astype(F32)
            chosen = c_ref[i, :, cut].astype(F32) + d_ref[i, :, cut].astype(F32)
            out[:, cut] = (soft + target * chosen).astype(out.dtype)


def first_kernel(parts, at_ref, grad_ref, own_ref, core_ref, spread_ref, *refs):
    sources, scales_ref, outs, buffers, sems = refs[:4], refs[4], refs[5:-5], refs[-5:-1], refs[-1]
    every = combine_start(parts, sources, buffers, sems)
    scales_ref[...] = row_scales(at_ref, grad_ref, own_ref, core_ref, spread_ref)
    combine_end(parts, every, scales_ref, buffers, outs)


def combine_kernel(parts, scales_ref, *refs):
    sources, outs, buffers, sems = refs[:4], refs[4:-5], refs[-5:-1], refs[-1]
    combine_end(parts, combine_start(parts, sources, buffers, sems), scales_ref, buffers, outs)


def join_kernel(a_ref, b_ref, c_ref, d_ref, out_ref):
    out_ref[...] = jnp.concatenate([r[...] for r in (a_ref, b_ref, c_ref, d_ref)], axis=0)


def shards(hidden, lm_weight, targets, loss_grad):
    half = ROWS // 2
    at = jnp.stack([lax.axis_index(a) for a in GROUP] + [lax.axis_index(GROUP) * WIDTH])
    targets, loss_grad = targets.reshape(1, ROWS), loss_grad.reshape(1, ROWS)
    lm_weight_in, lm_weight = lm_weight, pltpu.with_memory_space_constraint(lm_weight, pltpu.HBM)
    weights = [pltpu.VMEM((DEPTH, WIDTH), BF)]
    sems = pltpu.SemaphoreType.DMA((STEPS,))

    block = jnp.concatenate([hidden] + [send(hidden, to) for to in (to_x, to_z4, to_xz4)])
    block = pl.pallas_call(
        join_kernel,
        out_shape=jax.ShapeDtypeStruct((32, DEPTH), BF),
        in_specs=[VMEM] * 4,
        out_specs=VMEM,
        compiler_params=params(),
        name="join",
    )(block, *(send(block, to_first(-o)) for o in OFFSETS[1:]))
    near, back, far = (send(block, to_second(-o)) for o in OFFSETS[1:])

    aim, _ = lax.optimization_barrier((targets, block))
    target_own, target_out = pl.pallas_call(
        target_kernel,
        out_shape=[pltpu.HBM((half, DEPTH), BF)] * 2,
        in_specs=[SMEM, VMEM, ANY],
        out_specs=[HBM] * 2,
        scratch_shapes=weights + [pltpu.VMEM((half, DEPTH), BF)] * 2 + [sems] * 3,
        compiler_params=params(),
        cost_estimate=pl.CostEstimate(flops=2 * ROWS * DEPTH * WIDTH, bytes_accessed=12 << 20, transcendentals=0),
        name="target",
    )(at, aim, lm_weight)
    own, target_out = lax.optimization_barrier((block, target_out))
    pieces = [block, near, back, far] + [send(p, to_c) for p in (own, near, back, far)]

    own_stats, other_stats, soft_own, soft_out = pl.pallas_call(
        logits_kernel,
        out_shape=[jax.ShapeDtypeStruct((3, half), F32)] * 2 + [pltpu.HBM((half, DEPTH), F32), pltpu.HBM((half, DEPTH), BF)],
        in_specs=[SMEM] + [VMEM] * 10,
        out_specs=(VMEM, VMEM, HBM, HBM),
        scratch_shapes=[pltpu.VMEM((half, DEPTH), F32), pltpu.VMEM((half, DEPTH), BF)] + [sems] * 2,
        compiler_params=params(16),
        cost_estimate=pl.CostEstimate(flops=4 * ROWS * DEPTH * WIDTH, bytes_accessed=19 << 20, transcendentals=ROWS * WIDTH),
        name="logits",
    )(at, targets, *pieces, pltpu.with_memory_space_constraint(lm_weight_in, pltpu.VMEM))
    stats = [own_stats, send(other_stats, to_c), send(own_stats, to_x), send(other_stats, to_xc)]
    merged = pl.pallas_call(
        merge_kernel,
        out_shape=jax.ShapeDtypeStruct((32, 3, half), F32),
        in_specs=[VMEM] * 4,
        out_specs=VMEM,
        compiler_params=params(),
        name="merge",
    )(*stats)
    merged, soft_out, target_out = lax.optimization_barrier((merged, soft_out, target_out))
    soft_in, target_in = send(soft_out, to_c), send(target_out, to_c)
    spread = lax.all_to_all(merged, ("y", "z"), 0, 0)

    soft_own, target_own = (pltpu.with_memory_space_constraint(v, pltpu.HBM) for v in (soft_own, target_own))
    shares = (soft_own, soft_in, target_own, target_in)

    def combine(parts, dtype, kernel=combine_kernel, rows=()):
        n = len(parts)
        first = len(rows) > 1
        scales = [jax.ShapeDtypeStruct((half, 128), F32)] if first else []
        return pl.pallas_call(
            functools.partial(kernel, parts),
            out_shape=scales + [jax.ShapeDtypeStruct((32, DEPTH), dtype)] * n,
            in_specs=([SMEM] if first else []) + [VMEM] * (len(rows) - first) + [ANY] * 4,
            out_specs=[VMEM] * (n + first),
            scratch_shapes=[pltpu.VMEM((n, 32, DEPTH), F32)]
            + [pltpu.VMEM((n, 32, DEPTH), BF)] * 3
            + [pltpu.SemaphoreType.DMA((n, 4))],
            compiler_params=params(),
            cost_estimate=pl.CostEstimate(flops=6 * 32 * DEPTH * n, bytes_accessed=n * (3 << 20), transcendentals=0),
            name="combine",
        )(*rows, *shares)

    scales, far = combine((3,), BF, first_kernel, (at, loss_grad, stats[0], stats[1], spread))
    parts = [far, *combine((1, 2), BF, rows=(scales,))]
    log_total, target_logit = scales[:2, 3], scales[:2, 4]
    ce_loss = log_total - target_logit
    z_term = zloss_coef * log_total * log_total
    arrived = [send(p, to_second(o)).astype(F32) for p, o in zip(parts, (2, 1, -1))]
    part = combine((0,), F32, rows=(scales,))[0] + sum(arrived)
    part = part.reshape(4, 8, DEPTH)
    part = part[0] + sum(send(part[k].astype(BF), to_first(OFFSETS[k])).astype(F32) for k in (3, 1, 2))
    part = [part[0:2], send(part[2:4], to_x)] + [
        send(part[2 * k : 2 * k + 2].astype(BF), to).astype(F32) for k, to in ((2, to_z4), (3, to_xz4))
    ]
    part = (part[0] + part[1]) + (part[2] + part[3])
    return ce_loss, z_term, part.astype(BF)


def solution(mesh):
    mesh = Mesh(mesh.devices.reshape(NY, NX, NC, NZ, 2), (*GROUP, "dp"))
    own = ("dp", *GROUP)
    in_specs = (P(own, None), P(None, GROUP), P("dp"), P("dp"))
    out_specs = (P(own), P(own), P(own, None))
    return jax.shard_map(shards, mesh=mesh, in_specs=in_specs, out_specs=out_specs, check_vma=False)
```

```python
import functools

import jax
import jax.numpy as jnp
from jax import lax
from jax.experimental import pallas as pl
from jax.experimental.pallas import tpu as pltpu
from jax.sharding import Mesh
from jax.sharding import PartitionSpec as P

zloss_coef = 0.0001
NY, NX, NC, NZ = 4, 2, 2, 8
GROUP = ("y", "x", "c", "z")
OFFSETS = (0, 1, -1, 2)
BF, F32 = jnp.bfloat16, jnp.float32
ROWS, DEPTH, WIDTH = 256, 8192, 512
CHUNK = 1024
STEPS = DEPTH // CHUNK
VMEM = pl.BlockSpec(memory_space=pltpu.VMEM)
SMEM = pl.BlockSpec(memory_space=pltpu.SMEM)
ANY = pl.BlockSpec(memory_space=pl.ANY)
HBM = pl.BlockSpec(memory_space=pltpu.HBM)


def index_of(y, x, c, z):
    return (((y % NY) * NX + x % NX) * NC + c % NC) * NZ + z % NZ


def pairs(route):
    every = [(y, x, c, z) for y in range(NY) for x in range(NX) for c in range(NC) for z in range(NZ)]
    return [(index_of(*p), index_of(*route(*p))) for p in every]


def to_x(y, x, c, z):
    return y, x + 1, c, z


def to_c(y, x, c, z):
    return y, x, c + 1, z


def to_z4(y, x, c, z):
    return y, x, c, z + 4


def to_xc(y, x, c, z):
    return y, x + 1, c + 1, z


def to_xz4(y, x, c, z):
    return y, x + 1, c, z + 4


def to_first(step):
    return lambda y, x, c, z: (y, x, c, z + step) if c == 0 else (y + step, x, c, z)


def to_second(step):
    return lambda y, x, c, z: (y + step, x, c, z) if c == 0 else (y, x, c, z + step)


def send(value, route):
    return lax.ppermute(value, GROUP, pairs(route))


def params(mib=24):
    return pltpu.CompilerParams(vmem_limit_bytes=mib << 20)


def row_numbers(at_ref):
    y, x, c, z = (at_ref[i] for i in range(4))
    at = lax.broadcasted_iota(jnp.int32, (ROWS, 1), 0)
    r, near, q1, q2, cr = at & 1, (at >> 1) & 3, (at >> 3) & 3, (at >> 5) & 3, at >> 7
    xr, z4 = near & 1, near >> 1
    o1 = jnp.where(q1 == 2, -1, jnp.where(q1 == 3, 2, q1))
    o2 = jnp.where(q2 == 2, -1, jnp.where(q2 == 3, 2, q2))
    core = c ^ cr
    zo = jnp.where(core == 0, o1, o2) + 4 * z4
    yo = jnp.where(core == 0, o2, o1)
    return ((((y + yo) & 3) * 2 + (x ^ xr)) * 2 + core) * 16 + ((z + zo) & 7) * 2 + r


def placed(rows):
    return rows == lax.broadcasted_iota(jnp.int32, (rows.shape[0], ROWS), 1)


def placed_in_half(rows):
    return (rows >> 5) * 16 + (rows & 15) == lax.broadcasted_iota(jnp.int32, (rows.shape[0], ROWS // 2), 1)


def hits(at_ref, targets_ref, place):
    own = jnp.sum(jnp.where(place, targets_ref[...], 0), axis=1, keepdims=True) - at_ref[4]
    return lax.broadcasted_iota(jnp.int32, (ROWS, WIDTH), 1) == own


def column_copies(source, target, sems):
    cuts = [pl.ds(k * CHUNK, CHUNK) for k in range(STEPS)]
    return [pltpu.make_async_copy(source.at[:, cut], target.at[:, cut], sems.at[k]) for k, cut in enumerate(cuts)]


def weight_copies(source, target, sems):
    cuts = [pl.ds(k * CHUNK, CHUNK) for k in range(STEPS)]
    copies = [pltpu.make_async_copy(source.at[cut], target.at[cut], sems.at[k]) for k, cut in enumerate(cuts)]
    for copy in copies:
        copy.start()
    return copies


def logits_kernel(at_ref, targets_ref, p0, p1, p2, p3, p4, p5, p6, p7, w_ref, stats_ref, other_stats_ref, own_hbm, other_hbm, own_ref, other_ref, own_sems, other_sems):
    acc = jnp.zeros((ROWS, WIDTH), F32)
    for k in range(STEPS):
        cut = slice(k * CHUNK, (k + 1) * CHUNK)
        left = jnp.concatenate([p[:, cut] for p in (p0, p1, p2, p3, p4, p5, p6, p7)], axis=0)
        acc += jnp.dot(left, w_ref[cut, :], preferred_element_type=F32)
    top = jnp.max(acc, axis=1, keepdims=True)
    soft = jnp.exp(acc - top)
    total = jnp.sum(soft, axis=1, keepdims=True)
    rows = row_numbers(at_ref)
    hit = hits(at_ref, targets_ref, placed(rows))
    picked = jnp.sum(jnp.where(hit, acc, 0.0), axis=1, keepdims=True)
    half = ROWS // 2
    place = placed_in_half(rows)
    for i, column in enumerate((top, total, picked)):
        stats_ref[i : i + 1, :] = jnp.sum(jnp.where(place[:half], column[:half], 0.0), axis=0, keepdims=True)
        other_stats_ref[i : i + 1, :] = jnp.sum(jnp.where(place[half:], column[half:], 0.0), axis=0, keepdims=True)
    own = (own_ref, column_copies(own_ref, own_hbm, own_sems))
    other = (other_ref, column_copies(other_ref, other_hbm, other_sems))
    products(jnp.where(hit, 0.0, soft).astype(BF), None, w_ref, (own, other))


def products(left, copies, w_ref, pairs):
    for k in range(STEPS):
        cut = slice(k * CHUNK, (k + 1) * CHUNK)
        if copies is not None:
            copies[k].wait()
        part = lax.dot_general(left, w_ref[cut, :], (((1,), (1,)), ((), ())), preferred_element_type=F32)
        first = 0
        for buffer, outs in pairs:
            buffer[:, cut] = part[first : first + buffer.shape[0]].astype(buffer.dtype)
            outs[k].start()
            first += buffer.shape[0]
    for _, outs in pairs:
        for copy in outs:
            copy.wait()


def target_kernel(at_ref, targets_ref, w_hbm, own_hbm, other_hbm, w_ref, own_ref, other_ref, w_sems, own_sems, other_sems):
    copies = weight_copies(w_hbm, w_ref, w_sems)
    left = jnp.where(hits(at_ref, targets_ref, placed(row_numbers(at_ref))), 1.0, 0.0).astype(BF)
    own = (own_ref, column_copies(own_ref, own_hbm, own_sems))
    other = (other_ref, column_copies(other_ref, other_hbm, other_sems))
    products(left, copies, w_ref, (own, other))


def merge_kernel(own_ref, core_ref, x_ref, both_ref, out_ref):
    refs = (own_ref, core_ref, x_ref, both_ref)
    tops = [r[0:1, :] for r in refs]
    top = jnp.maximum(jnp.maximum(tops[0], tops[1]), jnp.maximum(tops[2], tops[3]))
    total = sum(r[1:2, :] * jnp.exp(t - top) for r, t in zip(refs, tops))
    picked = sum(r[2:3, :] for r in refs)
    merged = jnp.concatenate([top, total, picked], axis=0)
    for i in range(out_ref.shape[0]):
        out_ref[i] = merged


def row_scales(at_ref, grad_ref, own_ref, core_ref, spread_ref):
    rows = row_numbers(at_ref)[: ROWS // 2]
    place = placed_in_half(rows)

    def ordered(row):
        return jnp.sum(jnp.where(place, row, 0.0), axis=1, keepdims=True)

    tops = spread_ref[:, 0, :]
    highest = jnp.max(tops, axis=0, keepdims=True)
    total = jnp.sum(spread_ref[:, 1, :] * jnp.exp(tops - highest), axis=0, keepdims=True)
    log_total = ordered(highest + jnp.log(total))
    picked = ordered(jnp.sum(spread_ref[:, 2, :], axis=0, keepdims=True))
    factor = 1.0 + 2.0 * zloss_coef * log_total
    grad = jnp.sum(jnp.where(placed(rows), grad_ref[...], 0.0), axis=1, keepdims=True)
    target = (grad * (jnp.exp(picked - log_total) * factor - 1.0)).astype(BF).astype(F32)
    own, core = (grad * factor * jnp.exp(ordered(ref[0:1, :]) - log_total) for ref in (own_ref, core_ref))
    lane = lax.broadcasted_iota(jnp.int32, (ROWS // 2, 128), 1)
    rest = jnp.where(lane == 2, target, jnp.where(lane == 3, log_total, picked))
    return jnp.where(lane == 0, own, jnp.where(lane == 1, core, rest))


def combine_start(parts, sources, buffers, sems):
    every = []
    for i, q in enumerate(parts):
        copies = [
            pltpu.make_async_copy(s.at[pl.ds(32 * q, 32)], t.at[i], sems.at[i, j])
            for j, (s, t) in enumerate(zip(sources, buffers))
        ]
        for copy in copies:
            copy.start()
        every.append(copies)
    return every


def combine_end(parts, every, scales_ref, buffers, outs):
    a_ref, b_ref, c_ref, d_ref = buffers
    for i, (q, out) in enumerate(zip(parts, outs)):
        for copy in every[i]:
            copy.wait()
        own, core, target = (scales_ref[32 * q : 32 * q + 32, j : j + 1] for j in range(3))
        for k in range(0, DEPTH, CHUNK):
            cut = slice(k, k + CHUNK)
            soft = own * a_ref[i, :, cut] + core * b_ref[i, :, cut].astype(F32)
            chosen = c_ref[i, :, cut].astype(F32) + d_ref[i, :, cut].astype(F32)
            out[:, cut] = (soft + target * chosen).astype(out.dtype)


def first_kernel(parts, at_ref, grad_ref, own_ref, core_ref, spread_ref, *refs):
    sources, scales_ref, outs, buffers, sems = refs[:4], refs[4], refs[5:-5], refs[-5:-1], refs[-1]
    every = combine_start(parts, sources, buffers, sems)
    scales_ref[...] = row_scales(at_ref, grad_ref, own_ref, core_ref, spread_ref)
    combine_end(parts, every, scales_ref, buffers, outs)


def combine_kernel(parts, scales_ref, *refs):
    sources, outs, buffers, sems = refs[:4], refs[4:-5], refs[-5:-1], refs[-1]
    combine_end(parts, combine_start(parts, sources, buffers, sems), scales_ref, buffers, outs)


def shards(hidden, lm_weight, targets, loss_grad):
    half = ROWS // 2
    at = jnp.stack([lax.axis_index(a) for a in GROUP] + [lax.axis_index(GROUP) * WIDTH])
    targets, loss_grad = targets.reshape(1, ROWS), loss_grad.reshape(1, ROWS)
    lm_weight_in, lm_weight = lm_weight, pltpu.with_memory_space_constraint(lm_weight, pltpu.HBM)
    weights = [pltpu.VMEM((DEPTH, WIDTH), BF)]
    sems = pltpu.SemaphoreType.DMA((STEPS,))

    block = jnp.concatenate([hidden] + [send(hidden, to) for to in (to_x, to_z4, to_xz4)])
    block = jnp.concatenate([block] + [send(block, to_first(-o)) for o in OFFSETS[1:]])
    near, back, far = (send(block, to_second(-o)) for o in OFFSETS[1:])

    aim, _ = lax.optimization_barrier((targets, block))
    target_own, target_out = pl.pallas_call(
        target_kernel,
        out_shape=[pltpu.HBM((half, DEPTH), BF)] * 2,
        in_specs=[SMEM, VMEM, ANY],
        out_specs=[HBM] * 2,
        scratch_shapes=weights + [pltpu.VMEM((half, DEPTH), BF)] * 2 + [sems] * 3,
        compiler_params=params(),
        cost_estimate=pl.CostEstimate(flops=2 * ROWS * DEPTH * WIDTH, bytes_accessed=12 << 20, transcendentals=0),
        name="target",
    )(at, aim, lm_weight)
    own, target_out = lax.optimization_barrier((block, target_out))
    pieces = [block, near, back, far] + [send(p, to_c) for p in (own, near, back, far)]

    own_stats, other_stats, soft_own, soft_out = pl.pallas_call(
        logits_kernel,
        out_shape=[jax.ShapeDtypeStruct((3, half), F32)] * 2 + [pltpu.HBM((half, DEPTH), F32), pltpu.HBM((half, DEPTH), BF)],
        in_specs=[SMEM] + [VMEM] * 10,
        out_specs=(VMEM, VMEM, HBM, HBM),
        scratch_shapes=[pltpu.VMEM((half, DEPTH), F32), pltpu.VMEM((half, DEPTH), BF)] + [sems] * 2,
        compiler_params=params(16),
        cost_estimate=pl.CostEstimate(flops=4 * ROWS * DEPTH * WIDTH, bytes_accessed=19 << 20, transcendentals=ROWS * WIDTH),
        name="logits",
    )(at, targets, *pieces, pltpu.with_memory_space_constraint(lm_weight_in, pltpu.VMEM))
    stats = [own_stats, send(other_stats, to_c), send(own_stats, to_x), send(other_stats, to_xc)]
    merged = pl.pallas_call(
        merge_kernel,
        out_shape=jax.ShapeDtypeStruct((32, 3, half), F32),
        in_specs=[VMEM] * 4,
        out_specs=VMEM,
        compiler_params=params(),
        name="merge",
    )(*stats)
    merged, soft_out, target_out = lax.optimization_barrier((merged, soft_out, target_out))
    soft_in, target_in = send(soft_out, to_c), send(target_out, to_c)
    spread = lax.all_to_all(merged, ("y", "z"), 0, 0)

    soft_own, target_own = (pltpu.with_memory_space_constraint(v, pltpu.HBM) for v in (soft_own, target_own))
    shares = (soft_own, soft_in, target_own, target_in)

    def combine(parts, dtype, kernel=combine_kernel, rows=()):
        n = len(parts)
        first = len(rows) > 1
        scales = [jax.ShapeDtypeStruct((half, 128), F32)] if first else []
        return pl.pallas_call(
            functools.partial(kernel, parts),
            out_shape=scales + [jax.ShapeDtypeStruct((32, DEPTH), dtype)] * n,
            in_specs=([SMEM] if first else []) + [VMEM] * (len(rows) - first) + [ANY] * 4,
            out_specs=[VMEM] * (n + first),
            scratch_shapes=[pltpu.VMEM((n, 32, DEPTH), F32)]
            + [pltpu.VMEM((n, 32, DEPTH), BF)] * 3
            + [pltpu.SemaphoreType.DMA((n, 4))],
            compiler_params=params(),
            cost_estimate=pl.CostEstimate(flops=6 * 32 * DEPTH * n, bytes_accessed=n * (3 << 20), transcendentals=0),
            name="combine",
        )(*rows, *shares)

    scales, far = combine((3,), BF, first_kernel, (at, loss_grad, stats[0], stats[1], spread))
    parts = [far, *combine((1, 2), BF, rows=(scales,))]
    log_total, target_logit = scales[:2, 3], scales[:2, 4]
    ce_loss = log_total - target_logit
    z_term = zloss_coef * log_total * log_total
    arrived = [send(p, to_second(o)).astype(F32) for p, o in zip(parts, (2, 1, -1))]
    part = combine((0,), F32, rows=(scales,))[0] + sum(arrived)
    part = part.reshape(4, 8, DEPTH)
    part = part[0] + sum(send(part[k].astype(BF), to_first(OFFSETS[k])).astype(F32) for k in (3, 1, 2))
    part = [part[0:2], send(part[2:4], to_x)] + [
        send(part[2 * k : 2 * k + 2].astype(BF), to).astype(F32) for k, to in ((3, to_xz4), (2, to_z4))
    ]
    part = (part[0] + part[1]) + (part[2] + part[3])
    return ce_loss, z_term, part.astype(BF)


def solution(mesh):
    mesh = Mesh(mesh.devices.reshape(NY, NX, NC, NZ, 2), (*GROUP, "dp"))
    own = ("dp", *GROUP)
    in_specs = (P(own, None), P(None, GROUP), P("dp"), P("dp"))
    out_specs = (P(own), P(own), P(own, None))
    return jax.shard_map(shards, mesh=mesh, in_specs=in_specs, out_specs=out_specs, check_vma=False)
```

```python
import functools

import jax
import jax.numpy as jnp
from jax import lax
from jax.experimental import pallas as pl
from jax.experimental.pallas import tpu as pltpu
from jax.sharding import Mesh
from jax.sharding import PartitionSpec as P

zloss_coef = 0.0001
NY, NX, NC, NZ = 4, 2, 2, 8
GROUP = ("y", "x", "c", "z")
OFFSETS = (0, 1, -1, 2)
BF, F32 = jnp.bfloat16, jnp.float32
ROWS, DEPTH, WIDTH = 256, 8192, 512
CHUNK = 1024
STEPS = DEPTH // CHUNK
VMEM = pl.BlockSpec(memory_space=pltpu.VMEM)
SMEM = pl.BlockSpec(memory_space=pltpu.SMEM)
ANY = pl.BlockSpec(memory_space=pl.ANY)
HBM = pl.BlockSpec(memory_space=pltpu.HBM)


def index_of(y, x, c, z):
    return (((y % NY) * NX + x % NX) * NC + c % NC) * NZ + z % NZ


def pairs(route):
    every = [(y, x, c, z) for y in range(NY) for x in range(NX) for c in range(NC) for z in range(NZ)]
    return [(index_of(*p), index_of(*route(*p))) for p in every]


def to_x(y, x, c, z):
    return y, x + 1, c, z


def to_c(y, x, c, z):
    return y, x, c + 1, z


def to_z4(y, x, c, z):
    return y, x, c, z + 4


def to_xc(y, x, c, z):
    return y, x + 1, c + 1, z


def to_xz4(y, x, c, z):
    return y, x + 1, c, z + 4


def to_first(step):
    return lambda y, x, c, z: (y, x, c, z + step) if c == 0 else (y + step, x, c, z)


def to_second(step):
    return lambda y, x, c, z: (y + step, x, c, z) if c == 0 else (y, x, c, z + step)


def send(value, route):
    return lax.ppermute(value, GROUP, pairs(route))


def params(mib=24):
    return pltpu.CompilerParams(vmem_limit_bytes=mib << 20)


def row_numbers(at_ref):
    y, x, c, z = (at_ref[i] for i in range(4))
    at = lax.broadcasted_iota(jnp.int32, (ROWS, 1), 0)
    r, near, q1, q2, cr = at & 1, (at >> 1) & 3, (at >> 3) & 3, (at >> 5) & 3, at >> 7
    xr, z4 = near & 1, near >> 1
    o1 = jnp.where(q1 == 2, -1, jnp.where(q1 == 3, 2, q1))
    o2 = jnp.where(q2 == 2, -1, jnp.where(q2 == 3, 2, q2))
    core = c ^ cr
    zo = jnp.where(core == 0, o1, o2) + 4 * z4
    yo = jnp.where(core == 0, o2, o1)
    return ((((y + yo) & 3) * 2 + (x ^ xr)) * 2 + core) * 16 + ((z + zo) & 7) * 2 + r


def placed(rows):
    return rows == lax.broadcasted_iota(jnp.int32, (rows.shape[0], ROWS), 1)


def placed_in_half(rows):
    return (rows >> 5) * 16 + (rows & 15) == lax.broadcasted_iota(jnp.int32, (rows.shape[0], ROWS // 2), 1)


def hits(at_ref, targets_ref, place):
    own = jnp.sum(jnp.where(place, targets_ref[...], 0), axis=1, keepdims=True) - at_ref[4]
    return lax.broadcasted_iota(jnp.int32, (ROWS, WIDTH), 1) == own


def column_copies(source, target, sems):
    cuts = [pl.ds(k * CHUNK, CHUNK) for k in range(STEPS)]
    return [pltpu.make_async_copy(source.at[:, cut], target.at[:, cut], sems.at[k]) for k, cut in enumerate(cuts)]


def weight_copies(source, target, sems):
    cuts = [pl.ds(k * CHUNK, CHUNK) for k in range(STEPS)]
    copies = [pltpu.make_async_copy(source.at[cut], target.at[cut], sems.at[k]) for k, cut in enumerate(cuts)]
    for copy in copies:
        copy.start()
    return copies


def logits_kernel(at_ref, targets_ref, p0, p1, p2, p3, p4, p5, p6, p7, w_ref, stats_ref, other_stats_ref, soft_ref):
    acc = jnp.zeros((ROWS, WIDTH), F32)
    for k in range(STEPS):
        cut = slice(k * CHUNK, (k + 1) * CHUNK)
        left = jnp.concatenate([p[:, cut] for p in (p0, p1, p2, p3, p4, p5, p6, p7)], axis=0)
        acc += jnp.dot(left, w_ref[cut, :], preferred_element_type=F32)
    top = jnp.max(acc, axis=1, keepdims=True)
    soft = jnp.exp(acc - top)
    total = jnp.sum(soft, axis=1, keepdims=True)
    rows = row_numbers(at_ref)
    hit = hits(at_ref, targets_ref, placed(rows))
    picked = jnp.sum(jnp.where(hit, acc, 0.0), axis=1, keepdims=True)
    half = ROWS // 2
    place = placed_in_half(rows)
    for i, column in enumerate((top, total, picked)):
        stats_ref[i : i + 1, :] = jnp.sum(jnp.where(place[:half], column[:half], 0.0), axis=0, keepdims=True)
        other_stats_ref[i : i + 1, :] = jnp.sum(jnp.where(place[half:], column[half:], 0.0), axis=0, keepdims=True)
    soft_ref[...] = jnp.where(hit, 0.0, soft).astype(BF)


def soft_kernel(soft_ref, w_ref, own_hbm, other_hbm, own_ref, other_ref, own_sems, other_sems):
    own = (own_ref, column_copies(own_ref, own_hbm, own_sems))
    other = (other_ref, column_copies(other_ref, other_hbm, other_sems))
    products(soft_ref[...], None, w_ref, (own, other))


def products(left, copies, w_ref, pairs):
    for k in range(STEPS):
        cut = slice(k * CHUNK, (k + 1) * CHUNK)
        if copies is not None:
            copies[k].wait()
        part = lax.dot_general(left, w_ref[cut, :], (((1,), (1,)), ((), ())), preferred_element_type=F32)
        first = 0
        for buffer, outs in pairs:
            buffer[:, cut] = part[first : first + buffer.shape[0]].astype(buffer.dtype)
            outs[k].start()
            first += buffer.shape[0]
    for _, outs in pairs:
        for copy in outs:
            copy.wait()


def target_kernel(at_ref, targets_ref, w_hbm, own_hbm, other_hbm, w_ref, own_ref, other_ref, w_sems, own_sems, other_sems):
    copies = weight_copies(w_hbm, w_ref, w_sems)
    left = jnp.where(hits(at_ref, targets_ref, placed(row_numbers(at_ref))), 1.0, 0.0).astype(BF)
    own = (own_ref, column_copies(own_ref, own_hbm, own_sems))
    other = (other_ref, column_copies(other_ref, other_hbm, other_sems))
    products(left, copies, w_ref, (own, other))


def merge_kernel(own_ref, core_ref, x_ref, both_ref, out_ref):
    refs = (own_ref, core_ref, x_ref, both_ref)
    tops = [r[0:1, :] for r in refs]
    top = jnp.maximum(jnp.maximum(tops[0], tops[1]), jnp.maximum(tops[2], tops[3]))
    total = sum(r[1:2, :] * jnp.exp(t - top) for r, t in zip(refs, tops))
    picked = sum(r[2:3, :] for r in refs)
    merged = jnp.concatenate([top, total, picked], axis=0)
    for i in range(out_ref.shape[0]):
        out_ref[i] = merged


def row_scales(at_ref, grad_ref, own_ref, core_ref, spread_ref):
    rows = row_numbers(at_ref)[: ROWS // 2]
    place = placed_in_half(rows)

    def ordered(row):
        return jnp.sum(jnp.where(place, row, 0.0), axis=1, keepdims=True)

    tops = spread_ref[:, 0, :]
    highest = jnp.max(tops, axis=0, keepdims=True)
    total = jnp.sum(spread_ref[:, 1, :] * jnp.exp(tops - highest), axis=0, keepdims=True)
    log_total = ordered(highest + jnp.log(total))
    picked = ordered(jnp.sum(spread_ref[:, 2, :], axis=0, keepdims=True))
    factor = 1.0 + 2.0 * zloss_coef * log_total
    grad = jnp.sum(jnp.where(placed(rows), grad_ref[...], 0.0), axis=1, keepdims=True)
    target = (grad * (jnp.exp(picked - log_total) * factor - 1.0)).astype(BF).astype(F32)
    own, core = (grad * factor * jnp.exp(ordered(ref[0:1, :]) - log_total) for ref in (own_ref, core_ref))
    lane = lax.broadcasted_iota(jnp.int32, (ROWS // 2, 128), 1)
    rest = jnp.where(lane == 2, target, jnp.where(lane == 3, log_total, picked))
    return jnp.where(lane == 0, own, jnp.where(lane == 1, core, rest))


def combine_start(parts, sources, buffers, sems):
    every = []
    for i, q in enumerate(parts):
        copies = [
            pltpu.make_async_copy(s.at[pl.ds(32 * q, 32)], t.at[i], sems.at[i, j])
            for j, (s, t) in enumerate(zip(sources, buffers))
        ]
        for copy in copies:
            copy.start()
        every.append(copies)
    return every


def combine_end(parts, every, scales_ref, buffers, outs):
    a_ref, b_ref, c_ref, d_ref = buffers
    for i, (q, out) in enumerate(zip(parts, outs)):
        for copy in every[i]:
            copy.wait()
        own, core, target = (scales_ref[32 * q : 32 * q + 32, j : j + 1] for j in range(3))
        for k in range(0, DEPTH, CHUNK):
            cut = slice(k, k + CHUNK)
            soft = own * a_ref[i, :, cut] + core * b_ref[i, :, cut].astype(F32)
            chosen = c_ref[i, :, cut].astype(F32) + d_ref[i, :, cut].astype(F32)
            out[:, cut] = (soft + target * chosen).astype(out.dtype)


def first_kernel(parts, at_ref, grad_ref, own_ref, core_ref, spread_ref, *refs):
    sources, scales_ref, outs, buffers, sems = refs[:4], refs[4], refs[5:-5], refs[-5:-1], refs[-1]
    every = combine_start(parts, sources, buffers, sems)
    scales_ref[...] = row_scales(at_ref, grad_ref, own_ref, core_ref, spread_ref)
    combine_end(parts, every, scales_ref, buffers, outs)


def combine_kernel(parts, scales_ref, *refs):
    sources, outs, buffers, sems = refs[:4], refs[4:-5], refs[-5:-1], refs[-1]
    combine_end(parts, combine_start(parts, sources, buffers, sems), scales_ref, buffers, outs)


def shards(hidden, lm_weight, targets, loss_grad):
    half = ROWS // 2
    at = jnp.stack([lax.axis_index(a) for a in GROUP] + [lax.axis_index(GROUP) * WIDTH])
    targets, loss_grad = targets.reshape(1, ROWS), loss_grad.reshape(1, ROWS)
    lm_weight_in, lm_weight = lm_weight, pltpu.with_memory_space_constraint(lm_weight, pltpu.HBM)
    weights = [pltpu.VMEM((DEPTH, WIDTH), BF)]
    sems = pltpu.SemaphoreType.DMA((STEPS,))

    block = jnp.concatenate([hidden] + [send(hidden, to) for to in (to_x, to_z4, to_xz4)])
    block = jnp.concatenate([block] + [send(block, to_first(-o)) for o in OFFSETS[1:]])
    near, back, far = (send(block, to_second(-o)) for o in OFFSETS[1:])

    aim, _ = lax.optimization_barrier((targets, block))
    target_own, target_out = pl.pallas_call(
        target_kernel,
        out_shape=[pltpu.HBM((half, DEPTH), BF)] * 2,
        in_specs=[SMEM, VMEM, ANY],
        out_specs=[HBM] * 2,
        scratch_shapes=weights + [pltpu.VMEM((half, DEPTH), BF)] * 2 + [sems] * 3,
        compiler_params=params(),
        cost_estimate=pl.CostEstimate(flops=2 * ROWS * DEPTH * WIDTH, bytes_accessed=12 << 20, transcendentals=0),
        name="target",
    )(at, aim, lm_weight)
    own, target_out = lax.optimization_barrier((block, target_out))
    pieces = [block, near, back, far] + [send(p, to_c) for p in (own, near, back, far)]

    near_weights = pltpu.with_memory_space_constraint(lm_weight_in, pltpu.VMEM)
    own_stats, other_stats, soft = pl.pallas_call(
        logits_kernel,
        out_shape=[jax.ShapeDtypeStruct((3, half), F32)] * 2 + [jax.ShapeDtypeStruct((ROWS, WIDTH), BF)],
        in_specs=[SMEM] + [VMEM] * 10,
        out_specs=[VMEM] * 3,
        compiler_params=params(16),
        cost_estimate=pl.CostEstimate(flops=2 * ROWS * DEPTH * WIDTH, bytes_accessed=13 << 20, transcendentals=ROWS * WIDTH),
        name="logits",
    )(at, targets, *pieces, near_weights)
    soft_own, soft_out = pl.pallas_call(
        soft_kernel,
        out_shape=(pltpu.HBM((half, DEPTH), F32), pltpu.HBM((half, DEPTH), BF)),
        in_specs=[VMEM] * 2,
        out_specs=(HBM, HBM),
        scratch_shapes=[pltpu.VMEM((half, DEPTH), F32), pltpu.VMEM((half, DEPTH), BF)] + [sems] * 2,
        compiler_params=params(16),
        cost_estimate=pl.CostEstimate(flops=2 * ROWS * DEPTH * WIDTH, bytes_accessed=14 << 20, transcendentals=0),
        name="soft",
    )(soft, near_weights)
    stats = [own_stats, send(other_stats, to_c), send(own_stats, to_x), send(other_stats, to_xc)]
    merged = pl.pallas_call(
        merge_kernel,
        out_shape=jax.ShapeDtypeStruct((32, 3, half), F32),
        in_specs=[VMEM] * 4,
        out_specs=VMEM,
        compiler_params=params(),
        name="merge",
    )(*stats)
    merged, soft_out, target_out = lax.optimization_barrier((merged, soft_out, target_out))
    soft_in, target_in = send(soft_out, to_c), send(target_out, to_c)
    spread = lax.all_to_all(merged, ("y", "z"), 0, 0)

    soft_own, target_own = (pltpu.with_memory_space_constraint(v, pltpu.HBM) for v in (soft_own, target_own))
    shares = (soft_own, soft_in, target_own, target_in)

    def combine(parts, dtype, kernel=combine_kernel, rows=()):
        n = len(parts)
        first = len(rows) > 1
        scales = [jax.ShapeDtypeStruct((half, 128), F32)] if first else []
        return pl.pallas_call(
            functools.partial(kernel, parts),
            out_shape=scales + [jax.ShapeDtypeStruct((32, DEPTH), dtype)] * n,
            in_specs=([SMEM] if first else []) + [VMEM] * (len(rows) - first) + [ANY] * 4,
            out_specs=[VMEM] * (n + first),
            scratch_shapes=[pltpu.VMEM((n, 32, DEPTH), F32)]
            + [pltpu.VMEM((n, 32, DEPTH), BF)] * 3
            + [pltpu.SemaphoreType.DMA((n, 4))],
            compiler_params=params(),
            cost_estimate=pl.CostEstimate(flops=6 * 32 * DEPTH * n, bytes_accessed=n * (3 << 20), transcendentals=0),
            name="combine",
        )(*rows, *shares)

    scales, *parts = combine((3, 1, 2), BF, first_kernel, (at, loss_grad, stats[0], stats[1], spread))
    log_total, target_logit = scales[:2, 3], scales[:2, 4]
    ce_loss = log_total - target_logit
    z_term = zloss_coef * log_total * log_total
    arrived = [send(p, to_second(o)).astype(F32) for p, o in zip(parts, (2, 1, -1))]
    part = combine((0,), F32, rows=(scales,))[0] + sum(arrived)
    part = part.reshape(4, 8, DEPTH)
    part = part[0] + sum(send(part[k].astype(BF), to_first(OFFSETS[k])).astype(F32) for k in (3, 1, 2))
    moved = [send(part[2 * k : 2 * k + 2].astype(BF), to).astype(F32) for k, to in ((3, to_xz4), (2, to_z4))]
    part = [part[0:2], *moved, send(part[2:4], to_x)]
    part = (part[0] + part[1]) + (part[2] + part[3])
    return ce_loss, z_term, part.astype(BF)


def solution(mesh):
    mesh = Mesh(mesh.devices.reshape(NY, NX, NC, NZ, 2), (*GROUP, "dp"))
    own = ("dp", *GROUP)
    in_specs = (P(own, None), P(None, GROUP), P("dp"), P("dp"))
    out_specs = (P(own), P(own), P(own, None))
    return jax.shard_map(shards, mesh=mesh, in_specs=in_specs, out_specs=out_specs, check_vma=False)
```

```python
import functools

import jax
import jax.numpy as jnp
from jax import lax
from jax.experimental import pallas as pl
from jax.experimental.pallas import tpu as pltpu
from jax.sharding import Mesh
from jax.sharding import PartitionSpec as P

zloss_coef = 0.0001
NY, NX, NC, NZ = 4, 2, 2, 8
GROUP = ("y", "x", "c", "z")
OFFSETS = (0, 1, -1, 2)
BF, F32 = jnp.bfloat16, jnp.float32
ROWS, DEPTH, WIDTH = 256, 8192, 512
CHUNK = 1024
STEPS = DEPTH // CHUNK
VMEM = pl.BlockSpec(memory_space=pltpu.VMEM)
SMEM = pl.BlockSpec(memory_space=pltpu.SMEM)
ANY = pl.BlockSpec(memory_space=pl.ANY)
HBM = pl.BlockSpec(memory_space=pltpu.HBM)


def index_of(y, x, c, z):
    return (((y % NY) * NX + x % NX) * NC + c % NC) * NZ + z % NZ


def pairs(route):
    every = [(y, x, c, z) for y in range(NY) for x in range(NX) for c in range(NC) for z in range(NZ)]
    return [(index_of(*p), index_of(*route(*p))) for p in every]


def to_x(y, x, c, z):
    return y, x + 1, c, z


def to_c(y, x, c, z):
    return y, x, c + 1, z


def to_z4(y, x, c, z):
    return y, x, c, z + 4


def to_xc(y, x, c, z):
    return y, x + 1, c + 1, z


def to_xz4(y, x, c, z):
    return y, x + 1, c, z + 4


def to_first(step):
    return lambda y, x, c, z: (y, x, c, z + step) if c == 0 else (y + step, x, c, z)


def to_second(step):
    return lambda y, x, c, z: (y + step, x, c, z) if c == 0 else (y, x, c, z + step)


def send(value, route):
    return lax.ppermute(value, GROUP, pairs(route))


def params(mib=24):
    return pltpu.CompilerParams(vmem_limit_bytes=mib << 20)


def row_numbers(at_ref):
    y, x, c, z = (at_ref[i] for i in range(4))
    at = lax.broadcasted_iota(jnp.int32, (ROWS, 1), 0)
    r, near, q1, q2, cr = at & 1, (at >> 1) & 3, (at >> 3) & 3, (at >> 5) & 3, at >> 7
    xr, z4 = (near ^ (near >> 1)) & 1, near >> 1
    o1 = jnp.where(q1 == 2, -1, jnp.where(q1 == 3, 2, q1))
    o2 = jnp.where(q2 == 2, -1, jnp.where(q2 == 3, 2, q2))
    core = c ^ cr
    zo = jnp.where(core == 0, o1, o2) + 4 * z4
    yo = jnp.where(core == 0, o2, o1)
    return ((((y + yo) & 3) * 2 + (x ^ xr)) * 2 + core) * 16 + ((z + zo) & 7) * 2 + r


def placed(rows):
    return rows == lax.broadcasted_iota(jnp.int32, (rows.shape[0], ROWS), 1)


def placed_in_half(rows):
    return (rows >> 5) * 16 + (rows & 15) == lax.broadcasted_iota(jnp.int32, (rows.shape[0], ROWS // 2), 1)


def hits(at_ref, targets_ref, place):
    own = jnp.sum(jnp.where(place, targets_ref[...], 0), axis=1, keepdims=True) - at_ref[4]
    return lax.broadcasted_iota(jnp.int32, (ROWS, WIDTH), 1) == own


def column_copies(source, target, sems):
    cuts = [pl.ds(k * CHUNK, CHUNK) for k in range(STEPS)]
    return [pltpu.make_async_copy(source.at[:, cut], target.at[:, cut], sems.at[k]) for k, cut in enumerate(cuts)]


def weight_copies(source, target, sems):
    cuts = [pl.ds(k * CHUNK, CHUNK) for k in range(STEPS)]
    copies = [pltpu.make_async_copy(source.at[cut], target.at[cut], sems.at[k]) for k, cut in enumerate(cuts)]
    for copy in copies:
        copy.start()
    return copies


def logits_kernel(at_ref, targets_ref, p0, p1, p2, p3, p4, p5, p6, p7, w_ref, stats_ref, other_stats_ref, soft_ref):
    acc = jnp.zeros((ROWS, WIDTH), F32)
    for k in range(STEPS):
        cut = slice(k * CHUNK, (k + 1) * CHUNK)
        left = jnp.concatenate([p[:, cut] for p in (p0, p1, p2, p3, p4, p5, p6, p7)], axis=0)
        acc += jnp.dot(left, w_ref[cut, :], preferred_element_type=F32)
    top = jnp.max(acc, axis=1, keepdims=True)
    soft = jnp.exp(acc - top)
    total = jnp.sum(soft, axis=1, keepdims=True)
    rows = row_numbers(at_ref)
    hit = hits(at_ref, targets_ref, placed(rows))
    picked = jnp.sum(jnp.where(hit, acc, 0.0), axis=1, keepdims=True)
    half = ROWS // 2
    place = placed_in_half(rows)
    for i, column in enumerate((top, total, picked)):
        stats_ref[i : i + 1, :] = jnp.sum(jnp.where(place[:half], column[:half], 0.0), axis=0, keepdims=True)
        other_stats_ref[i : i + 1, :] = jnp.sum(jnp.where(place[half:], column[half:], 0.0), axis=0, keepdims=True)
    soft_ref[...] = jnp.where(hit, 0.0, soft).astype(BF)


def soft_kernel(soft_ref, w_ref, own_hbm, other_hbm, own_ref, other_ref, own_sems, other_sems):
    own = (own_ref, column_copies(own_ref, own_hbm, own_sems))
    other = (other_ref, column_copies(other_ref, other_hbm, other_sems))
    products(soft_ref[...], None, w_ref, (own, other))


def products(left, copies, w_ref, pairs):
    for k in range(STEPS):
        cut = slice(k * CHUNK, (k + 1) * CHUNK)
        if copies is not None:
            copies[k].wait()
        part = lax.dot_general(left, w_ref[cut, :], (((1,), (1,)), ((), ())), preferred_element_type=F32)
        first = 0
        for buffer, outs in pairs:
            buffer[:, cut] = part[first : first + buffer.shape[0]].astype(buffer.dtype)
            outs[k].start()
            first += buffer.shape[0]
    for _, outs in pairs:
        for copy in outs:
            copy.wait()


def target_kernel(at_ref, targets_ref, w_hbm, own_hbm, other_hbm, w_ref, own_ref, other_ref, w_sems, own_sems, other_sems):
    copies = weight_copies(w_hbm, w_ref, w_sems)
    left = jnp.where(hits(at_ref, targets_ref, placed(row_numbers(at_ref))), 1.0, 0.0).astype(BF)
    own = (own_ref, column_copies(own_ref, own_hbm, own_sems))
    other = (other_ref, column_copies(other_ref, other_hbm, other_sems))
    products(left, copies, w_ref, (own, other))


def merge_kernel(own_ref, core_ref, x_ref, both_ref, out_ref):
    refs = (own_ref, core_ref, x_ref, both_ref)
    tops = [r[0:1, :] for r in refs]
    top = jnp.maximum(jnp.maximum(tops[0], tops[1]), jnp.maximum(tops[2], tops[3]))
    total = sum(r[1:2, :] * jnp.exp(t - top) for r, t in zip(refs, tops))
    picked = sum(r[2:3, :] for r in refs)
    merged = jnp.concatenate([top, total, picked], axis=0)
    for i in range(out_ref.shape[0]):
        out_ref[i] = merged


def row_scales(at_ref, grad_ref, own_ref, core_ref, spread_ref):
    rows = row_numbers(at_ref)[: ROWS // 2]
    place = placed_in_half(rows)

    def ordered(row):
        return jnp.sum(jnp.where(place, row, 0.0), axis=1, keepdims=True)

    tops = spread_ref[:, 0, :]
    highest = jnp.max(tops, axis=0, keepdims=True)
    total = jnp.sum(spread_ref[:, 1, :] * jnp.exp(tops - highest), axis=0, keepdims=True)
    log_total = ordered(highest + jnp.log(total))
    picked = ordered(jnp.sum(spread_ref[:, 2, :], axis=0, keepdims=True))
    factor = 1.0 + 2.0 * zloss_coef * log_total
    grad = jnp.sum(jnp.where(placed(rows), grad_ref[...], 0.0), axis=1, keepdims=True)
    target = (grad * (jnp.exp(picked - log_total) * factor - 1.0)).astype(BF).astype(F32)
    own, core = (grad * factor * jnp.exp(ordered(ref[0:1, :]) - log_total) for ref in (own_ref, core_ref))
    lane = lax.broadcasted_iota(jnp.int32, (ROWS // 2, 128), 1)
    rest = jnp.where(lane == 2, target, jnp.where(lane == 3, log_total, picked))
    return jnp.where(lane == 0, own, jnp.where(lane == 1, core, rest))


def combine_start(parts, sources, buffers, sems):
    every = []
    for i, q in enumerate(parts):
        copies = [
            pltpu.make_async_copy(s.at[pl.ds(32 * q, 32)], t.at[i], sems.at[i, j])
            for j, (s, t) in enumerate(zip(sources, buffers))
        ]
        for copy in copies:
            copy.start()
        every.append(copies)
    return every


def combine_end(parts, every, scales_ref, buffers, outs):
    a_ref, b_ref, c_ref, d_ref = buffers
    for i, (q, out) in enumerate(zip(parts, outs)):
        for copy in every[i]:
            copy.wait()
        own, core, target = (scales_ref[32 * q : 32 * q + 32, j : j + 1] for j in range(3))
        for k in range(0, DEPTH, CHUNK):
            cut = slice(k, k + CHUNK)
            soft = own * a_ref[i, :, cut] + core * b_ref[i, :, cut].astype(F32)
            chosen = c_ref[i, :, cut].astype(F32) + d_ref[i, :, cut].astype(F32)
            out[:, cut] = (soft + target * chosen).astype(out.dtype)


def first_kernel(parts, at_ref, grad_ref, own_ref, core_ref, spread_ref, *refs):
    sources, scales_ref, outs, buffers, sems = refs[:4], refs[4], refs[5:-5], refs[-5:-1], refs[-1]
    every = combine_start(parts, sources, buffers, sems)
    scales_ref[...] = row_scales(at_ref, grad_ref, own_ref, core_ref, spread_ref)
    combine_end(parts, every, scales_ref, buffers, outs)


def combine_kernel(parts, scales_ref, *refs):
    sources, outs, buffers, sems = refs[:4], refs[4:-5], refs[-5:-1], refs[-1]
    combine_end(parts, combine_start(parts, sources, buffers, sems), scales_ref, buffers, outs)


def join_kernel(a_ref, b_ref, c_ref, d_ref, out_ref):
    out_ref[...] = jnp.concatenate([r[...] for r in (a_ref, b_ref, c_ref, d_ref)], axis=0)


def shards(hidden, lm_weight, targets, loss_grad):
    half = ROWS // 2
    at = jnp.stack([lax.axis_index(a) for a in GROUP] + [lax.axis_index(GROUP) * WIDTH])
    targets, loss_grad = targets.reshape(1, ROWS), loss_grad.reshape(1, ROWS)
    lm_weight_in, lm_weight = lm_weight, pltpu.with_memory_space_constraint(lm_weight, pltpu.HBM)
    weights = [pltpu.VMEM((DEPTH, WIDTH), BF)]
    sems = pltpu.SemaphoreType.DMA((STEPS,))

    block = jnp.concatenate([hidden] + [send(hidden, to) for to in (to_x, to_xz4, to_z4)])
    block = pl.pallas_call(
        join_kernel,
        out_shape=jax.ShapeDtypeStruct((32, DEPTH), BF),
        in_specs=[VMEM] * 4,
        out_specs=VMEM,
        compiler_params=params(),
        name="join",
    )(block, *(send(block, to_first(-o)) for o in OFFSETS[1:]))
    near, back, far = (send(block, to_second(-o)) for o in OFFSETS[1:])

    aim, _ = lax.optimization_barrier((targets, block))
    target_own, target_out = pl.pallas_call(
        target_kernel,
        out_shape=[pltpu.HBM((half, DEPTH), BF)] * 2,
        in_specs=[SMEM, VMEM, ANY],
        out_specs=[HBM] * 2,
        scratch_shapes=weights + [pltpu.VMEM((half, DEPTH), BF)] * 2 + [sems] * 3,
        compiler_params=params(),
        cost_estimate=pl.CostEstimate(flops=2 * ROWS * DEPTH * WIDTH, bytes_accessed=12 << 20, transcendentals=0),
        name="target",
    )(at, aim, lm_weight)
    own, target_out = lax.optimization_barrier((block, target_out))
    pieces = [block, near, back, far] + [send(p, to_c) for p in (own, near, back, far)]

    near_weights = pltpu.with_memory_space_constraint(lm_weight_in, pltpu.VMEM)
    own_stats, other_stats, soft = pl.pallas_call(
        logits_kernel,
        out_shape=[jax.ShapeDtypeStruct((3, half), F32)] * 2 + [jax.ShapeDtypeStruct((ROWS, WIDTH), BF)],
        in_specs=[SMEM] + [VMEM] * 10,
        out_specs=[VMEM] * 3,
        compiler_params=params(16),
        cost_estimate=pl.CostEstimate(flops=2 * ROWS * DEPTH * WIDTH, bytes_accessed=13 << 20, transcendentals=ROWS * WIDTH),
        name="logits",
    )(at, targets, *pieces, near_weights)
    soft_own, soft_out = pl.pallas_call(
        soft_kernel,
        out_shape=(pltpu.HBM((half, DEPTH), F32), pltpu.HBM((half, DEPTH), BF)),
        in_specs=[VMEM] * 2,
        out_specs=(HBM, HBM),
        scratch_shapes=[pltpu.VMEM((half, DEPTH), F32), pltpu.VMEM((half, DEPTH), BF)] + [sems] * 2,
        compiler_params=params(16),
        cost_estimate=pl.CostEstimate(flops=2 * ROWS * DEPTH * WIDTH, bytes_accessed=14 << 20, transcendentals=0),
        name="soft",
    )(soft, near_weights)
    stats = [own_stats, send(other_stats, to_c), send(own_stats, to_x), send(other_stats, to_xc)]
    merged = pl.pallas_call(
        merge_kernel,
        out_shape=jax.ShapeDtypeStruct((32, 3, half), F32),
        in_specs=[VMEM] * 4,
        out_specs=VMEM,
        compiler_params=params(),
        name="merge",
    )(*stats)
    merged, soft_out, target_out = lax.optimization_barrier((merged, soft_out, target_out))
    soft_in, target_in = send(soft_out, to_c), send(target_out, to_c)
    spread = lax.all_to_all(merged, ("y", "z"), 0, 0)

    soft_own, target_own = (pltpu.with_memory_space_constraint(v, pltpu.HBM) for v in (soft_own, target_own))
    shares = (soft_own, soft_in, target_own, target_in)

    def combine(parts, dtype, kernel=combine_kernel, rows=()):
        n = len(parts)
        first = len(rows) > 1
        scales = [jax.ShapeDtypeStruct((half, 128), F32)] if first else []
        return pl.pallas_call(
            functools.partial(kernel, parts),
            out_shape=scales + [jax.ShapeDtypeStruct((32, DEPTH), dtype)] * n,
            in_specs=([SMEM] if first else []) + [VMEM] * (len(rows) - first) + [ANY] * 4,
            out_specs=[VMEM] * (n + first),
            scratch_shapes=[pltpu.VMEM((n, 32, DEPTH), F32)]
            + [pltpu.VMEM((n, 32, DEPTH), BF)] * 3
            + [pltpu.SemaphoreType.DMA((n, 4))],
            compiler_params=params(),
            cost_estimate=pl.CostEstimate(flops=6 * 32 * DEPTH * n, bytes_accessed=n * (3 << 20), transcendentals=0),
            name="combine",
        )(*rows, *shares)

    scales, *parts = combine((3, 1, 2), BF, first_kernel, (at, loss_grad, stats[0], stats[1], spread))
    log_total, target_logit = scales[:2, 3], scales[:2, 4]
    ce_loss = log_total - target_logit
    z_term = zloss_coef * log_total * log_total
    arrived = [send(p, to_second(o)).astype(F32) for p, o in zip(parts, (2, 1, -1))]
    part = combine((0,), F32, rows=(scales,))[0] + sum(arrived)
    part = part.reshape(4, 8, DEPTH)
    part = part[0] + sum(send(part[k].astype(BF), to_first(OFFSETS[k])).astype(F32) for k in (3, 1, 2))
    moved = [send(part[2 * k : 2 * k + 2].astype(BF), to).astype(F32) for k, to in ((2, to_xz4), (3, to_z4))]
    part = [part[0:2], *moved, send(part[2:4], to_x)]
    part = (part[0] + part[1]) + (part[2] + part[3])
    return ce_loss, z_term, part.astype(BF)


def solution(mesh):
    mesh = Mesh(mesh.devices.reshape(NY, NX, NC, NZ, 2), (*GROUP, "dp"))
    own = ("dp", *GROUP)
    in_specs = (P(own, None), P(None, GROUP), P("dp"), P("dp"))
    out_specs = (P(own), P(own), P(own, None))
    return jax.shard_map(shards, mesh=mesh, in_specs=in_specs, out_specs=out_specs, check_vma=False)
```

```python
import functools

import jax
import jax.numpy as jnp
from jax import lax
from jax.experimental import pallas as pl
from jax.experimental.pallas import tpu as pltpu
from jax.sharding import Mesh
from jax.sharding import PartitionSpec as P

zloss_coef = 0.0001
NY, NX, NC, NZ = 4, 2, 2, 8
GROUP = ("y", "x", "c", "z")
OFFSETS = (0, 1, -1, 2)
BF, F32 = jnp.bfloat16, jnp.float32
ROWS, DEPTH, WIDTH = 256, 8192, 512
CHUNK = 1024
STEPS = DEPTH // CHUNK
VMEM = pl.BlockSpec(memory_space=pltpu.VMEM)
SMEM = pl.BlockSpec(memory_space=pltpu.SMEM)
ANY = pl.BlockSpec(memory_space=pl.ANY)
HBM = pl.BlockSpec(memory_space=pltpu.HBM)


def index_of(y, x, c, z):
    return (((y % NY) * NX + x % NX) * NC + c % NC) * NZ + z % NZ


def pairs(route):
    every = [(y, x, c, z) for y in range(NY) for x in range(NX) for c in range(NC) for z in range(NZ)]
    return [(index_of(*p), index_of(*route(*p))) for p in every]


def to_x(y, x, c, z):
    return y, x + 1, c, z


def to_c(y, x, c, z):
    return y, x, c + 1, z


def to_z4(y, x, c, z):
    return y, x, c, z + 4


def to_xc(y, x, c, z):
    return y, x + 1, c + 1, z


def to_xz4(y, x, c, z):
    return y, x + 1, c, z + 4


def to_first(step):
    return lambda y, x, c, z: (y, x, c, z + step) if c == 0 else (y + step, x, c, z)


def to_second(step):
    return lambda y, x, c, z: (y + step, x, c, z) if c == 0 else (y, x, c, z + step)


def send(value, route):
    return lax.ppermute(value, GROUP, pairs(route))


def params(mib=24):
    return pltpu.CompilerParams(vmem_limit_bytes=mib << 20)


def row_numbers(at_ref):
    y, x, c, z = (at_ref[i] for i in range(4))
    at = lax.broadcasted_iota(jnp.int32, (ROWS, 1), 0)
    r, near, q1, q2, cr = at & 1, (at >> 1) & 3, (at >> 3) & 3, (at >> 5) & 3, at >> 7
    xr, z4 = near & 1, near >> 1
    o1 = jnp.where(q1 == 2, -1, jnp.where(q1 == 3, 2, q1))
    o2 = jnp.where(q2 == 2, -1, jnp.where(q2 == 3, 2, q2))
    core = c ^ cr
    zo = jnp.where(core == 0, o1, o2) + 4 * z4
    yo = jnp.where(core == 0, o2, o1)
    return ((((y + yo) & 3) * 2 + (x ^ xr)) * 2 + core) * 16 + ((z + zo) & 7) * 2 + r


def placed(rows):
    return rows == lax.broadcasted_iota(jnp.int32, (rows.shape[0], ROWS), 1)


def placed_in_half(rows):
    return (rows >> 5) * 16 + (rows & 15) == lax.broadcasted_iota(jnp.int32, (rows.shape[0], ROWS // 2), 1)


def hits(at_ref, targets_ref, place):
    own = jnp.sum(jnp.where(place, targets_ref[...], 0), axis=1, keepdims=True) - at_ref[4]
    return lax.broadcasted_iota(jnp.int32, (ROWS, WIDTH), 1) == own


def column_copies(source, target, sems):
    cuts = [pl.ds(k * CHUNK, CHUNK) for k in range(STEPS)]
    return [pltpu.make_async_copy(source.at[:, cut], target.at[:, cut], sems.at[k]) for k, cut in enumerate(cuts)]


def weight_copies(source, target, sems):
    cuts = [pl.ds(k * CHUNK, CHUNK) for k in range(STEPS)]
    copies = [pltpu.make_async_copy(source.at[cut], target.at[cut], sems.at[k]) for k, cut in enumerate(cuts)]
    for copy in copies:
        copy.start()
    return copies


def logits_kernel(at_ref, targets_ref, p0, p1, p2, p3, p4, p5, p6, p7, w_ref, stats_ref, other_stats_ref, soft_ref):
    acc = jnp.zeros((ROWS, WIDTH), F32)
    for k in range(STEPS):
        cut = slice(k * CHUNK, (k + 1) * CHUNK)
        left = jnp.concatenate([p[:, cut] for p in (p0, p1, p2, p3, p4, p5, p6, p7)], axis=0)
        acc += jnp.dot(left, w_ref[cut, :], preferred_element_type=F32)
    top = jnp.max(acc, axis=1, keepdims=True)
    soft = jnp.exp(acc - top)
    total = jnp.sum(soft, axis=1, keepdims=True)
    rows = row_numbers(at_ref)
    hit = hits(at_ref, targets_ref, placed(rows))
    picked = jnp.sum(jnp.where(hit, acc, 0.0), axis=1, keepdims=True)
    half = ROWS // 2
    place = placed_in_half(rows)
    for i, column in enumerate((top, total, picked)):
        stats_ref[i : i + 1, :] = jnp.sum(jnp.where(place[:half], column[:half], 0.0), axis=0, keepdims=True)
        other_stats_ref[i : i + 1, :] = jnp.sum(jnp.where(place[half:], column[half:], 0.0), axis=0, keepdims=True)
    soft_ref[...] = jnp.where(hit, 0.0, soft).astype(BF)


def soft_kernel(soft_ref, w_ref, own_hbm, other_hbm, own_ref, other_ref, own_sems, other_sems):
    own = (own_ref, column_copies(own_ref, own_hbm, own_sems))
    other = (other_ref, column_copies(other_ref, other_hbm, other_sems))
    products(soft_ref[...], None, w_ref, (own, other))


def products(left, copies, w_ref, pairs):
    for k in range(STEPS):
        cut = slice(k * CHUNK, (k + 1) * CHUNK)
        if copies is not None:
            copies[k].wait()
        part = lax.dot_general(left, w_ref[cut, :], (((1,), (1,)), ((), ())), preferred_element_type=F32)
        first = 0
        for buffer, outs in pairs:
            buffer[:, cut] = part[first : first + buffer.shape[0]].astype(buffer.dtype)
            outs[k].start()
            first += buffer.shape[0]
    for _, outs in pairs:
        for copy in outs:
            copy.wait()


def target_kernel(at_ref, targets_ref, w_hbm, own_hbm, other_hbm, w_ref, own_ref, other_ref, w_sems, own_sems, other_sems):
    copies = weight_copies(w_hbm, w_ref, w_sems)
    left = jnp.where(hits(at_ref, targets_ref, placed(row_numbers(at_ref))), 1.0, 0.0).astype(BF)
    own = (own_ref, column_copies(own_ref, own_hbm, own_sems))
    other = (other_ref, column_copies(other_ref, other_hbm, other_sems))
    products(left, copies, w_ref, (own, other))


def merge_kernel(own_ref, core_ref, x_ref, both_ref, out_ref):
    refs = (own_ref, core_ref, x_ref, both_ref)
    tops = [r[0:1, :] for r in refs]
    top = jnp.maximum(jnp.maximum(tops[0], tops[1]), jnp.maximum(tops[2], tops[3]))
    total = sum(r[1:2, :] * jnp.exp(t - top) for r, t in zip(refs, tops))
    picked = sum(r[2:3, :] for r in refs)
    merged = jnp.concatenate([top, total, picked], axis=0)
    for i in range(out_ref.shape[0]):
        out_ref[i] = merged


def row_scales(at_ref, grad_ref, own_ref, core_ref, spread_ref):
    rows = row_numbers(at_ref)[: ROWS // 2]
    place = placed_in_half(rows)

    def ordered(row):
        return jnp.sum(jnp.where(place, row, 0.0), axis=1, keepdims=True)

    tops = spread_ref[:, 0, :]
    highest = jnp.max(tops, axis=0, keepdims=True)
    total = jnp.sum(spread_ref[:, 1, :] * jnp.exp(tops - highest), axis=0, keepdims=True)
    log_total = ordered(highest + jnp.log(total))
    picked = ordered(jnp.sum(spread_ref[:, 2, :], axis=0, keepdims=True))
    factor = 1.0 + 2.0 * zloss_coef * log_total
    grad = jnp.sum(jnp.where(placed(rows), grad_ref[...], 0.0), axis=1, keepdims=True)
    target = (grad * (jnp.exp(picked - log_total) * factor - 1.0)).astype(BF).astype(F32)
    own, core = (grad * factor * jnp.exp(ordered(ref[0:1, :]) - log_total) for ref in (own_ref, core_ref))
    lane = lax.broadcasted_iota(jnp.int32, (ROWS // 2, 128), 1)
    rest = jnp.where(lane == 2, target, jnp.where(lane == 3, log_total, picked))
    return jnp.where(lane == 0, own, jnp.where(lane == 1, core, rest))


def combine_start(parts, sources, buffers, sems):
    every = []
    for i, q in enumerate(parts):
        copies = [
            pltpu.make_async_copy(s.at[pl.ds(32 * q, 32)], t.at[i], sems.at[i, j])
            for j, (s, t) in enumerate(zip(sources, buffers))
        ]
        for copy in copies:
            copy.start()
        every.append(copies)
    return every


def combine_end(parts, every, scales_ref, buffers, outs):
    a_ref, b_ref, c_ref, d_ref = buffers
    for i, (q, out) in enumerate(zip(parts, outs)):
        for copy in every[i]:
            copy.wait()
        own, core, target = (scales_ref[32 * q : 32 * q + 32, j : j + 1] for j in range(3))
        for k in range(0, DEPTH, CHUNK):
            cut = slice(k, k + CHUNK)
            soft = own * a_ref[i, :, cut] + core * b_ref[i, :, cut].astype(F32)
            chosen = c_ref[i, :, cut].astype(F32) + d_ref[i, :, cut].astype(F32)
            out[:, cut] = (soft + target * chosen).astype(out.dtype)


def first_kernel(parts, at_ref, grad_ref, own_ref, core_ref, spread_ref, *refs):
    sources, scales_ref, outs, buffers, sems = refs[:4], refs[4], refs[5:-5], refs[-5:-1], refs[-1]
    every = combine_start(parts, sources, buffers, sems)
    scales_ref[...] = row_scales(at_ref, grad_ref, own_ref, core_ref, spread_ref)
    combine_end(parts, every, scales_ref, buffers, outs)


def combine_kernel(parts, scales_ref, *refs):
    sources, outs, buffers, sems = refs[:4], refs[4:-5], refs[-5:-1], refs[-1]
    combine_end(parts, combine_start(parts, sources, buffers, sems), scales_ref, buffers, outs)


def shards(hidden, lm_weight, targets, loss_grad):
    half = ROWS // 2
    at = jnp.stack([lax.axis_index(a) for a in GROUP] + [lax.axis_index(GROUP) * WIDTH])
    targets, loss_grad = targets.reshape(1, ROWS), loss_grad.reshape(1, ROWS)
    lm_weight_in, lm_weight = lm_weight, pltpu.with_memory_space_constraint(lm_weight, pltpu.HBM)
    weights = [pltpu.VMEM((DEPTH, WIDTH), BF)]
    sems = pltpu.SemaphoreType.DMA((STEPS,))

    block = jnp.concatenate([hidden] + [send(hidden, to) for to in (to_x, to_z4, to_xz4)])
    block = jnp.concatenate([block] + [send(block, to_first(-o)) for o in OFFSETS[1:]])
    near, back, far = (send(block, to_second(-o)) for o in OFFSETS[1:])

    aim, _ = lax.optimization_barrier((targets, block))
    target_own, target_out = pl.pallas_call(
        target_kernel,
        out_shape=[pltpu.HBM((half, DEPTH), BF)] * 2,
        in_specs=[SMEM, VMEM, ANY],
        out_specs=[HBM] * 2,
        scratch_shapes=weights + [pltpu.VMEM((half, DEPTH), BF)] * 2 + [sems] * 3,
        compiler_params=params(),
        cost_estimate=pl.CostEstimate(flops=2 * ROWS * DEPTH * WIDTH, bytes_accessed=12 << 20, transcendentals=0),
        name="target",
    )(at, aim, lm_weight)
    own, target_out = lax.optimization_barrier((block, target_out))
    pieces = [block, near, back, far] + [send(p, to_c) for p in (own, near, back, far)]

    near_weights = pltpu.with_memory_space_constraint(lm_weight_in, pltpu.VMEM)
    own_stats, other_stats, soft = pl.pallas_call(
        logits_kernel,
        out_shape=[jax.ShapeDtypeStruct((3, half), F32)] * 2 + [jax.ShapeDtypeStruct((ROWS, WIDTH), BF)],
        in_specs=[SMEM] + [VMEM] * 10,
        out_specs=[VMEM] * 3,
        compiler_params=params(16),
        cost_estimate=pl.CostEstimate(flops=2 * ROWS * DEPTH * WIDTH, bytes_accessed=13 << 20, transcendentals=ROWS * WIDTH),
        name="logits",
    )(at, targets, *pieces, near_weights)
    soft_own, soft_out = pl.pallas_call(
        soft_kernel,
        out_shape=(pltpu.HBM((half, DEPTH), F32), pltpu.HBM((half, DEPTH), BF)),
        in_specs=[VMEM] * 2,
        out_specs=(HBM, HBM),
        scratch_shapes=[pltpu.VMEM((half, DEPTH), F32), pltpu.VMEM((half, DEPTH), BF)] + [sems] * 2,
        compiler_params=params(16),
        cost_estimate=pl.CostEstimate(flops=2 * ROWS * DEPTH * WIDTH, bytes_accessed=14 << 20, transcendentals=0),
        name="soft",
    )(soft, near_weights)
    stats = [own_stats, send(other_stats, to_c), send(own_stats, to_x), send(other_stats, to_xc)]
    merged = pl.pallas_call(
        merge_kernel,
        out_shape=jax.ShapeDtypeStruct((32, 3, half), F32),
        in_specs=[VMEM] * 4,
        out_specs=VMEM,
        compiler_params=params(),
        name="merge",
    )(*stats)
    merged, soft_out, target_out = lax.optimization_barrier((merged, soft_out, target_out))
    soft_in, target_in = send(soft_out, to_c), send(target_out, to_c)
    spread = lax.all_to_all(merged, ("y", "z"), 0, 0)

    soft_own, target_own = (pltpu.with_memory_space_constraint(v, pltpu.HBM) for v in (soft_own, target_own))
    shares = (soft_own, soft_in, target_own, target_in)

    def combine(parts, dtype, kernel=combine_kernel, rows=()):
        n = len(parts)
        first = len(rows) > 1
        scales = [jax.ShapeDtypeStruct((half, 128), F32)] if first else []
        return pl.pallas_call(
            functools.partial(kernel, parts),
            out_shape=scales + [jax.ShapeDtypeStruct((32, DEPTH), dtype)] * n,
            in_specs=([SMEM] if first else []) + [VMEM] * (len(rows) - first) + [ANY] * 4,
            out_specs=[VMEM] * (n + first),
            scratch_shapes=[pltpu.VMEM((n, 32, DEPTH), F32)]
            + [pltpu.VMEM((n, 32, DEPTH), BF)] * 3
            + [pltpu.SemaphoreType.DMA((n, 4))],
            compiler_params=params(),
            cost_estimate=pl.CostEstimate(flops=6 * 32 * DEPTH * n, bytes_accessed=n * (3 << 20), transcendentals=0),
            name="combine",
        )(*rows, *shares)

    scales, *parts = combine((3, 1, 2), BF, first_kernel, (at, loss_grad, stats[0], stats[1], spread))
    log_total, target_logit = scales[:2, 3], scales[:2, 4]
    ce_loss = log_total - target_logit
    z_term = zloss_coef * log_total * log_total
    arrived = [send(p, to_second(o)).astype(F32) for p, o in zip(parts, (2, 1, -1))]
    part = combine((0,), F32, rows=(scales,))[0] + sum(arrived)
    part = part.reshape(4, 8, DEPTH)
    part = part[0] + sum(send(part[k].astype(BF), to_first(OFFSETS[k])).astype(F32) for k in (3, 1, 2))
    moved = [
        send(part[2 * k : 2 * k + 2].astype(BF), to).astype(F32) for k, to in ((3, to_xz4), (2, to_z4), (1, to_x))
    ]
    part = [part[0:2], *moved]
    part = (part[0] + part[1]) + (part[2] + part[3])
    return ce_loss, z_term, part.astype(BF)


def solution(mesh):
    mesh = Mesh(mesh.devices.reshape(NY, NX, NC, NZ, 2), (*GROUP, "dp"))
    own = ("dp", *GROUP)
    in_specs = (P(own, None), P(None, GROUP), P("dp"), P("dp"))
    out_specs = (P(own), P(own), P(own, None))
    return jax.shard_map(shards, mesh=mesh, in_specs=in_specs, out_specs=out_specs, check_vma=False)
```
